256 devices in a mesh: seq: 64 (over z, y, core), fsdp: 4 (over x).
Axes of the slice: x: 4, y: 4, z: 8, core: 2. Of those that a mesh axis runs over, the one named last changes fastest.
Arguments:
- activations: bfloat16 [4, 8192, 2048], P('fsdp', 'seq'), may hold values from -6 to 6
- w_query: bfloat16 [2048, 128], P('fsdp'), may hold values from -0.125 to 0.125
- w_key: bfloat16 [2048, 128], P('fsdp'), may hold values from -0.125 to 0.125
- w_value: bfloat16 [2048, 1024], P('fsdp'), may hold values from -0.125 to 0.125
- conv_query: float32 [3, 128], replicated, may hold values from -3 to 3
- conv_key: float32 [3, 128], replicated, may hold values from -3 to 3
- conv_value: float32 [3, 1024], replicated, may hold values from -3 to 3
- norm_gain: float32 [1024], replicated, may hold values from 0.1 to 1.9
- cotangent: bfloat16 [4, 8192, 1024], P('fsdp', 'seq'), may hold values from -6 to 6
Outputs:
- attended: bfloat16 [4, 8192, 1024], P('fsdp', 'seq')
- grad_input: bfloat16 [4, 8192, 2048], P('fsdp', 'seq')
- grad_query: float32 [2048, 128], P('fsdp')
- grad_key: float32 [2048, 128], P('fsdp')
- grad_value: float32 [2048, 1024], P('fsdp')
- grad_conv_query: float32 [3, 128], replicated
- grad_conv_key: float32 [3, 128], replicated
- grad_conv_value: float32 [3, 1024], replicated
- grad_gain: float32 [1024], replicated
The draws below stay inside these ranges and needn't reach their ends.
All inputs are finite; a program needn't handle non-finite values.
Results may differ from the reference program's by a relative error of at most 0.023.
Values may be sent and summed in bfloat16 or wider, within the bound.
A program may use at most 320 MiB of HBM per device.

```python
import math
import jax
import jax.numpy as jnp
from jax import lax

D = 2048
H = 8
F = 16
DV = 128
TOK_DEV = 128
PHI = 273
C = 1280
L = 8192
B = 4
N_SEQ = 64


def steps_of(rng, extent, pieces, smallest, high):
    level, own = 1.0, jax.random.fold_in(rng, 6)
    for axis_at, parts in pieces:
        draws = jnp.exp(jax.random.uniform(jax.random.fold_in(own, axis_at), (parts,), jnp.float32, smallest / len(pieces), high / len(pieces)))
        level = level * jnp.repeat(draws, extent[axis_at] // parts).reshape([-1 if axis == axis_at else 1 for axis in range(len(extent))])
    return level


def gaussian(rng, dims, deviation, most, pieces=(), kind=jnp.bfloat16):
    result = jax.random.normal(rng, dims, jnp.float32) * deviation
    if len(pieces) > 0:
        result = steps_of(rng, dims, pieces, -0.22, 0.18) * result
    return jnp.clip(result, min=-most, max=most).astype(kind)


def setup_inputs(seed: int = 0) -> dict:
    key_of = jax.random.split(jax.random.key(seed), 10)
    activations = gaussian(key_of[0], (B, L, D), 1.0, 6.0, ((0, 4), (1, 64)))
    w_query = gaussian(key_of[1], (D, H * F), D ** -0.5, 0.125, ((0, 4),))
    w_key = gaussian(key_of[2], (D, H * F), D ** -0.5, 0.125, ((0, 4),))
    w_value = gaussian(key_of[3], (D, H * DV), D ** -0.5, 0.125, ((0, 4),))
    conv_query = gaussian(key_of[4], (3, H * F), 0.5, 3.0, (), jnp.float32)
    conv_key = gaussian(key_of[5], (3, H * F), 0.5, 3.0, (), jnp.float32)
    conv_value = gaussian(key_of[6], (3, H * DV), 0.5, 3.0, (), jnp.float32)
    norm_gain = jnp.clip(1.0 + 0.18 * jax.random.normal(key_of[7], (H * DV,), jnp.float32), 0.1, 1.9)
    cotangent = gaussian(key_of[8], (B, L, H * DV), 1.0, 6.0, ((0, 4), (1, 64)))
    return dict(activations=activations, w_query=w_query, w_key=w_key, w_value=w_value, conv_query=conv_query, conv_key=conv_key, conv_value=conv_value, norm_gain=norm_gain, cotangent=cotangent)


def features(vectors):
    feat_dim = vectors.shape[-1]
    second_order = (vectors[..., :, None] * vectors[..., None, :]).reshape(vectors.shape[:-1] + (feat_dim * feat_dim,))
    second_order = second_order / (math.sqrt(feat_dim) * math.sqrt(2.0))
    leading = jnp.ones(vectors.shape[:-1] + (1,), vectors.dtype)
    return jnp.concatenate([leading, vectors / feat_dim ** 0.25, second_order], -1)

def attend(query_conv, key_conv, value_conv, state_in, gain_table):
    feat_dim = query_conv.shape[-1]
    row_count = query_conv.shape[0]
    scores = jnp.einsum('thf,shf->hts', query_conv, key_conv) / math.sqrt(feat_dim)
    weights = 1.0 + scores + 0.5 * scores * scores
    causal = jnp.arange(row_count)[:, None] >= jnp.arange(row_count)[None, :]
    weights = jnp.where(causal[None], weights, 0.0)
    query_feat = features(query_conv)
    averaged = jnp.einsum('hts,shd->thd', weights, value_conv) + jnp.einsum('thp,hpd->thd', query_feat, state_in)
    inverse_rms = lax.rsqrt(lax.optimization_barrier(jnp.mean(averaged * averaged, -1, keepdims=True)) + 1e-06)
    return (averaged * inverse_rms * gain_table).reshape(row_count, -1)

def summarize(key_conv, value_conv):
    key_feat = features(key_conv)
    return jnp.einsum('shp,shd->hpd', key_feat, value_conv)

def split_parts(convolved):
    row_count = convolved.shape[0]
    query_conv = convolved[:, :H * F].reshape(row_count, H, F)
    key_conv = convolved[:, H * F:2 * H * F].reshape(row_count, H, F)
    value_conv = convolved[:, 2 * H * F:].reshape(row_count, H, DV)
    return (query_conv, key_conv, value_conv)

def reference(activations, w_query, w_key, w_value, conv_query, conv_key, conv_value, norm_gain, cotangent):
    tap_weights = jnp.concatenate([conv_query, conv_key, conv_value], 1)
    gain_table = norm_gain.reshape(H, DV)
    weights_cat = jnp.concatenate([w_query, w_key, w_value], 1)
    block_count = N_SEQ
    block_rows = TOK_DEV
    start_state = jnp.zeros((H, PHI, DV), jnp.float32)

    def one_sequence(inputs):
        tokens, cot_rows = inputs
        projected = jnp.dot(tokens, weights_cat, preferred_element_type=jnp.float32).astype(jnp.bfloat16)
        ext_wide = jnp.concatenate([jnp.zeros((2, C), jnp.float32), projected.astype(jnp.float32)], 0)
        convolved = tap_weights[0] * ext_wide[2:] + tap_weights[1] * ext_wide[1:-1] + tap_weights[2] * ext_wide[:-2]
        blocks = convolved.reshape(block_count, block_rows, C)

        def forward_step(running, block):
            query_conv, key_conv, value_conv = split_parts(block)
            return (running + summarize(key_conv, value_conv), running)
        _, states_in = lax.scan(forward_step, start_state, blocks)

        def backward_local(element):
            block, state_in, cot_block = element
            query_conv, key_conv, value_conv = split_parts(block)
            normed, pullback = jax.vjp(attend, query_conv, key_conv, value_conv, state_in, gain_table)
            return (normed, pullback(cot_block.astype(jnp.float32)))
        normed, grads = lax.map(backward_local, (blocks, states_in, cot_rows.reshape(block_count, block_rows, -1)))
        grad_q, grad_k1, grad_v1, grad_state, grad_gains = grads

        def back_step(running, element):
            return (running + element, running)
        _, later_state = lax.scan(back_step, start_state, grad_state, reverse=True)

        def second(element):
            block, state_later = element
            query_conv, key_conv, value_conv = split_parts(block)
            _, pullback = jax.vjp(summarize, key_conv, value_conv)
            return pullback(state_later)
        grad_k2, grad_v2 = lax.map(second, (blocks, later_state))
        seq_len = block_count * block_rows
        conv_grad = jnp.concatenate([grad_q.reshape(seq_len, -1), (grad_k1 + grad_k2).reshape(seq_len, -1), (grad_v1 + grad_v2).reshape(seq_len, -1)], 1)
        padded = jnp.concatenate([conv_grad, jnp.zeros((2, C), jnp.float32)], 0)
        proj_grad = (tap_weights[0] * padded[:-2] + tap_weights[1] * padded[1:-1] + tap_weights[2] * padded[2:]).astype(jnp.bfloat16)
        tap_grad = jnp.stack([lax.optimization_barrier(jnp.sum(conv_grad * ext_wide[2:], 0)), lax.optimization_barrier(jnp.sum(conv_grad * ext_wide[1:-1], 0)), lax.optimization_barrier(jnp.sum(conv_grad * ext_wide[:-2], 0))])
        grad_rows = lax.dot_general(proj_grad, weights_cat, (((1,), (1,)), ((), ())), preferred_element_type=jnp.float32).astype(jnp.bfloat16)
        weight_grad = lax.dot_general(tokens, proj_grad, (((0,), (0,)), ((), ())), preferred_element_type=jnp.float32)
        return (normed.reshape(seq_len, -1).astype(jnp.bfloat16), grad_rows, weight_grad, tap_grad, lax.optimization_barrier(jnp.sum(grad_gains, 0)).reshape(-1))
    attended, grad_input, weight_grads, tap_grads, gain_grads = lax.map(one_sequence, (activations, cotangent))
    weight_grad = lax.optimization_barrier(jnp.sum(weight_grads, 0))
    tap_grad = lax.optimization_barrier(jnp.sum(tap_grads, 0))
    grad_gain = lax.optimization_barrier(jnp.sum(gain_grads, 0))
    return (attended, grad_input, weight_grad[:, :H * F], weight_grad[:, H * F:2 * H * F], weight_grad[:, 2 * H * F:], tap_grad[:, :H * F], tap_grad[:, H * F:2 * H * F], tap_grad[:, 2 * H * F:], grad_gain)
```

```python
import itertools

import jax
import jax.numpy as jnp
from jax import lax
from jax.experimental import pallas as pl
from jax.experimental.pallas import tpu as pltpu
from jax.sharding import PartitionSpec as P

MESH = pl.DeviceIdType.MESH
H, F, DV = 8, 16, 128
NX, NY, NZ, GROUP = 4, 4, 8, 8
TOK, D = 128, 2048
T = GROUP * TOK
ROWS = D // NX
CH = 2 * F + DV
BANDS = F // 2 + 1
PHI = F * (BANDS + 2)
SMALL = 32
PIECE = 80
FULL = NZ * PIECE + SMALL
BT = 256
f32, bf16 = jnp.float32, jnp.bfloat16
MATES = [(0, 1), (1, 0), (3, 0), (1, 1), (3, 1), (2, 0), (2, 1)]


def nn(a, b):
    return lax.dot_general(a, b, (((1,), (0,)), ((), ())), preferred_element_type=f32)


def nt(a, b):
    return lax.dot_general(a, b, (((1,), (1,)), ((), ())), preferred_element_type=f32)


def band_weight(d):
    return (1.0 if d in (0, F // 2) else 2.0) / 32.0


def first_row(cols):
    return jnp.where(lax.broadcasted_iota(jnp.int32, (F, cols), 0) == 0, 1.0, 0.0)


def key_features(k):
    bands = [k * (pltpu.roll(k, d, 0) if d else k) for d in range(BANDS)]
    return jnp.concatenate(bands + [k, first_row(k.shape[1])], 0)


def query_features(q):
    bands = [band_weight(d) * q * (pltpu.roll(q, d, 0) if d else q) for d in range(BANDS)]
    return jnp.concatenate(bands + [0.25 * q, first_row(q.shape[1])], 0)


def features_back(u, grad, weighted):
    total = grad[F * BANDS : F * (BANDS + 1)] * (0.25 if weighted else 1.0)
    for d in range(BANDS):
        e = grad[F * d : F * (d + 1)]
        if weighted:
            e = e * band_weight(d)
        if d:
            total += e * pltpu.roll(u, d, 0) + pltpu.roll(e * u, F - d, 0)
        else:
            total += 2.0 * e * u
    return total


def kernel(
    a, wq, wk, wv, cq, ck, cv, gain, cot,
    att_o, gi_o, gq_o, gk_o, gv_o, tq_o, tk_o, tv_o, gg_o,
    AS, HS, HF, HR, HA, WC, WV, COT, TPAD, TCOL, PT, XT, KPAD, QPAD, KN, VN, VB, QS, PHQ, PHK,
    SS, SR, SA, GS, GR, GA, WT, OT, COTT, DO, DQ, DK, DVT, ATN, CG, CHS, CHR, DPT, DPN, TDV, TDQK,
    CM, XS, XR, XO, ZS, ZR, ZB, FG, QTF, ss, rs,
):
    s = lax.axis_index("seq")
    f = lax.axis_index("fsdp")
    z, j = lax.div(s, 8), lax.rem(s, 8)
    y, c = lax.div(j, 2), lax.rem(j, 2)
    ids = itertools.count()

    def at(dx=0, dy=0, dz=0, dc=0):
        zz, yy, cc = lax.rem(z + dz + NZ, NZ), lax.rem(y + dy, NY), lax.rem(c + dc, 2)
        return {"seq": (zz * NY + yy) * 2 + cc, "fsdp": lax.rem(f + dx, NX)}

    def mate(dy, dc):
        return lax.rem(y + dy, NY) * 2 + lax.rem(c + dc, 2)

    def rc(src, dst, to):
        i = next(ids)
        return pltpu.make_async_remote_copy(
            src_ref=src, dst_ref=dst, send_sem=ss.at[i], recv_sem=rs.at[i],
            device_id=to, device_id_type=MESH,
        )

    def blk(i, size):
        return pl.ds(pl.multiple_of(i * size, size), size)

    bar = pltpu.get_barrier_semaphore()
    peers = [at(dx=k) for k in range(1, NX)] + [at(dy=dy, dc=dc) for dy, dc in MATES]
    peers += [at(dz=k) for k in range(1, NZ)]
    for p in peers:
        pl.semaphore_signal(bar, inc=1, device_id=p, device_id_type=MESH)
    x = a[TOK - 16 :, :].astype(f32)
    for i in range(8):
        HF[2 * i : 2 * i + 2, :] = x[14:16, i * 256 : (i + 1) * 256]
    HS[...] = HF[...].astype(bf16)

    @pl.when(z == 0)
    def _():
        HR[...] = jnp.zeros_like(HR)

    pl.semaphore_wait(bar, len(peers))

    halo_z = rc(HS, HR, at(dz=1))
    halo_g = [rc(HR, HR, at(dy=dy, dc=dc)) for dy, dc in MATES]
    last = j == GROUP - 1

    @pl.when(jnp.logical_and(last, z < NZ - 1))
    def _():
        halo_z.start()

    mine = blk(1 + j, TOK)
    a_sib = rc(a, AS.at[mine], at(dc=1))
    a_out = {dy: rc(a, AS.at[mine], at(dy=dy)) for dy in (1, 3, 2)}
    a_sib.start()
    for dy in (1, 3, 2):
        a_out[dy].start()
    half = blk(c, ROWS // 2)
    mine_half = blk(2 * f + c, ROWS // 2)
    wq_out, wk_out, wh_out, wv_out = {}, {}, {}, {}
    for k in (1, 3, 2):
        wq_out[k] = rc(wq.at[half], WC.at[mine_half, 0:128], at(dx=k))
        wk_out[k] = rc(wk.at[half], WC.at[mine_half, 128:256], at(dx=k))
        wh_out[k] = rc(wv.at[:, blk(j, DV)], WC.at[blk(f, ROWS), 256:384], at(dx=k))
        wv_out[k] = rc(wv.at[half], WV.at[mine_half], at(dx=k))
    for k in (1, 3, 2):
        wq_out[k].start()
        wk_out[k].start()
    for k in (1, 3, 2):
        wh_out[k].start()
    cot_out = [
        rc(cot.at[:, blk(mate(dy, dc), DV)], COT.at[blk(j, TOK)], at(dy=dy, dc=dc))
        for dy, dc in MATES
    ]
    for cp in cot_out:
        cp.start()

    AS[mine] = a[...]
    WC[blk(f, ROWS), 0:128] = wq[...]
    WC[blk(f, ROWS), 128:256] = wk[...]
    WC[blk(f, ROWS), 256:384] = wv[:, blk(j, DV)]
    WV[blk(f, ROWS)] = wv[...]
    COT[blk(j, TOK)] = cot[:, blk(j, DV)]

    TPAD[...] = jnp.zeros_like(TPAD)
    TPAD[0:3, 0:128] = cq[...]
    TPAD[0:3, 128:256] = ck[...]
    TPAD[0:3, 256:384] = cv[:, blk(j, DV)]
    TPAD[3:4, 256:384] = gain[:, blk(j, DV)]
    for i in range(3):
        TCOL[i * 128 : (i + 1) * 128, :] = TPAD[:, i * 128 : (i + 1) * 128].T

    @pl.when(jnp.logical_and(last, z > 0))
    def _():
        halo_z.wait_recv()
        for cp in halo_g:
            cp.start()

    w_fwd, wv_fwd, a_fwd = [], {}, []
    for k in (1, 3, 2):
        from_x = lax.rem(f + NX - k, NX)
        rows = blk(2 * from_x + c, ROWS // 2)
        wq_out[k].wait_recv()
        wk_out[k].wait_recv()
        cp = rc(WC.at[rows, 0:256], WC.at[rows, 0:256], at(dc=1))
        cp.start()
        w_fwd.append(cp)
        wv_fwd[k] = rc(WV.at[rows], WV.at[rows], at(dc=1))
    for k in (1, 3, 2):
        wh_out[k].wait_recv()
    for k in (1, 3, 2):
        wv_out[k].start()
    for dy in (1, 3, 2):
        a_out[dy].wait_recv()
        from_j = lax.rem(y + NY - dy, NY) * 2 + c
        cp = rc(AS.at[blk(1 + from_j, TOK)], AS.at[blk(1 + from_j, TOK)], at(dc=1))
        cp.start()
        a_fwd.append(cp)
    a_sib.wait_recv()
    for cp in w_fwd + a_fwd:
        cp.wait_recv()

    @pl.when(jnp.logical_and(jnp.logical_not(last), z > 0))
    def _():
        for (dy, dc), cp in zip(MATES, halo_g):
            from_j = lax.rem(y + NY - dy, NY) * 2 + lax.rem(c + dc, 2)

            @pl.when(from_j == GROUP - 1)
            def _():
                cp.wait_recv()

    HF[...] = HR[...].astype(f32)
    HA[...] = jnp.zeros_like(HA)
    for i in range(8):
        HA[14:16, i * 256 : (i + 1) * 256] = HF[2 * i : 2 * i + 2, :]

    AS[0 : TOK - 16] = jnp.zeros((TOK - 16, D), bf16)
    AS[TOK - 16 : TOK] = HA[...].astype(bf16)

    def project(i, carry):
        p = nn(AS[blk(i, 128)], WC[...]).astype(bf16).astype(f32)
        PT[:, blk(i, 128)] = p.T
        return carry

    lax.fori_loop(0, GROUP + 1, project, 0)

    q_rows, k_rows = blk(j, F), pl.ds(pl.multiple_of(128 + j * F, F), F)
    parts = ((q_rows, 0, F), (k_rows, F, F), (pl.ds(256, DV), 2 * F, DV))
    for rows, to, size in parts:
        p, taps = PT[rows, :], TCOL[rows, :]
        XT[to : to + size, :] = (
            taps[:, 0:1] * p[:, TOK:]
            + taps[:, 1:2] * pltpu.roll(p, 1, 1)[:, TOK:]
            + taps[:, 2:3] * pltpu.roll(p, 2, 1)[:, TOK:]
        )
    q, k, v = XT[0:F, :], XT[F : 2 * F, :], XT[2 * F :, :]
    VB[...] = v.astype(bf16)
    PHK[...] = key_features(k).astype(bf16)
    SS[...] = nt(PHK[...], VB[...]).astype(bf16)
    s_out = {k: rc(SS, SR.at[k - 1], at(dz=k)) for k in range(1, NZ)}
    for k_, cp in s_out.items():
        pl.when(z + k_ < NZ)(cp.start)
    PHQ[...] = query_features(q).astype(bf16)
    KPAD[...] = jnp.zeros_like(KPAD)
    KPAD[0:F, :] = k
    KN[...] = KPAD[...].T.astype(bf16)
    QPAD[...] = jnp.zeros_like(QPAD)
    QPAD[0:F, :] = (0.25 * q).astype(bf16)
    QS[...] = k.astype(bf16)
    VN[...] = v.T.astype(bf16)
    COTT[...] = jnp.zeros_like(COTT)
    seen = lax.broadcasted_iota(jnp.int32, (BT, BT), 0) <= lax.broadcasted_iota(
        jnp.int32, (BT, BT), 1
    )

    def causal(block):
        n = block.shape[0]
        tail = jnp.where(seen, block[n - BT :], 0.0)
        return tail if n == BT else jnp.concatenate([block[: n - BT], tail], 0)

    for tb in range(T // BT):
        n, cols = (tb + 1) * BT, slice(tb * BT, (tb + 1) * BT)
        sc = nn(KN[:n, :], QPAD[:, cols])
        w = causal(1.0 + sc * (1.0 + 0.5 * sc)).astype(bf16)
        WT[:n, cols] = w
        OT[:, cols] = nn(VB[:, :n], w)
    for cp in cot_out:
        cp.wait_recv()
    COTT[...] = COT[...].astype(f32).T
    SA[...] = jnp.zeros_like(SA)
    for k_, cp in s_out.items():

        @pl.when(z >= k_)
        def _():
            cp.wait_recv()
            SA[...] += SR[k_ - 1].astype(f32)

    gcol = TCOL[256:384, 3:4]
    o = OT[...] + nn(SA[...].T.astype(bf16), PHQ[...])
    r = lax.rsqrt(jnp.mean(o * o, 0, keepdims=True) + 1e-06)
    hat = o * r
    ATN[...] = (hat * gcol).T.astype(bf16)
    att_out = [
        rc(ATN.at[blk(mate(dy, dc), TOK)], att_o.at[:, blk(j, DV)], at(dy=dy, dc=dc))
        for dy, dc in MATES
    ]
    ct = COTT[...]
    gain_grad = jnp.sum(ct * hat, 1, keepdims=True)
    gn = ct * gcol
    DO[...] = (r * (gn - hat * jnp.mean(gn * hat, 0, keepdims=True))).astype(bf16)
    GS[...] = nt(PHQ[...], DO[...]).astype(bf16)
    g_out = {k: rc(GS, GR.at[k - 1], at(dz=NZ - k)) for k in range(1, NZ)}
    for k_, cp in g_out.items():
        pl.when(z >= k_)(cp.start)
    for cp in att_out:
        cp.start()
    att_o[:, blk(j, DV)] = ATN[blk(j, TOK)]
    DQ[...] = features_back(q, nn(SA[...].astype(bf16), DO[...]), True)
    DK[...] = jnp.zeros_like(DK)
    DVT[...] = jnp.zeros_like(DVT)
    for tb in range(T // BT):
        n, cols = (tb + 1) * BT, slice(tb * BT, (tb + 1) * BT)
        sc = nn(KN[:n, :], QPAD[:, cols])
        ds = causal(nn(VN[:n, :], DO[:, cols]) * (1.0 + sc)).astype(bf16)
        DQ[:, cols] += 0.25 * nn(QS[:, :n], ds)
        DK[:, :n] += nt(QPAD[0:F, cols], ds)
        DVT[:, :n] += nt(DO[:, cols], WT[:n, cols])
    GA[...] = jnp.zeros_like(GA)
    for k_, cp in g_out.items():

        @pl.when(z + k_ < NZ)
        def _():
            cp.wait_recv()
            GA[...] += GR[k_ - 1].astype(f32)

    dk = DK[...] + features_back(k, nn(GA[...].astype(bf16), VB[...]), False)
    CG[0:F, :T] = DQ[...]
    CG[F : 2 * F, :T] = dk
    CG[2 * F :, :T] = DVT[...] + nn(GA[...].T.astype(bf16), PHK[...])
    CHS[...] = CG[:, :TOK].astype(bf16)
    ch_out = rc(CHS, CHR, at(dz=NZ - 1))
    pl.when(z > 0)(ch_out.start)
    lane = lax.broadcasted_iota(jnp.int32, (DV, 128), 1)
    CM[...] = jnp.zeros_like(CM)
    for rows, to, size in parts:
        p, g = PT[rows, :], CG[to : to + size, :T]
        sums = [
            jnp.sum(g * (pltpu.roll(p, i, 1) if i else p)[:, TOK:], 1, keepdims=True)
            for i in range(3)
        ]
        if size == DV:
            sums.append(gain_grad)
        tile = jnp.zeros((size, 128), f32)
        for i, col in enumerate(sums):
            tile = jnp.where(lane[:size] == i, col, tile)
        CM[rows, :] = tile
    small = [CM[i * 128 : (i + 1) * 128, :].T[0:8, :] for i in range(3)]
    small = jnp.concatenate(small + [jnp.zeros((8, 128), f32)], 0)

    @pl.when(z == NZ - 1)
    def _():
        CG[:, T:] = jnp.zeros((CH, TOK), f32)

    @pl.when(z < NZ - 1)
    def _():
        ch_out.wait_recv()
        CG[:, T:] = CHR[...].astype(f32)

    for rows, to, size in parts:
        g, taps = CG[to : to + size, :], TCOL[rows, :]
        dp = (
            taps[:, 0:1] * g[:, :T]
            + taps[:, 1:2] * pltpu.roll(g, T + TOK - 1, 1)[:, :T]
            + taps[:, 2:3] * pltpu.roll(g, T + TOK - 2, 1)[:, :T]
        )
        DPT[to : to + size, :] = dp.astype(bf16)
        if size == DV:
            DPN[...] = dp.T.astype(bf16)
    dp_out = []
    for dy, dc in MATES:
        m = mate(dy, dc)
        dp_out.append(rc(DPN.at[blk(m, TOK)], TDV.at[:, blk(j, DV)], at(dy=dy, dc=dc)))
        dp_out.append(rc(DPT.at[0 : 2 * F, blk(m, TOK)], TDQK.at[blk(j, 2 * F)], at(dy=dy, dc=dc)))
    for cp in dp_out:
        cp.start()
    x_out = {k: rc(XS.at[k - 1], XR.at[k - 1], at(dx=k)) for k in (1, 3, 2)}

    def weight_part(to_x):
        return nn(DPT[...], AS[TOK:, blk(to_x, ROWS)])

    for k_ in (1, 3, 2):
        part = weight_part(lax.rem(f + k_, NX)).astype(bf16)
        for b in range(4):
            XS[k_ - 1, b * CH : (b + 1) * CH, :] = part[:, b * 128 : (b + 1) * 128]
        XS[k_ - 1, 4 * CH :, :] = small.astype(bf16)
        x_out[k_].start()
    part = weight_part(f)
    for b in range(4):
        XO[b * CH : (b + 1) * CH, :] = part[:, b * 128 : (b + 1) * 128]
    XO[4 * CH :, :] = small
    TDV[:, blk(j, DV)] = DPN[blk(j, TOK)]
    TDQK[blk(j, 2 * F)] = DPT[0 : 2 * F, blk(j, TOK)]
    for cp in dp_out:
        cp.wait_recv()
    tq = jnp.concatenate([TDQK[2 * F * h : 2 * F * h + F, :] for h in range(H)], 0)
    tk = jnp.concatenate([TDQK[2 * F * h + F : 2 * F * h + 2 * F, :] for h in range(H)], 0)
    tqk = jnp.concatenate([tq, tk], 0).astype(f32).T.astype(bf16)
    for k_ in (1, 3, 2):
        wv_out[k_].wait_recv()
        wv_fwd[k_].start()
    for k_ in (1, 3, 2):
        wv_fwd[k_].wait_recv()

    def input_grad(i, carry):
        rows = blk(i, 256)
        gi = nt(TDV[...], WV[rows]) + nt(tqk, WC[rows, 0:256])
        gi_o[:, rows] = gi.astype(bf16)
        return carry

    lax.fori_loop(0, D // 256, input_grad, 0)
    for k_ in (1, 3, 2):
        x_out[k_].wait_recv()
        XO[...] += XR[k_ - 1].astype(f32)
    for b in range(4):
        nat = XO[b * CH + 2 * F : (b + 1) * CH, :].T
        for i in range(2):
            ZS[2 * b + i, 0:64, :] = nat[i * 64 : (i + 1) * 64].astype(bf16)
            ZS[2 * b + i, 64:PIECE, :] = XO[b * CH + F * i : b * CH + F * (i + 1), :].astype(bf16)
            ZS[2 * b + i, PIECE:, :] = XO[4 * CH :, :].astype(bf16)
    z_out = {
        k: rc(ZS.at[lax.rem(z + k, NZ)], ZR.at[k - 1], at(dz=k)) for k in (4, 3, 5, 2, 6, 1, 7)
    }
    for cp in z_out.values():
        cp.start()
    red = ZS[z].astype(f32)
    for k_, cp in z_out.items():
        cp.wait_recv()
        red += ZR[k_ - 1].astype(f32)
    ZB[...] = red.astype(bf16)
    zg_dst = FG.at[j, blk(z, PIECE)]
    zg_out = {k: rc(ZB.at[0:PIECE], zg_dst, at(dz=k)) for k in (4, 3, 5, 2, 6, 1, 7)}
    for cp in zg_out.values():
        cp.start()
    FG[j, blk(z, PIECE), :] = ZB[0:PIECE, :]
    FG[j, NZ * PIECE :, :] = ZB[PIECE:, :]
    for cp in zg_out.values():
        cp.wait_recv()
    fg_sib = rc(FG.at[j], FG.at[j], at(dc=1))
    fg_out = {dy: rc(FG.at[j], FG.at[j], at(dy=dy)) for dy in (1, 3, 2)}
    for cp in [fg_out[1], fg_out[3], fg_out[2], fg_sib]:
        cp.start()
    fg_fwd = []
    for dy in (1, 3, 2):
        fg_out[dy].wait_recv()
        from_j = lax.rem(y + NY - dy, NY) * 2 + c
        cp = rc(FG.at[from_j], FG.at[from_j], at(dc=1))
        cp.start()
        fg_fwd.append(cp)
    fg_sib.wait_recv()
    for cp in fg_fwd:
        cp.wait_recv()
    tq_sum, tk_sum = jnp.zeros((8, 128), f32), jnp.zeros((8, 128), f32)
    for h in range(H):
        lanes = slice(h * DV, (h + 1) * DV)
        for p_ in range(NZ):
            base = p_ * PIECE
            gv_o[p_ * 64 : (p_ + 1) * 64, lanes] = FG[h, base : base + 64, :].astype(f32)
            qk = FG[h, base + 64 : base + PIECE, :].astype(f32)
            row = (p_ % 2) * 128 + h * F
            QTF[row : row + F, (p_ // 2) * 128 : (p_ // 2 + 1) * 128] = qk
        sm = FG[h, NZ * PIECE :, :].astype(f32)
        tq_sum += sm[0:8]
        tk_sum += sm[8:16]
        tv_o[:, lanes] = sm[16:19]
        gg_o[:, lanes] = sm[19:20]
    tq_o[...] = tq_sum[0:3]
    tk_o[...] = tk_sum[0:3]
    gq_o[...] = QTF[0:128, :].T
    gk_o[...] = QTF[128:256, :].T
    for cp in att_out:
        cp.wait_recv()
    pl.when(jnp.logical_and(last, z < NZ - 1))(halo_z.wait_send)

    @pl.when(jnp.logical_and(last, z > 0))
    def _():
        for cp in halo_g:
            cp.wait_send()

    for k_, cp in s_out.items():
        pl.when(z + k_ < NZ)(cp.wait_send)
    for k_, cp in g_out.items():
        pl.when(z >= k_)(cp.wait_send)
    pl.when(z > 0)(ch_out.wait_send)
    done = [a_sib, fg_sib] + cot_out + w_fwd + a_fwd + att_out + dp_out + fg_fwd
    for group in (a_out, wq_out, wk_out, wh_out, wv_out, wv_fwd, x_out, z_out, zg_out, fg_out):
        done += list(group.values())
    for cp in done:
        cp.wait_send()


N_SEMS = 104


def on_device(a, wq, wk, wv, cq, ck, cv, gain, cot):
    sd = jax.ShapeDtypeStruct
    outs = [
        sd((TOK, H * DV), bf16), sd((TOK, D), bf16),
        sd((ROWS, H * F), f32), sd((ROWS, H * F), f32), sd((ROWS, H * DV), f32),
        sd((3, H * F), f32), sd((3, H * F), f32), sd((3, H * DV), f32), sd((1, H * DV), f32),
    ]
    V = pltpu.VMEM
    scratch = [
        V((T + TOK, D), bf16), V((16, 256), bf16), V((16, 256), f32), V((16, 256), bf16),
        V((16, D), f32),
        V((D, 384), bf16), V((D, H * DV), bf16), V((T, DV), bf16),
        V((128, 384), f32), V((384, 128), f32), V((384, T + TOK), f32),
        V((CH, T), f32), V((128, T), f32), V((128, T), bf16), V((T, 128), bf16), V((T, DV), bf16),
        V((DV, T), bf16), V((F, T), bf16), V((PHI, T), bf16), V((PHI, T), bf16),
        V((PHI, DV), bf16), V((NZ - 1, PHI, DV), bf16), V((PHI, DV), f32),
        V((PHI, DV), bf16), V((NZ - 1, PHI, DV), bf16), V((PHI, DV), f32),
        V((T, T), bf16), V((DV, T), f32), V((DV, T), f32), V((DV, T), bf16),
        V((F, T), f32), V((F, T), f32), V((DV, T), f32), V((T, DV), bf16),
        V((CH, T + TOK), f32), V((CH, TOK), bf16), V((CH, TOK), bf16),
        V((CH, T), bf16), V((T, DV), bf16), V((TOK, H * DV), bf16), V((H * 2 * F, TOK), bf16),
        V((384, 128), f32),
        V((NX - 1, 4 * CH + SMALL, 128), bf16), V((NX - 1, 4 * CH + SMALL, 128), bf16),
        V((4 * CH + SMALL, 128), f32),
        V((NZ, PIECE + SMALL, 128), bf16), V((NZ - 1, PIECE + SMALL, 128), bf16),
        V((PIECE + SMALL, 128), bf16), V((H, FULL, 128), bf16), V((256, ROWS), f32),
        pltpu.SemaphoreType.DMA((N_SEMS,)), pltpu.SemaphoreType.DMA((N_SEMS,)),
    ]
    res = pl.pallas_call(
        kernel,
        out_shape=outs,
        in_specs=[pl.BlockSpec(memory_space=V)] * 9,
        out_specs=[pl.BlockSpec(memory_space=V)] * 9,
        scratch_shapes=scratch,
        compiler_params=pltpu.CompilerParams(
            collective_id=0, has_side_effects=True, vmem_limit_bytes=58 * 2**20
        ),
        name="based_layer",
    )(a.reshape(TOK, D), wq, wk, wv, cq, ck, cv, gain.reshape(1, -1), cot.reshape(TOK, H * DV))
    att, gi, gq, gk, gv, tq, tk, tv, gg = res
    return att[None], gi[None], gq, gk, gv, tq, tk, tv, gg.reshape(-1)


def solution(mesh):
    rows = P("fsdp", "seq", None)
    return jax.shard_map(
        on_device,
        mesh=mesh,
        in_specs=(rows, P("fsdp", None), P("fsdp", None), P("fsdp", None), P(), P(), P(), P(), rows),
        out_specs=(
            rows, rows, P("fsdp", None), P("fsdp", None), P("fsdp", None), P(), P(), P(), P(),
        ),
        check_vma=False,
    )
```

```python
import itertools

import jax
import jax.numpy as jnp
from jax import lax
from jax.experimental import pallas as pl
from jax.experimental.pallas import tpu as pltpu
from jax.sharding import PartitionSpec as P

MESH = pl.DeviceIdType.MESH
H, F, DV = 8, 16, 128
NX, NY, NZ, GROUP = 4, 4, 8, 8
TOK, D = 128, 2048
T = GROUP * TOK
ROWS = D // NX
CH = 2 * F + DV
BANDS = F // 2 + 1
PHI = F * (BANDS + 2)
SMALL = 32
PIECE = 80
FULL = NZ * PIECE + SMALL
BT = 256
HALF = TOK // 2
ORDER = (0, 1, 7, 2, 6, 3, 5, 4)
CHUNKS = ((0, 3), (3, 5), (5, 8))
f32, bf16 = jnp.float32, jnp.bfloat16
MATES = [(0, 1), (1, 0), (3, 0), (1, 1), (3, 1), (2, 0), (2, 1)]


def nn(a, b):
    return lax.dot_general(a, b, (((1,), (0,)), ((), ())), preferred_element_type=f32)


def nt(a, b):
    return lax.dot_general(a, b, (((1,), (1,)), ((), ())), preferred_element_type=f32)


def band_weight(d):
    return (1.0 if d in (0, F // 2) else 2.0) / 32.0


def first_row(cols):
    return jnp.where(lax.broadcasted_iota(jnp.int32, (F, cols), 0) == 0, 1.0, 0.0)


def key_features(k):
    bands = [k * (pltpu.roll(k, d, 0) if d else k) for d in range(BANDS)]
    return jnp.concatenate(bands + [k, first_row(k.shape[1])], 0)


def query_features(q):
    bands = [band_weight(d) * q * (pltpu.roll(q, d, 0) if d else q) for d in range(BANDS)]
    return jnp.concatenate(bands + [0.25 * q, first_row(q.shape[1])], 0)


def features_back(u, grad, weighted):
    total = grad[F * BANDS : F * (BANDS + 1)] * (0.25 if weighted else 1.0)
    for d in range(BANDS):
        e = grad[F * d : F * (d + 1)]
        if weighted:
            e = e * band_weight(d)
        if d:
            total += e * pltpu.roll(u, d, 0) + pltpu.roll(e * u, F - d, 0)
        else:
            total += 2.0 * e * u
    return total


def kernel(
    a, wq, wk, wv, cq, ck, cv, gain, cot,
    att_o, gi_o, fg_o,
    AS, HS, HF, HR, HA, WC, WV, COT, TPAD, TCOL, PT, XT, KPAD, QPAD, KN, VN, VB, QS, PHQ, PHK,
    SS, SR, SA, GS, GR, GA, WT, OT, COTT, DO, DQ, DK, DVT, ATN, CG, CHS, CHR, DPT, DPN, TDV, TDQK,
    TQK, GI, CM, XS, XR, XO, ZS, ZR, ZB, ss, rs, ls,
):
    s = lax.axis_index("seq")
    f = lax.axis_index("fsdp")
    z, j = lax.div(s, 8), lax.rem(s, 8)
    y, c = lax.div(j, 2), lax.rem(j, 2)
    ids = itertools.count()

    def at(dx=0, dy=0, dz=0, dc=0):
        zz, yy, cc = lax.rem(z + dz + NZ, NZ), lax.rem(y + dy, NY), lax.rem(c + dc, 2)
        return {"seq": (zz * NY + yy) * 2 + cc, "fsdp": lax.rem(f + dx, NX)}

    def mate(dy, dc):
        return lax.rem(y + dy, NY) * 2 + lax.rem(c + dc, 2)

    def rc(src, dst, to):
        i = next(ids)
        return pltpu.make_async_remote_copy(
            src_ref=src, dst_ref=dst, send_sem=ss.at[i], recv_sem=rs.at[i],
            device_id=to, device_id_type=MESH,
        )

    def blk(i, size):
        return pl.ds(pl.multiple_of(i * size, size), size)

    bar = pltpu.get_barrier_semaphore()
    peers = [at(dx=k) for k in range(1, NX)] + [at(dy=dy, dc=dc) for dy, dc in MATES]
    peers += [at(dz=k) for k in range(1, NZ)]
    for p in peers:
        pl.semaphore_signal(bar, inc=1, device_id=p, device_id_type=MESH)
    x = a[TOK - 16 :, :].astype(f32)
    for i in range(8):
        HF[2 * i : 2 * i + 2, :] = x[14:16, i * 256 : (i + 1) * 256]
    HS[...] = HF[...].astype(bf16)

    @pl.when(z == 0)
    def _():
        HR[...] = jnp.zeros_like(HR)

    pl.semaphore_wait(bar, len(peers))

    halo_z = rc(HS, HR, at(dz=1))
    halo_g = [rc(HR, HR, at(dy=dy, dc=dc)) for dy, dc in MATES]
    last = j == GROUP - 1

    @pl.when(jnp.logical_and(last, z < NZ - 1))
    def _():
        halo_z.start()

    def tok_rows(chip_y, part=None):
        base = (1 + lax.rem(chip_y + NY, NY) * 2 + c) * TOK
        if part is None:
            return pl.ds(pl.multiple_of(base, TOK), TOK)
        return pl.ds(pl.multiple_of(base + part * HALF, HALF), HALF)

    mine = tok_rows(y)
    a_sib = rc(a, AS.at[mine], at(dc=1))
    up, down = {}, {}
    for p_ in (0, 1):
        src = a.at[p_ * HALF : (p_ + 1) * HALF]
        up[p_] = rc(src, AS.at[tok_rows(y, p_)], at(dy=1))
        down[p_] = rc(src, AS.at[tok_rows(y, p_)], at(dy=3))
    relay_up = rc(AS.at[tok_rows(y - 1, 0)], AS.at[tok_rows(y - 1, 0)], at(dy=1))
    relay_down = rc(AS.at[tok_rows(y + 1, 1)], AS.at[tok_rows(y + 1, 1)], at(dy=3))
    across = {}
    for name, rows in (
        ("up", tok_rows(y - 1)), ("down", tok_rows(y + 1)),
        ("far0", tok_rows(y + 2, 0)), ("far1", tok_rows(y + 2, 1)),
    ):
        across[name] = rc(AS.at[rows], AS.at[rows], at(dc=1))
    up[0].start()
    down[1].start()
    up[1].start()
    down[0].start()
    a_sib.start()
    half = blk(c, ROWS // 2)
    mine_half = blk(2 * f + c, ROWS // 2)
    wq_out, wk_out, wh_out, wv_out = {}, {}, {}, {}
    for k in (1, 3, 2):
        wq_out[k] = rc(wq.at[half], WC.at[mine_half, 0:128], at(dx=k))
        wk_out[k] = rc(wk.at[half], WC.at[mine_half, 128:256], at(dx=k))
        wh_out[k] = rc(wv.at[:, blk(j, DV)], WC.at[blk(f, ROWS), 256:384], at(dx=k))
        wv_out[k] = rc(wv.at[half], WV.at[mine_half], at(dx=k))
    for k in (1, 3, 2):
        wq_out[k].start()
        wk_out[k].start()
    for k in (1, 3, 2):
        wh_out[k].start()
    cot_out = [
        rc(cot.at[:, blk(mate(dy, dc), DV)], COT.at[blk(j, TOK)], at(dy=dy, dc=dc))
        for dy, dc in MATES
    ]

    AS[mine] = a[...]
    WC[blk(f, ROWS), 0:128] = wq[...]
    WC[blk(f, ROWS), 128:256] = wk[...]
    WC[blk(f, ROWS), 256:384] = wv[:, blk(j, DV)]
    WV[blk(f, ROWS)] = wv[...]
    COT[blk(j, TOK)] = cot[:, blk(j, DV)]

    TPAD[...] = jnp.zeros_like(TPAD)
    TPAD[0:3, 0:128] = cq[...]
    TPAD[0:3, 128:256] = ck[...]
    TPAD[0:3, 256:384] = cv[:, blk(j, DV)]
    TPAD[3:4, 256:384] = gain[:, blk(j, DV)]
    for i in range(3):
        TCOL[i * 128 : (i + 1) * 128, :] = TPAD[:, i * 128 : (i + 1) * 128].T

    @pl.when(jnp.logical_and(last, z > 0))
    def _():
        halo_z.wait_recv()
        for cp in halo_g:
            cp.start()

    up[0].wait_recv()
    relay_up.start()
    down[1].wait_recv()
    relay_down.start()
    w_fwd, wv_fwd = [], {}
    for k in (1, 3, 2):
        from_x = lax.rem(f + NX - k, NX)
        rows = blk(2 * from_x + c, ROWS // 2)
        wq_out[k].wait_recv()
        wk_out[k].wait_recv()
        cp = rc(WC.at[rows, 0:256], WC.at[rows, 0:256], at(dc=1))
        cp.start()
        w_fwd.append(cp)
        wv_fwd[k] = rc(WV.at[rows], WV.at[rows], at(dc=1))
    up[1].wait_recv()
    across["up"].start()
    down[0].wait_recv()
    across["down"].start()
    for k in (1, 3, 2):
        wh_out[k].wait_recv()
    for k in (1, 3, 2):
        wv_out[k].start()
    a_sib.wait_recv()
    for cp in w_fwd:
        cp.wait_recv()

    def project(chip_y):
        chip = lax.rem(chip_y + NY, NY)
        p = nn(AS[pl.ds(pl.multiple_of(TOK + chip * 2 * TOK, TOK), 2 * TOK)], WC[...])
        cols = pl.ds(pl.multiple_of(TOK + chip * 2 * TOK, TOK), 2 * TOK)
        PT[:, cols] = p.astype(bf16).astype(f32).T

    project(y)
    across["up"].wait_recv()
    project(y - 1)
    across["down"].wait_recv()
    project(y + 1)
    relay_up.wait_recv()
    across["far0"].start()
    relay_down.wait_recv()
    across["far1"].start()
    for cp in cot_out:
        cp.start()

    @pl.when(jnp.logical_and(jnp.logical_not(last), z > 0))
    def _():
        for (dy, dc), cp in zip(MATES, halo_g):
            from_j = lax.rem(y + NY - dy, NY) * 2 + lax.rem(c + dc, 2)

            @pl.when(from_j == GROUP - 1)
            def _():
                cp.wait_recv()

    HF[...] = HR[...].astype(f32)
    HA[...] = jnp.zeros_like(HA)
    for i in range(8):
        HA[14:16, i * 256 : (i + 1) * 256] = HF[2 * i : 2 * i + 2, :]
    AS[0 : TOK - 16] = jnp.zeros((TOK - 16, D), bf16)
    AS[TOK - 16 : TOK] = HA[...].astype(bf16)
    ph = nn(AS[TOK - 16 : TOK], WC[...]).astype(bf16).astype(f32)
    PT[:, 0:TOK] = jnp.concatenate([jnp.zeros((TOK - 16, 384), f32), ph], 0).T
    across["far0"].wait_recv()
    across["far1"].wait_recv()
    project(y + 2)

    q_rows, k_rows = blk(j, F), pl.ds(pl.multiple_of(128 + j * F, F), F)
    parts = ((q_rows, 0, F), (k_rows, F, F), (pl.ds(256, DV), 2 * F, DV))
    for rows, to, size in parts:
        p, taps = PT[rows, :], TCOL[rows, :]
        XT[to : to + size, :] = (
            taps[:, 0:1] * p[:, TOK:]
            + taps[:, 1:2] * pltpu.roll(p, 1, 1)[:, TOK:]
            + taps[:, 2:3] * pltpu.roll(p, 2, 1)[:, TOK:]
        )
    q, k, v = XT[0:F, :], XT[F : 2 * F, :], XT[2 * F :, :]
    VB[...] = v.astype(bf16)
    PHK[...] = key_features(k).astype(bf16)
    SS[...] = nt(PHK[...], VB[...]).astype(bf16)
    s_out = {k: rc(SS, SR.at[k - 1], at(dz=k)) for k in range(1, NZ)}
    for k_, cp in s_out.items():
        pl.when(z + k_ < NZ)(cp.start)
    PHQ[...] = query_features(q).astype(bf16)
    KPAD[...] = jnp.zeros_like(KPAD)
    KPAD[0:F, :] = k
    KN[...] = KPAD[...].T.astype(bf16)
    QPAD[...] = jnp.zeros_like(QPAD)
    QPAD[0:F, :] = (0.25 * q).astype(bf16)
    QS[...] = k.astype(bf16)
    VN[...] = v.T.astype(bf16)
    COTT[...] = jnp.zeros_like(COTT)
    seen = lax.broadcasted_iota(jnp.int32, (BT, BT), 0) <= lax.broadcasted_iota(
        jnp.int32, (BT, BT), 1
    )

    def causal(block):
        n = block.shape[0]
        tail = jnp.where(seen, block[n - BT :], 0.0)
        return tail if n == BT else jnp.concatenate([block[: n - BT], tail], 0)

    for tb in range(T // BT):
        n, cols = (tb + 1) * BT, slice(tb * BT, (tb + 1) * BT)
        sc = nn(KN[:n, :], QPAD[:, cols])
        w = causal(1.0 + sc * (1.0 + 0.5 * sc)).astype(bf16)
        WT[:n, cols] = w
        OT[:, cols] = nn(VB[:, :n], w)
    for cp in cot_out:
        cp.wait_recv()
    COTT[...] = COT[...].astype(f32).T
    SA[...] = jnp.zeros_like(SA)
    for k_, cp in s_out.items():

        @pl.when(z >= k_)
        def _():
            cp.wait_recv()
            SA[...] += SR[k_ - 1].astype(f32)

    gcol = TCOL[256:384, 3:4]
    o = OT[...] + nn(SA[...].T.astype(bf16), PHQ[...])
    r = lax.rsqrt(jnp.mean(o * o, 0, keepdims=True) + 1e-06)
    hat = o * r
    ATN[...] = (hat * gcol).T.astype(bf16)
    att_out = [
        rc(ATN.at[blk(mate(dy, dc), TOK)], att_o.at[:, blk(j, DV)], at(dy=dy, dc=dc))
        for dy, dc in MATES
    ]
    ct = COTT[...]
    gain_grad = jnp.sum(ct * hat, 1, keepdims=True)
    gn = ct * gcol
    DO[...] = (r * (gn - hat * jnp.mean(gn * hat, 0, keepdims=True))).astype(bf16)
    GS[...] = nt(PHQ[...], DO[...]).astype(bf16)
    g_out = {k: rc(GS, GR.at[k - 1], at(dz=NZ - k)) for k in range(1, NZ)}
    for k_, cp in g_out.items():
        pl.when(z >= k_)(cp.start)
    for cp in att_out:
        cp.start()
    att_mine = pltpu.make_async_copy(ATN.at[blk(j, TOK)], att_o.at[:, blk(j, DV)], ls.at[0])
    att_mine.start()
    DQ[...] = features_back(q, nn(SA[...].astype(bf16), DO[...]), True)
    DK[...] = jnp.zeros_like(DK)
    DVT[...] = jnp.zeros_like(DVT)
    for tb in range(T // BT):
        n, cols = (tb + 1) * BT, slice(tb * BT, (tb + 1) * BT)
        sc = nn(KN[:n, :], QPAD[:, cols])
        ds = causal(nn(VN[:n, :], DO[:, cols]) * (1.0 + sc)).astype(bf16)
        DQ[:, cols] += 0.25 * nn(QS[:, :n], ds)
        DK[:, :n] += nt(QPAD[0:F, cols], ds)
        DVT[:, :n] += nt(DO[:, cols], WT[:n, cols])
    GA[...] = jnp.zeros_like(GA)
    for k_, cp in g_out.items():

        @pl.when(z + k_ < NZ)
        def _():
            cp.wait_recv()
            GA[...] += GR[k_ - 1].astype(f32)

    dk = DK[...] + features_back(k, nn(GA[...].astype(bf16), VB[...]), False)
    CG[0:F, TOK : TOK + T] = DQ[...]
    CG[F : 2 * F, TOK : TOK + T] = dk
    CG[2 * F :, TOK : TOK + T] = DVT[...] + nn(GA[...].T.astype(bf16), PHK[...])
    CHS[...] = CG[:, TOK : 2 * TOK].astype(bf16)
    ch_out = rc(CHS, CHR, at(dz=NZ - 1))
    pl.when(z > 0)(ch_out.start)
    CG[:, 0:TOK] = jnp.zeros((CH, TOK), f32)
    CG[:, TOK + T :] = jnp.zeros((CH, TOK), f32)

    def conv_back(rows, to, size, first, count):
        g, taps = CG[to : to + size, first : first + count + TOK], TCOL[rows, :]
        n = count + TOK
        return (
            taps[:, 0:1] * g[:, :count]
            + taps[:, 1:2] * pltpu.roll(g, n - 1, 1)[:, :count]
            + taps[:, 2:3] * pltpu.roll(g, n - 2, 1)[:, :count]
        )

    for rows, to, size in parts:
        DPT[to : to + size, :] = conv_back(rows, to, size, 0, T + TOK).astype(bf16)
    lane = lax.broadcasted_iota(jnp.int32, (DV, 128), 1)
    CM[...] = jnp.zeros_like(CM)
    for rows, to, size in parts:
        p, g = PT[rows, :], CG[to : to + size, TOK : TOK + T]
        sums = [
            jnp.sum(g * (pltpu.roll(p, i, 1) if i else p)[:, TOK:], 1, keepdims=True)
            for i in range(3)
        ]
        if size == DV:
            sums.append(gain_grad)
        tile = jnp.zeros((size, 128), f32)
        for i, col in enumerate(sums):
            tile = jnp.where(lane[:size] == i, col, tile)
        CM[rows, :] = tile
    small = [CM[i * 128 : (i + 1) * 128, :].T[0:8, :] for i in range(3)]
    small = jnp.concatenate(small + [jnp.zeros((8, 128), f32)], 0)

    x_out = {k: rc(XS.at[k - 1], XR.at[k - 1], at(dx=k)) for k in (1, 3, 2)}

    def weight_part(to_x):
        return nn(DPT[...], AS[:, blk(to_x, ROWS)])

    for k_ in (2, 1, 3):
        part = weight_part(lax.rem(f + k_, NX)).astype(bf16)
        for b in range(4):
            XS[k_ - 1, b * CH : (b + 1) * CH, :] = part[:, b * 128 : (b + 1) * 128]
        XS[k_ - 1, 4 * CH :, :] = small.astype(bf16)
        x_out[k_].start()
    part = weight_part(f)
    for b in range(4):
        XO[b * CH : (b + 1) * CH, :] = part[:, b * 128 : (b + 1) * 128]
    XO[4 * CH :, :] = small

    @pl.when(z < NZ - 1)
    def _():
        ch_out.wait_recv()
        CG[:, TOK + T :] = CHR[...].astype(f32)

    for rows, to, size in parts:
        DPT[to : to + size, T:] = conv_back(rows, to, size, T, TOK).astype(bf16)
    DPN[...] = DPT[2 * F :, TOK:].astype(f32).T.astype(bf16)
    dp_out = []
    for dy, dc in MATES:
        m = mate(dy, dc)
        dp_out.append(rc(DPN.at[blk(m, TOK)], TDV.at[:, blk(j, DV)], at(dy=dy, dc=dc)))
        dp_out.append(
            rc(DPT.at[0 : 2 * F, blk(1 + m, TOK)], TDQK.at[blk(j, 2 * F)], at(dy=dy, dc=dc))
        )
    for cp in dp_out:
        cp.start()
    TDV[:, blk(j, DV)] = DPN[blk(j, TOK)]
    TDQK[blk(j, 2 * F)] = DPT[0 : 2 * F, blk(1 + j, TOK)]
    for k_ in (1, 3, 2):
        wv_out[k_].wait_recv()
        wv_fwd[k_].start()
    for k_ in (1, 3, 2):
        x_out[k_].wait_recv()
        XO[...] += XR[k_ - 1].astype(f32)
    for b in range(4):
        nat = XO[b * CH + 2 * F : (b + 1) * CH, :].T
        for i in range(2):
            ZS[2 * b + i, 0:64, :] = nat[i * 64 : (i + 1) * 64].astype(bf16)
            ZS[2 * b + i, 64:PIECE, :] = XO[b * CH + F * i : b * CH + F * (i + 1), :].astype(bf16)
            ZS[2 * b + i, PIECE:, :] = XO[4 * CH :, :].astype(bf16)
    z_out = {
        k: rc(ZS.at[lax.rem(z + k, NZ)], ZR.at[k - 1], at(dz=k)) for k in (4, 3, 5, 2, 6, 1, 7)
    }
    for cp in z_out.values():
        cp.start()
    for k_ in (1, 3, 2):
        wv_fwd[k_].wait_recv()
    for cp in dp_out:
        cp.wait_recv()
    tq = jnp.concatenate([TDQK[2 * F * h : 2 * F * h + F, :] for h in range(H)], 0)
    tk = jnp.concatenate([TDQK[2 * F * h + F : 2 * F * h + 2 * F, :] for h in range(H)], 0)
    TQK[...] = jnp.concatenate([tq, tk], 0).astype(f32).T.astype(bf16)

    def input_grad(i, carry):
        rows = blk(i, 256)
        gi = nt(TDV[...], WV[rows]) + nt(TQK[...], WC[rows, 0:256])
        GI[:, rows] = gi.astype(bf16)
        return carry

    lax.fori_loop(0, D // 512, input_grad, 0)
    red = ZS[z].astype(f32)
    for k_, cp in z_out.items():
        cp.wait_recv()
        red += ZR[k_ - 1].astype(f32)
    ZB[...] = red.astype(bf16)
    zg_out = {}
    for i, k_ in enumerate(ORDER):
        rows = slice(i * PIECE, (i + 1) * PIECE)
        if k_:
            zg_out[k_] = rc(ZB.at[0:PIECE], fg_o.at[j, rows], at(dz=k_))
        else:
            fg_o[j, rows, :] = ZB[0:PIECE, :]
    for k_ in (1, 7, 2, 6, 3, 5, 4):
        zg_out[k_].start()
    fg_o[j, NZ * PIECE :, :] = ZB[PIECE:, :]
    lax.fori_loop(D // 512, D // 256, input_grad, 0)
    gi_copy = pltpu.make_async_copy(GI, gi_o, ls.at[1])
    gi_copy.start()
    fg_sib, fg_out, fg_fwd = [], {}, []
    for ci, (lo, hi) in enumerate(CHUNKS):
        for k_ in ORDER[lo:hi]:
            if k_:
                zg_out[k_].wait_recv()
        rows = slice(lo * PIECE, hi * PIECE + (SMALL if hi == NZ else 0))
        for dy in (1, 3, 2):
            fg_out[ci, dy] = rc(fg_o.at[j, rows], fg_o.at[j, rows], at(dy=dy))
            fg_out[ci, dy].start()
        fg_sib.append(rc(fg_o.at[j, rows], fg_o.at[j, rows], at(dc=1)))
        fg_sib[-1].start()
    for ci, (lo, hi) in enumerate(CHUNKS):
        rows = slice(lo * PIECE, hi * PIECE + (SMALL if hi == NZ else 0))
        for dy in (1, 3, 2):
            fg_out[ci, dy].wait_recv()
            from_j = lax.rem(y + NY - dy, NY) * 2 + c
            cp = rc(fg_o.at[from_j, rows], fg_o.at[from_j, rows], at(dc=1))
            cp.start()
            fg_fwd.append(cp)
    for cp in fg_sib + fg_fwd:
        cp.wait_recv()
    for cp in att_out:
        cp.wait_recv()
    att_mine.wait()
    gi_copy.wait()
    pl.when(jnp.logical_and(last, z < NZ - 1))(halo_z.wait_send)

    @pl.when(jnp.logical_and(last, z > 0))
    def _():
        for cp in halo_g:
            cp.wait_send()

    for k_, cp in s_out.items():
        pl.when(z + k_ < NZ)(cp.wait_send)
    for k_, cp in g_out.items():
        pl.when(z >= k_)(cp.wait_send)
    pl.when(z > 0)(ch_out.wait_send)
    done = [a_sib, relay_up, relay_down] + fg_sib + cot_out + w_fwd + att_out + dp_out + fg_fwd
    for group in (up, down, across, wq_out, wk_out, wh_out, wv_out, wv_fwd, x_out, z_out, zg_out, fg_out):
        done += list(group.values())
    for cp in done:
        cp.wait_send()


def unpack(att, gi, fg, att_o, gi_o, gq_o, gk_o, gv_o, tq_o, tk_o, tv_o, gg_o, QTF):
    z = lax.div(lax.axis_index("seq"), GROUP)
    att_o[...] = att[...]
    gi_o[...] = gi[...]
    for i, k in enumerate(ORDER):
        piece = lax.rem(z + NZ - k, NZ)
        band, kind = lax.div(piece, 2), lax.rem(piece, 2)
        rows = pl.ds(pl.multiple_of(piece * 64, 64), 64)
        cols = pl.ds(pl.multiple_of(band * 128, 128), 128)
        for h in range(H):
            base = i * PIECE
            gv_o[rows, h * DV : (h + 1) * DV] = fg[h, base : base + 64, :].astype(f32)
            row = pl.ds(pl.multiple_of(kind * 128 + h * F, F), F)
            QTF[row, cols] = fg[h, base + 64 : base + PIECE, :].astype(f32)
    tq_sum, tk_sum = jnp.zeros((8, 128), f32), jnp.zeros((8, 128), f32)
    for h in range(H):
        lanes = slice(h * DV, (h + 1) * DV)
        sm = fg[h, NZ * PIECE :, :].astype(f32)
        tq_sum += sm[0:8]
        tk_sum += sm[8:16]
        tv_o[:, lanes] = sm[16:19]
        gg_o[:, lanes] = sm[19:20]
    tq_o[...] = tq_sum[0:3]
    tk_o[...] = tk_sum[0:3]
    gq_o[...] = QTF[0:128, :].T
    gk_o[...] = QTF[128:256, :].T


N_SEMS = 128


def on_device(a, wq, wk, wv, cq, ck, cv, gain, cot):
    sd = jax.ShapeDtypeStruct
    V = pltpu.VMEM
    vmem, anywhere = pl.BlockSpec(memory_space=V), pl.BlockSpec(memory_space=pl.ANY)
    scratch = [
        V((T + TOK, D), bf16), V((16, 256), bf16), V((16, 256), f32), V((16, 256), bf16),
        V((16, D), f32),
        V((D, 384), bf16), V((D, H * DV), bf16), V((T, DV), bf16),
        V((128, 384), f32), V((384, 128), f32), V((384, T + TOK), f32),
        V((CH, T), f32), V((128, T), f32), V((128, T), bf16), V((T, 128), bf16), V((T, DV), bf16),
        V((DV, T), bf16), V((F, T), bf16), V((PHI, T), bf16), V((PHI, T), bf16),
        V((PHI, DV), bf16), V((NZ - 1, PHI, DV), bf16), V((PHI, DV), f32),
        V((PHI, DV), bf16), V((NZ - 1, PHI, DV), bf16), V((PHI, DV), f32),
        V((T, T), bf16), V((DV, T), f32), V((DV, T), f32), V((DV, T), bf16),
        V((F, T), f32), V((F, T), f32), V((DV, T), f32), V((T, DV), bf16),
        V((CH, T + 2 * TOK), f32), V((CH, TOK), bf16), V((CH, TOK), bf16),
        V((CH, T + TOK), bf16), V((T, DV), bf16), V((TOK, H * DV), bf16),
        V((H * 2 * F, TOK), bf16), V((TOK, H * 2 * F), bf16), V((TOK, D), bf16),
        V((384, 128), f32),
        V((NX - 1, 4 * CH + SMALL, 128), bf16), V((NX - 1, 4 * CH + SMALL, 128), bf16),
        V((4 * CH + SMALL, 128), f32),
        V((NZ, PIECE + SMALL, 128), bf16), V((NZ - 1, PIECE + SMALL, 128), bf16),
        V((PIECE + SMALL, 128), bf16),
        pltpu.SemaphoreType.DMA((N_SEMS,)), pltpu.SemaphoreType.DMA((N_SEMS,)),
        pltpu.SemaphoreType.DMA((2,)),
    ]
    att, gi, fg = pl.pallas_call(
        kernel,
        out_shape=[
            sd((TOK, H * DV), bf16), sd((TOK, D), bf16), sd((H, FULL, 128), bf16),
        ],
        in_specs=[vmem] * 9,
        out_specs=[anywhere, anywhere, vmem],
        scratch_shapes=scratch,
        compiler_params=pltpu.CompilerParams(
            collective_id=0, has_side_effects=True, vmem_limit_bytes=56 * 2**20
        ),
        name="based_layer",
    )(a.reshape(TOK, D), wq, wk, wv, cq, ck, cv, gain.reshape(1, -1), cot.reshape(TOK, H * DV))
    att, gi, gq, gk, gv, tq, tk, tv, gg = pl.pallas_call(
        unpack,
        out_shape=[
            sd((TOK, H * DV), bf16), sd((TOK, D), bf16),
            sd((ROWS, H * F), f32), sd((ROWS, H * F), f32), sd((ROWS, H * DV), f32),
            sd((3, H * F), f32), sd((3, H * F), f32), sd((3, H * DV), f32), sd((1, H * DV), f32),
        ],
        in_specs=[vmem] * 3,
        out_specs=[vmem] * 9,
        scratch_shapes=[V((256, ROWS), f32)],
        name="unpack",
    )(att, gi, fg)
    return att[None], gi[None], gq, gk, gv, tq, tk, tv, gg.reshape(-1)


def solution(mesh):
    rows = P("fsdp", "seq", None)
    return jax.shard_map(
        on_device,
        mesh=mesh,
        in_specs=(rows, P("fsdp", None), P("fsdp", None), P("fsdp", None), P(), P(), P(), P(), rows),
        out_specs=(
            rows, rows, P("fsdp", None), P("fsdp", None), P("fsdp", None), P(), P(), P(), P(),
        ),
        check_vma=False,
    )
```

```python
import itertools

import jax
import jax.numpy as jnp
from jax import lax
from jax.experimental import pallas as pl
from jax.experimental.pallas import tpu as pltpu
from jax.sharding import PartitionSpec as P

MESH = pl.DeviceIdType.MESH
H, F, DV = 8, 16, 128
NX, NY, NZ, GROUP = 4, 4, 8, 8
TOK, D = 128, 2048
T = GROUP * TOK
ROWS = D // NX
CH = 2 * F + DV
BANDS = F // 2
PHI = F * (BANDS + 2)
SMALL = 16
PIECE = 80
FULL = NZ * PIECE + SMALL
BT = 256
HALF = TOK // 2
ORDER = (0, 1, 7, 2, 6, 3, 5, 4)
CHUNKS = ((0, 1), (1, 3), (3, 5), (5, 8))
FAR_FIRST = (4, 3, 5, 2, 6, 1, 7)
f32, bf16 = jnp.float32, jnp.bfloat16
MATES = [(0, 1), (1, 0), (3, 0), (1, 1), (3, 1), (2, 0), (2, 1)]


def piece_rows(lo, hi):
    return slice(SMALL + lo * PIECE if lo else 0, SMALL + hi * PIECE)


def nn(a, b):
    return lax.dot_general(a, b, (((1,), (0,)), ((), ())), preferred_element_type=f32)


def nt(a, b):
    return lax.dot_general(a, b, (((1,), (1,)), ((), ())), preferred_element_type=f32)


def pair_rows(u, weighted):
    scale = 1.0 / 32.0 if weighted else 1.0
    bands = [scale * u * u]
    for d in range(1, BANDS):
        bands.append((2.0 * scale if weighted else 1.0) * u * pltpu.roll(u, d, 0))
    bands.append((2.0 * scale if weighted else 1.0) * u[:BANDS] * u[BANDS:])
    one = lax.broadcasted_iota(jnp.int32, (F - BANDS, u.shape[1]), 0) == 0
    return jnp.concatenate(bands + [jnp.where(one, 1.0, 0.0), 0.25 * u if weighted else u], 0)


def pair_rows_back(u, grad, weighted):
    scale = 1.0 / 32.0 if weighted else 1.0
    total = grad[F * (BANDS + 1) :] * (0.25 if weighted else 1.0) + 2.0 * scale * grad[:F] * u
    twice = 2.0 * scale if weighted else 1.0
    for d in range(1, BANDS):
        e = twice * grad[F * d : F * (d + 1)]
        total += e * pltpu.roll(u, d, 0) + pltpu.roll(e * u, F - d, 0)
    e = twice * grad[F * BANDS : F * BANDS + BANDS]
    return total + jnp.concatenate([e * u[BANDS:], e * u[:BANDS]], 0)


def kernel(
    a, wq, wk, wv, cq, ck, cv, gain, cot,
    att_o, gi_o, fg_o,
    AS, HS, HF, HR, HA, WC, WV, COT, TPAD, TCOL, PT, XT, KPAD, QPAD, KN, VN, VB, QS, PHQ, PHK,
    SS, SR, SA, GS, GR, GA, WT, OT, COTT, DO, DQ, DK, DVT, ATN, CG, CHS, CHR, DPT, DPN, TDV, TDQK,
    TQK, GI, CM, SMF, SMB, SMR, XS, XR, XO, ZS, ZR, ZB, ss, rs, ls,
):
    s = lax.axis_index("seq")
    f = lax.axis_index("fsdp")
    z, j = lax.div(s, 8), lax.rem(s, 8)
    y, c = lax.div(j, 2), lax.rem(j, 2)
    ids = itertools.count()

    def at(dx=0, dy=0, dz=0, dc=0):
        zz, yy, cc = lax.rem(z + dz + NZ, NZ), lax.rem(y + dy, NY), lax.rem(c + dc, 2)
        return {"seq": (zz * NY + yy) * 2 + cc, "fsdp": lax.rem(f + dx, NX)}

    def mate(dy, dc):
        return lax.rem(y + dy, NY) * 2 + lax.rem(c + dc, 2)

    def rc(src, dst, to):
        i = next(ids)
        return pltpu.make_async_remote_copy(
            src_ref=src, dst_ref=dst, send_sem=ss.at[i], recv_sem=rs.at[i],
            device_id=to, device_id_type=MESH,
        )

    def blk(i, size):
        return pl.ds(pl.multiple_of(i * size, size), size)

    bar = pltpu.get_barrier_semaphore()
    peers = [at(dx=k) for k in range(1, NX)] + [at(dy=dy, dc=dc) for dy, dc in MATES]
    peers += [at(dz=k) for k in range(1, NZ)]
    for p in peers:
        pl.semaphore_signal(bar, inc=1, device_id=p, device_id_type=MESH)
    x = a[TOK - 16 :, :].astype(f32)
    for i in range(8):
        HF[2 * i : 2 * i + 2, :] = x[14:16, i * 256 : (i + 1) * 256]
    HS[...] = HF[...].astype(bf16)

    @pl.when(z == 0)
    def _():
        HR[...] = jnp.zeros_like(HR)

    AS[blk(1 + j, TOK)] = a[...]
    WC[blk(f, ROWS), 0:128] = wq[...]
    WC[blk(f, ROWS), 128:256] = wk[...]
    WC[blk(f, ROWS), 256:384] = wv[:, blk(j, DV)]
    WV[blk(f, ROWS)] = wv[...]
    COT[blk(j, TOK)] = cot[:, blk(j, DV)]

    TPAD[...] = jnp.zeros_like(TPAD)
    TPAD[0:3, 0:128] = cq[...]
    TPAD[0:3, 128:256] = ck[...]
    TPAD[0:3, 256:384] = cv[:, blk(j, DV)]
    TPAD[3:4, 256:384] = gain[:, blk(j, DV)]
    for i in range(3):
        TCOL[i * 128 : (i + 1) * 128, :] = TPAD[:, i * 128 : (i + 1) * 128].T

    pl.semaphore_wait(bar, len(peers))
    halo_z = rc(HS, HR, at(dz=1))
    halo_g = [rc(HR, HR, at(dy=dy, dc=dc)) for dy, dc in MATES]
    last = j == GROUP - 1

    @pl.when(jnp.logical_and(last, z < NZ - 1))
    def _():
        halo_z.start()

    def tok_rows(chip_y, part=None):
        base = (1 + lax.rem(chip_y + NY, NY) * 2 + c) * TOK
        if part is None:
            return pl.ds(pl.multiple_of(base, TOK), TOK)
        return pl.ds(pl.multiple_of(base + part * HALF, HALF), HALF)

    mine = tok_rows(y)
    a_sib = rc(a, AS.at[mine], at(dc=1))
    up, down = {}, {}
    for p_ in (0, 1):
        src = a.at[p_ * HALF : (p_ + 1) * HALF]
        up[p_] = rc(src, AS.at[tok_rows(y, p_)], at(dy=1))
        down[p_] = rc(src, AS.at[tok_rows(y, p_)], at(dy=3))
    relay_up = rc(AS.at[tok_rows(y - 1, 0)], AS.at[tok_rows(y - 1, 0)], at(dy=1))
    relay_down = rc(AS.at[tok_rows(y + 1, 1)], AS.at[tok_rows(y + 1, 1)], at(dy=3))
    across = {}
    for name, rows in (
        ("up", tok_rows(y - 1)), ("down", tok_rows(y + 1)),
        ("far0", tok_rows(y + 2, 0)), ("far1", tok_rows(y + 2, 1)),
    ):
        across[name] = rc(AS.at[rows], AS.at[rows], at(dc=1))
    up[0].start()
    down[1].start()
    up[1].start()
    down[0].start()
    a_sib.start()
    half = blk(c, ROWS // 2)
    mine_half = blk(2 * f + c, ROWS // 2)
    wq_out, wk_out, wh_out, wv_out = {}, {}, {}, {}
    for k in (1, 3, 2):
        wq_out[k] = rc(wq.at[half], WC.at[mine_half, 0:128], at(dx=k))
        wk_out[k] = rc(wk.at[half], WC.at[mine_half, 128:256], at(dx=k))
        wh_out[k] = rc(wv.at[:, blk(j, DV)], WC.at[blk(f, ROWS), 256:384], at(dx=k))
        wv_out[k] = rc(wv.at[half], WV.at[mine_half], at(dx=k))
    for k in (1, 3, 2):
        wq_out[k].start()
        wk_out[k].start()
    for k in (1, 3, 2):
        wh_out[k].start()
    cot_out = [
        rc(cot.at[:, blk(mate(dy, dc), DV)], COT.at[blk(j, TOK)], at(dy=dy, dc=dc))
        for dy, dc in MATES
    ]

    @pl.when(jnp.logical_and(last, z > 0))
    def _():
        halo_z.wait_recv()
        for cp in halo_g:
            cp.start()

    up[0].wait_recv()
    relay_up.start()
    down[1].wait_recv()
    relay_down.start()
    w_fwd, wv_fwd = [], {}
    for k in (1, 3, 2):
        from_x = lax.rem(f + NX - k, NX)
        rows = blk(2 * from_x + c, ROWS // 2)
        wq_out[k].wait_recv()
        wk_out[k].wait_recv()
        cp = rc(WC.at[rows, 0:256], WC.at[rows, 0:256], at(dc=1))
        cp.start()
        w_fwd.append(cp)
        wv_fwd[k] = rc(WV.at[rows], WV.at[rows], at(dc=1))
    up[1].wait_recv()
    across["up"].start()
    down[0].wait_recv()
    across["down"].start()
    for k in (1, 3, 2):
        wh_out[k].wait_recv()
    for k in (1, 3, 2):
        wv_out[k].start()
    a_sib.wait_recv()
    for cp in w_fwd:
        cp.wait_recv()

    def project(chip_y):
        chip = lax.rem(chip_y + NY, NY)
        p = nn(AS[pl.ds(pl.multiple_of(TOK + chip * 2 * TOK, TOK), 2 * TOK)], WC[...])
        cols = pl.ds(pl.multiple_of(TOK + chip * 2 * TOK, TOK), 2 * TOK)
        PT[:, cols] = p.astype(bf16).astype(f32).T

    project(y)
    across["up"].wait_recv()
    project(y - 1)
    across["down"].wait_recv()
    project(y + 1)
    relay_up.wait_recv()
    across["far0"].start()
    relay_down.wait_recv()
    across["far1"].start()
    for cp in cot_out:
        cp.start()

    @pl.when(jnp.logical_and(jnp.logical_not(last), z > 0))
    def _():
        for (dy, dc), cp in zip(MATES, halo_g):
            from_j = lax.rem(y + NY - dy, NY) * 2 + lax.rem(c + dc, 2)

            @pl.when(from_j == GROUP - 1)
            def _():
                cp.wait_recv()

    HF[...] = HR[...].astype(f32)
    HA[...] = jnp.zeros_like(HA)
    for i in range(8):
        HA[14:16, i * 256 : (i + 1) * 256] = HF[2 * i : 2 * i + 2, :]
    AS[0 : TOK - 16] = jnp.zeros((TOK - 16, D), bf16)
    AS[TOK - 16 : TOK] = HA[...].astype(bf16)
    ph = nn(AS[TOK - 16 : TOK], WC[...]).astype(bf16).astype(f32)
    PT[:, 0:TOK] = jnp.concatenate([jnp.zeros((TOK - 16, 384), f32), ph], 0).T
    across["far0"].wait_recv()
    across["far1"].wait_recv()
    project(y + 2)

    q_rows, k_rows = blk(j, F), pl.ds(pl.multiple_of(128 + j * F, F), F)
    parts = ((q_rows, 0, F), (k_rows, F, F), (pl.ds(256, DV), 2 * F, DV))
    for rows, to, size in parts:
        p, taps = PT[rows, :], TCOL[rows, :]
        XT[to : to + size, :] = (
            taps[:, 0:1] * p[:, TOK:]
            + taps[:, 1:2] * pltpu.roll(p, 1, 1)[:, TOK:]
            + taps[:, 2:3] * pltpu.roll(p, 2, 1)[:, TOK:]
        )
    q, k, v = XT[0:F, :], XT[F : 2 * F, :], XT[2 * F :, :]
    VB[...] = v.astype(bf16)
    PHK[...] = pair_rows(k, False).astype(bf16)
    SS[...] = nt(PHK[...], VB[...]).astype(bf16)
    s_out = {k: rc(SS, SR.at[k - 1], at(dz=k)) for k in FAR_FIRST}
    for k_, cp in s_out.items():
        pl.when(z + k_ < NZ)(cp.start)
    PHQ[...] = pair_rows(q, True).astype(bf16)
    KPAD[...] = jnp.zeros_like(KPAD)
    KPAD[0:F, :] = k
    KN[...] = KPAD[...].T.astype(bf16)
    QPAD[...] = jnp.zeros_like(QPAD)
    QPAD[0:F, :] = (0.25 * q).astype(bf16)
    QS[...] = k.astype(bf16)
    VN[...] = v.T.astype(bf16)
    COTT[...] = jnp.zeros_like(COTT)
    seen = lax.broadcasted_iota(jnp.int32, (BT, BT), 0) <= lax.broadcasted_iota(
        jnp.int32, (BT, BT), 1
    )

    def causal(block):
        n = block.shape[0]
        tail = jnp.where(seen, block[n - BT :], 0.0)
        return tail if n == BT else jnp.concatenate([block[: n - BT], tail], 0)

    for tb in range(T // BT):
        n, cols = (tb + 1) * BT, slice(tb * BT, (tb + 1) * BT)
        sc = nn(KN[:n, :], QPAD[:, cols])
        w = causal(1.0 + sc * (1.0 + 0.5 * sc)).astype(bf16)
        WT[:n, cols] = w
        OT[:, cols] = nn(VB[:, :n], w)
    for cp in cot_out:
        cp.wait_recv()
    COTT[...] = COT[...].astype(f32).T
    SA[...] = jnp.zeros_like(SA)
    for k_, cp in s_out.items():

        @pl.when(z >= k_)
        def _():
            cp.wait_recv()
            SA[...] += SR[k_ - 1].astype(f32)

    gcol = TCOL[256:384, 3:4]
    o = OT[...] + nn(SA[...].T.astype(bf16), PHQ[...])
    r = lax.rsqrt(jnp.mean(o * o, 0, keepdims=True) + 1e-06)
    hat = o * r
    ct = COTT[...]
    gain_grad = jnp.sum(ct * hat, 1, keepdims=True)
    gn = ct * gcol
    DO[...] = (r * (gn - hat * jnp.mean(gn * hat, 0, keepdims=True))).astype(bf16)
    GS[...] = nt(PHQ[...], DO[...]).astype(bf16)
    g_out = {k: rc(GS, GR.at[k - 1], at(dz=NZ - k)) for k in FAR_FIRST}
    for k_, cp in g_out.items():
        pl.when(z >= k_)(cp.start)
    ATN[...] = (hat * gcol).T.astype(bf16)
    att_out = [
        rc(ATN.at[blk(mate(dy, dc), TOK)], att_o.at[:, blk(j, DV)], at(dy=dy, dc=dc))
        for dy, dc in MATES
    ]
    for cp in att_out:
        cp.start()
    att_mine = pltpu.make_async_copy(ATN.at[blk(j, TOK)], att_o.at[:, blk(j, DV)], ls.at[0])
    att_mine.start()
    DQ[...] = pair_rows_back(q, nn(SA[...].astype(bf16), DO[...]), True)
    DK[...] = jnp.zeros_like(DK)
    DVT[...] = jnp.zeros_like(DVT)
    for tb in range(T // BT):
        n, cols = (tb + 1) * BT, slice(tb * BT, (tb + 1) * BT)
        sc = nn(KN[:n, :], QPAD[:, cols])
        ds = causal(nn(VN[:n, :], DO[:, cols]) * (1.0 + sc)).astype(bf16)
        DQ[:, cols] += 0.25 * nn(QS[:, :n], ds)
        DK[:, :n] += nt(QPAD[0:F, cols], ds)
        DVT[:, :n] += nt(DO[:, cols], WT[:n, cols])
    GA[...] = jnp.zeros_like(GA)
    for k_, cp in g_out.items():

        @pl.when(z + k_ < NZ)
        def _():
            cp.wait_recv()
            GA[...] += GR[k_ - 1].astype(f32)

    dk = DK[...] + pair_rows_back(k, nn(GA[...].astype(bf16), VB[...]), False)
    CG[0:F, TOK : TOK + T] = DQ[...]
    CG[F : 2 * F, TOK : TOK + T] = dk
    CG[2 * F :, TOK : TOK + T] = DVT[...] + nn(GA[...].T.astype(bf16), PHK[...])
    CHS[...] = CG[:, TOK : 2 * TOK].astype(bf16)
    ch_out = rc(CHS, CHR, at(dz=NZ - 1))
    pl.when(z > 0)(ch_out.start)
    CG[:, 0:TOK] = jnp.zeros((CH, TOK), f32)
    CG[:, TOK + T :] = jnp.zeros((CH, TOK), f32)

    def conv_back(rows, to, size, first, count):
        g, taps = CG[to : to + size, first : first + count + TOK], TCOL[rows, :]
        n = count + TOK
        return (
            taps[:, 0:1] * g[:, :count]
            + taps[:, 1:2] * pltpu.roll(g, n - 1, 1)[:, :count]
            + taps[:, 2:3] * pltpu.roll(g, n - 2, 1)[:, :count]
        )

    for rows, to, size in parts:
        DPT[to : to + size, :] = conv_back(rows, to, size, 0, T + TOK).astype(bf16)
    x_out = {k: rc(XS.at[k - 1], XR.at[k - 1], at(dx=k)) for k in (1, 3, 2)}

    sm_out = {k: rc(SMB, SMR.at[k - 1], at(dx=k)) for k in (1, 3, 2)}
    SMF[...] = jnp.zeros_like(SMF)

    def weight_part(to_x):
        return nn(DPT[...], AS[:, blk(to_x, ROWS)])

    for k_ in (2, 1, 3):
        part = weight_part(lax.rem(f + k_, NX)).astype(bf16)
        for b in range(4):
            XS[k_ - 1, b * CH : (b + 1) * CH, :] = part[:, b * 128 : (b + 1) * 128]
        x_out[k_].start()
    part = weight_part(f)
    for b in range(4):
        XO[b * CH : (b + 1) * CH, :] = part[:, b * 128 : (b + 1) * 128]
    lane = lax.broadcasted_iota(jnp.int32, (DV, 128), 1)
    CM[...] = jnp.zeros_like(CM)
    for rows, to, size in parts:
        p, g = PT[rows, :], CG[to : to + size, TOK : TOK + T]
        sums = [
            jnp.sum(g * (pltpu.roll(p, i, 1) if i else p)[:, TOK:], 1, keepdims=True)
            for i in range(3)
        ]
        if size == DV:
            sums.append(gain_grad)
        tile = jnp.zeros((size, 128), f32)
        for i, col in enumerate(sums):
            tile = jnp.where(lane[:size] == i, col, tile)
        CM[rows, :] = tile
    for i, (lo, n) in enumerate(((0, 3), (3, 3), (6, 4))):
        SMF[lo : lo + n, :] = CM[i * 128 : (i + 1) * 128, :].T[0:n, :]
    SMB[...] = SMF[...].astype(bf16)
    for cp in sm_out.values():
        cp.start()

    @pl.when(z < NZ - 1)
    def _():
        ch_out.wait_recv()
        CG[:, TOK + T :] = CHR[...].astype(f32)

    for rows, to, size in parts:
        DPT[to : to + size, T:] = conv_back(rows, to, size, T, TOK).astype(bf16)
    DPN[...] = DPT[2 * F :, TOK:].astype(f32).T.astype(bf16)
    dp_out = []
    for dy, dc in MATES:
        m = mate(dy, dc)
        dp_out.append(rc(DPN.at[blk(m, TOK)], TDV.at[:, blk(j, DV)], at(dy=dy, dc=dc)))
        dp_out.append(
            rc(DPT.at[0 : 2 * F, blk(1 + m, TOK)], TDQK.at[blk(j, 2 * F)], at(dy=dy, dc=dc))
        )
    for cp in dp_out:
        cp.start()
    TDV[:, blk(j, DV)] = DPN[blk(j, TOK)]
    TDQK[blk(j, 2 * F)] = DPT[0 : 2 * F, blk(1 + j, TOK)]
    for k_ in (1, 3, 2):
        wv_out[k_].wait_recv()
        wv_fwd[k_].start()
    for k_ in (1, 3, 2):
        x_out[k_].wait_recv()
        XO[...] += XR[k_ - 1].astype(f32)
        sm_out[k_].wait_recv()
        SMF[...] += SMR[k_ - 1].astype(f32)
    for b in range(4):
        nat = XO[b * CH + 2 * F : (b + 1) * CH, :].T
        for i in range(2):
            ZS[2 * b + i, 0:64, :] = nat[i * 64 : (i + 1) * 64].astype(bf16)
            ZS[2 * b + i, 64:PIECE, :] = XO[b * CH + F * i : b * CH + F * (i + 1), :].astype(bf16)
            ZS[2 * b + i, PIECE:, :] = SMF[...].astype(bf16)
    z_out = {
        k: rc(ZS.at[lax.rem(z + k, NZ)], ZR.at[k - 1], at(dz=k)) for k in FAR_FIRST
    }
    for cp in z_out.values():
        cp.start()
    red = ZS[z].astype(f32)
    for k_, cp in z_out.items():
        cp.wait_recv()
        red += ZR[k_ - 1].astype(f32)
    ZB[...] = red.astype(bf16)
    zg_out = {
        k: rc(ZB.at[0:PIECE], fg_o.at[j, piece_rows(ORDER.index(k), ORDER.index(k) + 1)], at(dz=k))
        for k in FAR_FIRST
    }
    for cp in zg_out.values():
        cp.start()
    fg_o[j, 0:SMALL, :] = ZB[PIECE:, :]
    fg_o[j, SMALL : SMALL + PIECE, :] = ZB[0:PIECE, :]
    fg_sib, fg_out, fg_fwd = [], {}, []

    def to_group(ci):
        rows = piece_rows(*CHUNKS[ci])
        for dy in (2, 1, 3):
            fg_out[ci, dy] = rc(fg_o.at[j, rows], fg_o.at[j, rows], at(dy=dy))
            fg_out[ci, dy].start()
        fg_sib.append(rc(fg_o.at[j, rows], fg_o.at[j, rows], at(dc=1)))
        fg_sib[-1].start()

    to_group(0)
    for k_ in (1, 3, 2):
        wv_fwd[k_].wait_recv()
    for cp in dp_out:
        cp.wait_recv()
    tq = jnp.concatenate([TDQK[2 * F * h : 2 * F * h + F, :] for h in range(H)], 0)
    tk = jnp.concatenate([TDQK[2 * F * h + F : 2 * F * h + 2 * F, :] for h in range(H)], 0)
    TQK[...] = jnp.concatenate([tq, tk], 0).astype(f32).T.astype(bf16)

    def input_grad(i, carry):
        rows = blk(i, 256)
        gi = nt(TDV[...], WV[rows]) + nt(TQK[...], WC[rows, 0:256])
        GI[:, rows] = gi.astype(bf16)
        return carry

    lax.fori_loop(0, D // 256, input_grad, 0)
    gi_copy = pltpu.make_async_copy(GI, gi_o, ls.at[1])
    gi_copy.start()
    for ci in range(1, len(CHUNKS)):
        for k_ in ORDER[slice(*CHUNKS[ci])]:
            zg_out[k_].wait_recv()
        to_group(ci)
    for ci, chunk in enumerate(CHUNKS):
        rows = piece_rows(*chunk)
        for dy in (1, 3, 2):
            fg_out[ci, dy].wait_recv()
            from_j = lax.rem(y + NY - dy, NY) * 2 + c
            cp = rc(fg_o.at[from_j, rows], fg_o.at[from_j, rows], at(dc=1))
            cp.start()
            fg_fwd.append(cp)
    for cp in fg_sib + fg_fwd:
        cp.wait_recv()
    for cp in att_out:
        cp.wait_recv()
    att_mine.wait()
    gi_copy.wait()
    pl.when(jnp.logical_and(last, z < NZ - 1))(halo_z.wait_send)

    @pl.when(jnp.logical_and(last, z > 0))
    def _():
        for cp in halo_g:
            cp.wait_send()

    for k_, cp in s_out.items():
        pl.when(z + k_ < NZ)(cp.wait_send)
    for k_, cp in g_out.items():
        pl.when(z >= k_)(cp.wait_send)
    pl.when(z > 0)(ch_out.wait_send)
    done = [a_sib, relay_up, relay_down] + fg_sib + cot_out + w_fwd + att_out + dp_out + fg_fwd
    for group in (up, down, across, sm_out, wq_out, wk_out, wh_out, wv_out, wv_fwd, x_out, z_out, zg_out, fg_out):
        done += list(group.values())
    for cp in done:
        cp.wait_send()


def unpack(att, gi, fg, att_o, gi_o, gq_o, gk_o, gv_o, tq_o, tk_o, tv_o, gg_o, QTF):
    z = lax.div(lax.axis_index("seq"), GROUP)
    att_o[...] = att[...]
    gi_o[...] = gi[...]
    for i, k in enumerate(ORDER):
        piece = lax.rem(z + NZ - k, NZ)
        band, kind = lax.div(piece, 2), lax.rem(piece, 2)
        rows = pl.ds(pl.multiple_of(piece * 64, 64), 64)
        cols = pl.ds(pl.multiple_of(band * 128, 128), 128)
        for h in range(H):
            base = SMALL + i * PIECE
            gv_o[rows, h * DV : (h + 1) * DV] = fg[h, base : base + 64, :].astype(f32)
            row = pl.ds(pl.multiple_of(kind * 128 + h * F, F), F)
            QTF[row, cols] = fg[h, base + 64 : base + PIECE, :].astype(f32)
    qk_sum = jnp.zeros((8, 128), f32)
    for h in range(H):
        lanes = slice(h * DV, (h + 1) * DV)
        sm = fg[h, 0:SMALL, :].astype(f32)
        qk_sum += sm[0:8]
        tv_o[:, lanes] = sm[6:9]
        gg_o[:, lanes] = sm[9:10]
    tq_o[...] = qk_sum[0:3]
    tk_o[...] = qk_sum[3:6]
    gq_o[...] = QTF[0:128, :].T
    gk_o[...] = QTF[128:256, :].T


N_SEMS = 136


def on_device(a, wq, wk, wv, cq, ck, cv, gain, cot):
    sd = jax.ShapeDtypeStruct
    V = pltpu.VMEM
    vmem, anywhere = pl.BlockSpec(memory_space=V), pl.BlockSpec(memory_space=pl.ANY)
    scratch = [
        V((T + TOK, D), bf16), V((16, 256), bf16), V((16, 256), f32), V((16, 256), bf16),
        V((16, D), f32),
        V((D, 384), bf16), V((D, H * DV), bf16), V((T, DV), bf16),
        V((128, 384), f32), V((384, 128), f32), V((384, T + TOK), f32),
        V((CH, T), f32), V((128, T), f32), V((128, T), bf16), V((T, 128), bf16), V((T, DV), bf16),
        V((DV, T), bf16), V((F, T), bf16), V((PHI, T), bf16), V((PHI, T), bf16),
        V((PHI, DV), bf16), V((NZ - 1, PHI, DV), bf16), V((PHI, DV), f32),
        V((PHI, DV), bf16), V((NZ - 1, PHI, DV), bf16), V((PHI, DV), f32),
        V((T, T), bf16), V((DV, T), f32), V((DV, T), f32), V((DV, T), bf16),
        V((F, T), f32), V((F, T), f32), V((DV, T), f32), V((T, DV), bf16),
        V((CH, T + 2 * TOK), f32), V((CH, TOK), bf16), V((CH, TOK), bf16),
        V((CH, T + TOK), bf16), V((T, DV), bf16), V((TOK, H * DV), bf16),
        V((H * 2 * F, TOK), bf16), V((TOK, H * 2 * F), bf16), V((TOK, D), bf16),
        V((384, 128), f32), V((SMALL, 128), f32), V((SMALL, 128), bf16),
        V((NX - 1, SMALL, 128), bf16),
        V((NX - 1, 4 * CH, 128), bf16), V((NX - 1, 4 * CH, 128), bf16),
        V((4 * CH, 128), f32),
        V((NZ, PIECE + SMALL, 128), bf16), V((NZ - 1, PIECE + SMALL, 128), bf16),
        V((PIECE + SMALL, 128), bf16),
        pltpu.SemaphoreType.DMA((N_SEMS,)), pltpu.SemaphoreType.DMA((N_SEMS,)),
        pltpu.SemaphoreType.DMA((2,)),
    ]
    att, gi, fg = pl.pallas_call(
        kernel,
        out_shape=[
            sd((TOK, H * DV), bf16), sd((TOK, D), bf16), sd((H, FULL, 128), bf16),
        ],
        in_specs=[vmem] * 9,
        out_specs=[anywhere, anywhere, vmem],
        scratch_shapes=scratch,
        compiler_params=pltpu.CompilerParams(
            collective_id=0, has_side_effects=True, vmem_limit_bytes=56 * 2**20
        ),
        name="based_layer",
    )(a.reshape(TOK, D), wq, wk, wv, cq, ck, cv, gain.reshape(1, -1), cot.reshape(TOK, H * DV))
    att, gi, gq, gk, gv, tq, tk, tv, gg = pl.pallas_call(
        unpack,
        out_shape=[
            sd((TOK, H * DV), bf16), sd((TOK, D), bf16),
            sd((ROWS, H * F), f32), sd((ROWS, H * F), f32), sd((ROWS, H * DV), f32),
            sd((3, H * F), f32), sd((3, H * F), f32), sd((3, H * DV), f32), sd((1, H * DV), f32),
        ],
        in_specs=[vmem] * 3,
        out_specs=[vmem] * 9,
        scratch_shapes=[V((256, ROWS), f32)],
        name="unpack",
    )(att, gi, fg)
    return att[None], gi[None], gq, gk, gv, tq, tk, tv, gg.reshape(-1)


def solution(mesh):
    rows = P("fsdp", "seq", None)
    return jax.shard_map(
        on_device,
        mesh=mesh,
        in_specs=(rows, P("fsdp", None), P("fsdp", None), P("fsdp", None), P(), P(), P(), P(), rows),
        out_specs=(
            rows, rows, P("fsdp", None), P("fsdp", None), P("fsdp", None), P(), P(), P(), P(),
        ),
        check_vma=False,
    )
```

```python
import itertools

import jax
import jax.numpy as jnp
from jax import lax
from jax.experimental import pallas as pl
from jax.experimental.pallas import tpu as pltpu
from jax.sharding import PartitionSpec as P

MESH = pl.DeviceIdType.MESH
H, F, DV = 8, 16, 128
NX, NY, NZ, GROUP = 4, 4, 8, 8
TOK, D = 128, 2048
T = GROUP * TOK
ROWS = D // NX
CH = 2 * F + DV
BANDS = F // 2
PHI = F * (BANDS + 2)
SMALL = 16
PIECE = 80
FULL = NZ * PIECE + SMALL
BT = 256
HALF = TOK // 2
ORDER = (0, 1, 7, 2, 6, 3, 5, 4)
CHUNKS = ((0, 1), (1, 3), (3, 5), (5, 8))
FAR_FIRST = (4, 3, 5, 2, 6, 1, 7)
f32, bf16 = jnp.float32, jnp.bfloat16
MATES = [(0, 1), (1, 0), (3, 0), (1, 1), (3, 1), (2, 0), (2, 1)]


def piece_rows(lo, hi):
    return slice(SMALL + lo * PIECE if lo else 0, SMALL + hi * PIECE)


def nn(a, b):
    return lax.dot_general(a, b, (((1,), (0,)), ((), ())), preferred_element_type=f32)


def nt(a, b):
    return lax.dot_general(a, b, (((1,), (1,)), ((), ())), preferred_element_type=f32)


def pair_rows(u, weighted):
    scale = 1.0 / 32.0 if weighted else 1.0
    bands = [scale * u * u]
    for d in range(1, BANDS):
        bands.append((2.0 * scale if weighted else 1.0) * u * pltpu.roll(u, d, 0))
    bands.append((2.0 * scale if weighted else 1.0) * u[:BANDS] * u[BANDS:])
    one = lax.broadcasted_iota(jnp.int32, (F - BANDS, u.shape[1]), 0) == 0
    return jnp.concatenate(bands + [jnp.where(one, 1.0, 0.0), 0.25 * u if weighted else u], 0)


def pair_rows_back(u, grad, weighted):
    scale = 1.0 / 32.0 if weighted else 1.0
    total = grad[F * (BANDS + 1) :] * (0.25 if weighted else 1.0) + 2.0 * scale * grad[:F] * u
    twice = 2.0 * scale if weighted else 1.0
    for d in range(1, BANDS):
        e = twice * grad[F * d : F * (d + 1)]
        total += e * pltpu.roll(u, d, 0) + pltpu.roll(e * u, F - d, 0)
    e = twice * grad[F * BANDS : F * BANDS + BANDS]
    return total + jnp.concatenate([e * u[BANDS:], e * u[:BANDS]], 0)


def kernel(
    a_in, wq_in, wk_in, wv_in, cq_in, ck_in, cv_in, gain_in, cot_in,
    att_o, gi_o, fg_o,
    cq, ck, cv, gain, cot, AS, HS, HF, HR, HA, WC, WV, COT, TPAD, TCOL, PT, XT, KPAD, QPAD, KN, VN, VB, QS, PHQ, PHK,
    SS, SR, SA, GS, GR, GA, WT, OT, COTT, DO, DQ, DK, DVT, ATN, CG, CHS, CHR, DPT, DPN, TDV, TDQK,
    TQK, GI, CM, SMF, SMB, SMR, XS, XR, XO, ZS, ZR, ZB, ss, rs, ls,
):
    s = lax.axis_index("seq")
    f = lax.axis_index("fsdp")
    z, j = lax.div(s, 8), lax.rem(s, 8)
    y, c = lax.div(j, 2), lax.rem(j, 2)
    ids = itertools.count()

    def at(dx=0, dy=0, dz=0, dc=0):
        zz, yy, cc = lax.rem(z + dz + NZ, NZ), lax.rem(y + dy, NY), lax.rem(c + dc, 2)
        return {"seq": (zz * NY + yy) * 2 + cc, "fsdp": lax.rem(f + dx, NX)}

    def mate(dy, dc):
        return lax.rem(y + dy, NY) * 2 + lax.rem(c + dc, 2)

    def rc(src, dst, to):
        i = next(ids)
        return pltpu.make_async_remote_copy(
            src_ref=src, dst_ref=dst, send_sem=ss.at[i], recv_sem=rs.at[i],
            device_id=to, device_id_type=MESH,
        )

    def blk(i, size):
        return pl.ds(pl.multiple_of(i * size, size), size)

    bar = pltpu.get_barrier_semaphore()
    peers = [at(dx=k) for k in range(1, NX)] + [at(dy=dy, dc=dc) for dy, dc in MATES]
    peers += [at(dz=k) for k in range(1, NZ)]
    for p in peers:
        pl.semaphore_signal(bar, inc=1, device_id=p, device_id_type=MESH)
    own_rows, own_w = blk(1 + j, TOK), blk(f, ROWS)
    fetch = [
        pltpu.make_async_copy(src, dst, ls.at[2 + i])
        for i, (src, dst) in enumerate((
            (a_in, AS.at[own_rows]),
            (wq_in, WC.at[own_w, 0:128]),
            (wk_in, WC.at[own_w, 128:256]),
            (wv_in.at[:, blk(j, DV)], WC.at[own_w, 256:384]),
            (wv_in, WV.at[own_w]),
            (cot_in, cot),
            (cq_in, cq), (ck_in, ck), (cv_in, cv), (gain_in, gain),
        ))
    ]
    for cp in fetch:
        cp.start()

    @pl.when(z == 0)
    def _():
        HR[...] = jnp.zeros_like(HR)

    TPAD[...] = jnp.zeros_like(TPAD)
    for cp in fetch:
        cp.wait()
    x = AS[own_rows, :][TOK - 16 :, :].astype(f32)
    for i in range(8):
        HF[2 * i : 2 * i + 2, :] = x[14:16, i * 256 : (i + 1) * 256]
    HS[...] = HF[...].astype(bf16)
    COT[blk(j, TOK)] = cot[:, blk(j, DV)]

    TPAD[0:3, 0:128] = cq[...]
    TPAD[0:3, 128:256] = ck[...]
    TPAD[0:3, 256:384] = cv[:, blk(j, DV)]
    TPAD[3:4, 256:384] = gain[:, blk(j, DV)]
    for i in range(3):
        TCOL[i * 128 : (i + 1) * 128, :] = TPAD[:, i * 128 : (i + 1) * 128].T

    pl.semaphore_wait(bar, len(peers))
    halo_z = rc(HS, HR, at(dz=1))
    halo_g = [rc(HR, HR, at(dy=dy, dc=dc)) for dy, dc in MATES]
    last = j == GROUP - 1

    @pl.when(jnp.logical_and(last, z < NZ - 1))
    def _():
        halo_z.start()

    def tok_rows(chip_y, part=None):
        base = (1 + lax.rem(chip_y + NY, NY) * 2 + c) * TOK
        if part is None:
            return pl.ds(pl.multiple_of(base, TOK), TOK)
        return pl.ds(pl.multiple_of(base + part * HALF, HALF), HALF)

    mine = tok_rows(y)
    a_sib = rc(AS.at[mine], AS.at[mine], at(dc=1))
    up, down = {}, {}
    for p_ in (0, 1):
        src = AS.at[tok_rows(y, p_)]
        up[p_] = rc(src, AS.at[tok_rows(y, p_)], at(dy=1))
        down[p_] = rc(src, AS.at[tok_rows(y, p_)], at(dy=3))
    relay_up = rc(AS.at[tok_rows(y - 1, 0)], AS.at[tok_rows(y - 1, 0)], at(dy=1))
    relay_down = rc(AS.at[tok_rows(y + 1, 1)], AS.at[tok_rows(y + 1, 1)], at(dy=3))
    across = {}
    for name, rows in (
        ("up", tok_rows(y - 1)), ("down", tok_rows(y + 1)),
        ("far0", tok_rows(y + 2, 0)), ("far1", tok_rows(y + 2, 1)),
    ):
        across[name] = rc(AS.at[rows], AS.at[rows], at(dc=1))
    up[0].start()
    down[1].start()
    up[1].start()
    down[0].start()
    a_sib.start()
    mine_half = blk(2 * f + c, ROWS // 2)
    wqk_out, wh_out, wv_out = {}, {}, {}
    for k in (1, 3, 2):
        wqk_out[k] = rc(WC.at[mine_half, 0:256], WC.at[mine_half, 0:256], at(dx=k))
        wh_out[k] = rc(WC.at[own_w, 256:384], WC.at[own_w, 256:384], at(dx=k))
        wv_out[k] = rc(WV.at[mine_half], WV.at[mine_half], at(dx=k))
    for k in (1, 3, 2):
        wqk_out[k].start()
    for k in (1, 3, 2):
        wh_out[k].start()
    cot_out = [
        rc(cot.at[:, blk(mate(dy, dc), DV)], COT.at[blk(j, TOK)], at(dy=dy, dc=dc))
        for dy, dc in MATES
    ]

    @pl.when(jnp.logical_and(last, z > 0))
    def _():
        halo_z.wait_recv()
        for cp in halo_g:
            cp.start()

    up[0].wait_recv()
    relay_up.start()
    down[1].wait_recv()
    relay_down.start()
    w_fwd, wv_fwd = [], {}
    for k in (1, 3, 2):
        from_x = lax.rem(f + NX - k, NX)
        rows = blk(2 * from_x + c, ROWS // 2)
        wqk_out[k].wait_recv()
        cp = rc(WC.at[rows, 0:256], WC.at[rows, 0:256], at(dc=1))
        cp.start()
        w_fwd.append(cp)
        wv_fwd[k] = rc(WV.at[rows], WV.at[rows], at(dc=1))
    up[1].wait_recv()
    across["up"].start()
    down[0].wait_recv()
    across["down"].start()
    for k in (1, 3, 2):
        wh_out[k].wait_recv()
    for k in (1, 3, 2):
        wv_out[k].start()
    a_sib.wait_recv()
    for cp in w_fwd:
        cp.wait_recv()

    def project(chip_y):
        chip = lax.rem(chip_y + NY, NY)
        p = nn(AS[pl.ds(pl.multiple_of(TOK + chip * 2 * TOK, TOK), 2 * TOK)], WC[...])
        cols = pl.ds(pl.multiple_of(TOK + chip * 2 * TOK, TOK), 2 * TOK)
        PT[:, cols] = p.astype(bf16).astype(f32).T

    project(y)
    across["up"].wait_recv()
    project(y - 1)
    across["down"].wait_recv()
    project(y + 1)
    relay_up.wait_recv()
    across["far0"].start()
    relay_down.wait_recv()
    across["far1"].start()
    for cp in cot_out:
        cp.start()

    @pl.when(jnp.logical_and(jnp.logical_not(last), z > 0))
    def _():
        for (dy, dc), cp in zip(MATES, halo_g):
            from_j = lax.rem(y + NY - dy, NY) * 2 + lax.rem(c + dc, 2)

            @pl.when(from_j == GROUP - 1)
            def _():
                cp.wait_recv()

    HF[...] = HR[...].astype(f32)
    HA[...] = jnp.zeros_like(HA)
    for i in range(8):
        HA[14:16, i * 256 : (i + 1) * 256] = HF[2 * i : 2 * i + 2, :]
    AS[0 : TOK - 16] = jnp.zeros((TOK - 16, D), bf16)
    AS[TOK - 16 : TOK] = HA[...].astype(bf16)
    ph = nn(AS[TOK - 16 : TOK], WC[...]).astype(bf16).astype(f32)
    PT[:, 0:TOK] = jnp.concatenate([jnp.zeros((TOK - 16, 384), f32), ph], 0).T
    across["far0"].wait_recv()
    across["far1"].wait_recv()
    project(y + 2)

    q_rows, k_rows = blk(j, F), pl.ds(pl.multiple_of(128 + j * F, F), F)
    parts = ((q_rows, 0, F), (k_rows, F, F), (pl.ds(256, DV), 2 * F, DV))
    for rows, to, size in parts:
        p, taps = PT[rows, :], TCOL[rows, :]
        XT[to : to + size, :] = (
            taps[:, 0:1] * p[:, TOK:]
            + taps[:, 1:2] * pltpu.roll(p, 1, 1)[:, TOK:]
            + taps[:, 2:3] * pltpu.roll(p, 2, 1)[:, TOK:]
        )
    q, k, v = XT[0:F, :], XT[F : 2 * F, :], XT[2 * F :, :]
    VB[...] = v.astype(bf16)
    PHK[...] = pair_rows(k, False).astype(bf16)
    SS[...] = nt(PHK[...], VB[...]).astype(bf16)
    s_out = {k: rc(SS, SR.at[k - 1], at(dz=k)) for k in FAR_FIRST}
    for k_, cp in s_out.items():
        pl.when(z + k_ < NZ)(cp.start)
    PHQ[...] = pair_rows(q, True).astype(bf16)
    KPAD[...] = jnp.zeros_like(KPAD)
    KPAD[0:F, :] = k
    KN[...] = KPAD[...].T.astype(bf16)
    QPAD[...] = jnp.zeros_like(QPAD)
    QPAD[0:F, :] = (0.25 * q).astype(bf16)
    QS[...] = k.astype(bf16)
    VN[...] = v.T.astype(bf16)
    COTT[...] = jnp.zeros_like(COTT)
    seen = lax.broadcasted_iota(jnp.int32, (BT, BT), 0) <= lax.broadcasted_iota(
        jnp.int32, (BT, BT), 1
    )

    def causal(block):
        n = block.shape[0]
        tail = jnp.where(seen, block[n - BT :], 0.0)
        return tail if n == BT else jnp.concatenate([block[: n - BT], tail], 0)

    for tb in range(T // BT):
        n, cols = (tb + 1) * BT, slice(tb * BT, (tb + 1) * BT)
        sc = nn(KN[:n, :], QPAD[:, cols])
        w = causal(1.0 + sc * (1.0 + 0.5 * sc)).astype(bf16)
        WT[:n, cols] = w
        OT[:, cols] = nn(VB[:, :n], w)
    for cp in cot_out:
        cp.wait_recv()
    COTT[...] = COT[...].astype(f32).T
    SA[...] = jnp.zeros_like(SA)
    for k_, cp in s_out.items():

        @pl.when(z >= k_)
        def _():
            cp.wait_recv()
            SA[...] += SR[k_ - 1].astype(f32)

    gcol = TCOL[256:384, 3:4]
    o = OT[...] + nn(SA[...].T.astype(bf16), PHQ[...])
    r = lax.rsqrt(jnp.mean(o * o, 0, keepdims=True) + 1e-06)
    hat = o * r
    ct = COTT[...]
    gain_grad = jnp.sum(ct * hat, 1, keepdims=True)
    gn = ct * gcol
    DO[...] = (r * (gn - hat * jnp.mean(gn * hat, 0, keepdims=True))).astype(bf16)
    GS[...] = nt(PHQ[...], DO[...]).astype(bf16)
    g_out = {k: rc(GS, GR.at[k - 1], at(dz=NZ - k)) for k in FAR_FIRST}
    for k_, cp in g_out.items():
        pl.when(z >= k_)(cp.start)
    ATN[...] = (hat * gcol).T.astype(bf16)
    att_out = [
        rc(ATN.at[blk(mate(dy, dc), TOK)], att_o.at[:, blk(j, DV)], at(dy=dy, dc=dc))
        for dy, dc in MATES
    ]
    for cp in att_out:
        cp.start()
    att_mine = pltpu.make_async_copy(ATN.at[blk(j, TOK)], att_o.at[:, blk(j, DV)], ls.at[0])
    att_mine.start()
    DQ[...] = pair_rows_back(q, nn(SA[...].astype(bf16), DO[...]), True)
    DK[...] = jnp.zeros_like(DK)
    DVT[...] = jnp.zeros_like(DVT)
    for tb in range(T // BT):
        n, cols = (tb + 1) * BT, slice(tb * BT, (tb + 1) * BT)
        sc = nn(KN[:n, :], QPAD[:, cols])
        ds = causal(nn(VN[:n, :], DO[:, cols]) * (1.0 + sc)).astype(bf16)
        DQ[:, cols] += 0.25 * nn(QS[:, :n], ds)
        DK[:, :n] += nt(QPAD[0:F, cols], ds)
        DVT[:, :n] += nt(DO[:, cols], WT[:n, cols])
    GA[...] = jnp.zeros_like(GA)
    for k_, cp in g_out.items():

        @pl.when(z + k_ < NZ)
        def _():
            cp.wait_recv()
            GA[...] += GR[k_ - 1].astype(f32)

    dk = DK[...] + pair_rows_back(k, nn(GA[...].astype(bf16), VB[...]), False)
    CG[0:F, TOK : TOK + T] = DQ[...]
    CG[F : 2 * F, TOK : TOK + T] = dk
    CG[2 * F :, TOK : TOK + T] = DVT[...] + nn(GA[...].T.astype(bf16), PHK[...])
    CHS[...] = CG[:, TOK : 2 * TOK].astype(bf16)
    ch_out = rc(CHS, CHR, at(dz=NZ - 1))
    pl.when(z > 0)(ch_out.start)
    CG[:, 0:TOK] = jnp.zeros((CH, TOK), f32)
    CG[:, TOK + T :] = jnp.zeros((CH, TOK), f32)

    def conv_back(rows, to, size, first, count):
        g, taps = CG[to : to + size, first : first + count + TOK], TCOL[rows, :]
        n = count + TOK
        return (
            taps[:, 0:1] * g[:, :count]
            + taps[:, 1:2] * pltpu.roll(g, n - 1, 1)[:, :count]
            + taps[:, 2:3] * pltpu.roll(g, n - 2, 1)[:, :count]
        )

    for rows, to, size in parts:
        DPT[to : to + size, :] = conv_back(rows, to, size, 0, T + TOK).astype(bf16)
    x_out = {k: rc(XS.at[k - 1], XR.at[k - 1], at(dx=k)) for k in (1, 3, 2)}

    sm_out = {k: rc(SMB, SMR.at[k - 1], at(dx=k)) for k in (1, 3, 2)}
    SMF[...] = jnp.zeros_like(SMF)

    def weight_part(to_x):
        return nn(DPT[...], AS[:, blk(to_x, ROWS)])

    for k_ in (2, 1, 3):
        part = weight_part(lax.rem(f + k_, NX)).astype(bf16)
        for b in range(4):
            XS[k_ - 1, b * CH : (b + 1) * CH, :] = part[:, b * 128 : (b + 1) * 128]
        x_out[k_].start()
    part = weight_part(f)
    for b in range(4):
        XO[b * CH : (b + 1) * CH, :] = part[:, b * 128 : (b + 1) * 128]
    lane = lax.broadcasted_iota(jnp.int32, (DV, 128), 1)
    CM[...] = jnp.zeros_like(CM)
    for rows, to, size in parts:
        p, g = PT[rows, :], CG[to : to + size, TOK : TOK + T]
        sums = [
            jnp.sum(g * (pltpu.roll(p, i, 1) if i else p)[:, TOK:], 1, keepdims=True)
            for i in range(3)
        ]
        if size == DV:
            sums.append(gain_grad)
        tile = jnp.zeros((size, 128), f32)
        for i, col in enumerate(sums):
            tile = jnp.where(lane[:size] == i, col, tile)
        CM[rows, :] = tile
    for i, (lo, n) in enumerate(((0, 3), (3, 3), (6, 4))):
        SMF[lo : lo + n, :] = CM[i * 128 : (i + 1) * 128, :].T[0:n, :]
    SMB[...] = SMF[...].astype(bf16)
    for cp in sm_out.values():
        cp.start()

    @pl.when(z < NZ - 1)
    def _():
        ch_out.wait_recv()
        CG[:, TOK + T :] = CHR[...].astype(f32)

    for rows, to, size in parts:
        DPT[to : to + size, T:] = conv_back(rows, to, size, T, TOK).astype(bf16)
    DPN[...] = DPT[2 * F :, TOK:].astype(f32).T.astype(bf16)
    dp_out = []
    for dy, dc in MATES:
        m = mate(dy, dc)
        dp_out.append(rc(DPN.at[blk(m, TOK)], TDV.at[:, blk(j, DV)], at(dy=dy, dc=dc)))
        dp_out.append(
            rc(DPT.at[0 : 2 * F, blk(1 + m, TOK)], TDQK.at[blk(j, 2 * F)], at(dy=dy, dc=dc))
        )
    for cp in dp_out:
        cp.start()
    TDV[:, blk(j, DV)] = DPN[blk(j, TOK)]
    TDQK[blk(j, 2 * F)] = DPT[0 : 2 * F, blk(1 + j, TOK)]
    for k_ in (1, 3, 2):
        wv_out[k_].wait_recv()
        wv_fwd[k_].start()
    for k_ in (1, 3, 2):
        x_out[k_].wait_recv()
        XO[...] += XR[k_ - 1].astype(f32)
        sm_out[k_].wait_recv()
        SMF[...] += SMR[k_ - 1].astype(f32)
    for b in range(4):
        nat = XO[b * CH + 2 * F : (b + 1) * CH, :].T
        for i in range(2):
            ZS[2 * b + i, 0:64, :] = nat[i * 64 : (i + 1) * 64].astype(bf16)
            ZS[2 * b + i, 64:PIECE, :] = XO[b * CH + F * i : b * CH + F * (i + 1), :].astype(bf16)
            ZS[2 * b + i, PIECE:, :] = SMF[...].astype(bf16)
    z_out = {
        k: rc(ZS.at[lax.rem(z + k, NZ)], ZR.at[k - 1], at(dz=k)) for k in FAR_FIRST
    }
    for cp in z_out.values():
        cp.start()
    red = ZS[z].astype(f32)
    for k_, cp in z_out.items():
        cp.wait_recv()
        red += ZR[k_ - 1].astype(f32)
    ZB[...] = red.astype(bf16)
    zg_out = {
        k: rc(ZB.at[0:PIECE], fg_o.at[j, piece_rows(ORDER.index(k), ORDER.index(k) + 1)], at(dz=k))
        for k in ORDER[1:]
    }
    for cp in zg_out.values():
        cp.start()
    fg_o[j, 0:SMALL, :] = ZB[PIECE:, :]
    fg_o[j, SMALL : SMALL + PIECE, :] = ZB[0:PIECE, :]
    fg_sib, fg_out, fg_fwd = [], {}, []

    def to_group(ci):
        rows = piece_rows(*CHUNKS[ci])
        for dy in (2, 1, 3):
            fg_out[ci, dy] = rc(fg_o.at[j, rows], fg_o.at[j, rows], at(dy=dy))
            fg_out[ci, dy].start()
        fg_sib.append(rc(fg_o.at[j, rows], fg_o.at[j, rows], at(dc=1)))
        fg_sib[-1].start()

    to_group(0)
    for k_ in (1, 3, 2):
        wv_fwd[k_].wait_recv()
    for cp in dp_out:
        cp.wait_recv()
    tq = jnp.concatenate([TDQK[2 * F * h : 2 * F * h + F, :] for h in range(H)], 0)
    tk = jnp.concatenate([TDQK[2 * F * h + F : 2 * F * h + 2 * F, :] for h in range(H)], 0)
    TQK[...] = jnp.concatenate([tq, tk], 0).astype(f32).T.astype(bf16)

    def input_grad(i, carry):
        rows = blk(i, 256)
        gi = nt(TDV[...], WV[rows]) + nt(TQK[...], WC[rows, 0:256])
        GI[:, rows] = gi.astype(bf16)
        return carry

    lax.fori_loop(0, D // 256, input_grad, 0)
    gi_copy = pltpu.make_async_copy(GI, gi_o, ls.at[1])
    gi_copy.start()
    for ci in range(1, len(CHUNKS)):
        for k_ in ORDER[slice(*CHUNKS[ci])]:
            zg_out[k_].wait_recv()
        to_group(ci)
    for ci, chunk in enumerate(CHUNKS):
        rows = piece_rows(*chunk)
        for dy in (1, 3, 2):
            fg_out[ci, dy].wait_recv()
            from_j = lax.rem(y + NY - dy, NY) * 2 + c
            cp = rc(fg_o.at[from_j, rows], fg_o.at[from_j, rows], at(dc=1))
            cp.start()
            fg_fwd.append(cp)
    for cp in fg_sib + fg_fwd:
        cp.wait_recv()
    for cp in att_out:
        cp.wait_recv()
    att_mine.wait()
    gi_copy.wait()
    pl.when(jnp.logical_and(last, z < NZ - 1))(halo_z.wait_send)

    @pl.when(jnp.logical_and(last, z > 0))
    def _():
        for cp in halo_g:
            cp.wait_send()

    for k_, cp in s_out.items():
        pl.when(z + k_ < NZ)(cp.wait_send)
    for k_, cp in g_out.items():
        pl.when(z >= k_)(cp.wait_send)
    pl.when(z > 0)(ch_out.wait_send)
    done = [a_sib, relay_up, relay_down] + fg_sib + cot_out + w_fwd + att_out + dp_out + fg_fwd
    for group in (up, down, across, sm_out, wqk_out, wh_out, wv_out, wv_fwd, x_out, z_out, zg_out, fg_out):
        done += list(group.values())
    for cp in done:
        cp.wait_send()


def unpack(att, gi, fg, att_o, gi_o, gq_o, gk_o, gv_o, tq_o, tk_o, tv_o, gg_o, QTF):
    z = lax.div(lax.axis_index("seq"), GROUP)
    att_o[...] = att[...]
    gi_o[...] = gi[...]
    for i, k in enumerate(ORDER):
        piece = lax.rem(z + NZ - k, NZ)
        band, kind = lax.div(piece, 2), lax.rem(piece, 2)
        rows = pl.ds(pl.multiple_of(piece * 64, 64), 64)
        cols = pl.ds(pl.multiple_of(band * 128, 128), 128)
        for h in range(H):
            base = SMALL + i * PIECE
            gv_o[rows, h * DV : (h + 1) * DV] = fg[h, base : base + 64, :].astype(f32)
            row = pl.ds(pl.multiple_of(kind * 128 + h * F, F), F)
            QTF[row, cols] = fg[h, base + 64 : base + PIECE, :].astype(f32)
    qk_sum = jnp.zeros((8, 128), f32)
    for h in range(H):
        lanes = slice(h * DV, (h + 1) * DV)
        sm = fg[h, 0:SMALL, :].astype(f32)
        qk_sum += sm[0:8]
        tv_o[:, lanes] = sm[6:9]
        gg_o[:, lanes] = sm[9:10]
    tq_o[...] = qk_sum[0:3]
    tk_o[...] = qk_sum[3:6]
    gq_o[...] = QTF[0:128, :].T
    gk_o[...] = QTF[128:256, :].T


N_SEMS = 136


def on_device(a, wq, wk, wv, cq, ck, cv, gain, cot):
    sd = jax.ShapeDtypeStruct
    V = pltpu.VMEM
    vmem, anywhere = pl.BlockSpec(memory_space=V), pl.BlockSpec(memory_space=pl.ANY)
    scratch = [
        V((3, H * F), f32), V((3, H * F), f32), V((3, H * DV), f32), V((1, H * DV), f32),
        V((TOK, H * DV), bf16),
        V((T + TOK, D), bf16), V((16, 256), bf16), V((16, 256), f32), V((16, 256), bf16),
        V((16, D), f32),
        V((D, 384), bf16), V((D, H * DV), bf16), V((T, DV), bf16),
        V((128, 384), f32), V((384, 128), f32), V((384, T + TOK), f32),
        V((CH, T), f32), V((128, T), f32), V((128, T), bf16), V((T, 128), bf16), V((T, DV), bf16),
        V((DV, T), bf16), V((F, T), bf16), V((PHI, T), bf16), V((PHI, T), bf16),
        V((PHI, DV), bf16), V((NZ - 1, PHI, DV), bf16), V((PHI, DV), f32),
        V((PHI, DV), bf16), V((NZ - 1, PHI, DV), bf16), V((PHI, DV), f32),
        V((T, T), bf16), V((DV, T), f32), V((DV, T), f32), V((DV, T), bf16),
        V((F, T), f32), V((F, T), f32), V((DV, T), f32), V((T, DV), bf16),
        V((CH, T + 2 * TOK), f32), V((CH, TOK), bf16), V((CH, TOK), bf16),
        V((CH, T + TOK), bf16), V((T, DV), bf16), V((TOK, H * DV), bf16),
        V((H * 2 * F, TOK), bf16), V((TOK, H * 2 * F), bf16), V((TOK, D), bf16),
        V((384, 128), f32), V((SMALL, 128), f32), V((SMALL, 128), bf16),
        V((NX - 1, SMALL, 128), bf16),
        V((NX - 1, 4 * CH, 128), bf16), V((NX - 1, 4 * CH, 128), bf16),
        V((4 * CH, 128), f32),
        V((NZ, PIECE + SMALL, 128), bf16), V((NZ - 1, PIECE + SMALL, 128), bf16),
        V((PIECE + SMALL, 128), bf16),
        pltpu.SemaphoreType.DMA((N_SEMS,)), pltpu.SemaphoreType.DMA((N_SEMS,)),
        pltpu.SemaphoreType.DMA((12,)),
    ]
    att, gi, fg = pl.pallas_call(
        kernel,
        out_shape=[
            sd((TOK, H * DV), bf16), sd((TOK, D), bf16), sd((H, FULL, 128), bf16),
        ],
        in_specs=[anywhere] * 9,
        out_specs=[anywhere, anywhere, vmem],
        scratch_shapes=scratch,
        compiler_params=pltpu.CompilerParams(
            collective_id=0, has_side_effects=True, vmem_limit_bytes=56 * 2**20
        ),
        name="based_layer",
    )(a.reshape(TOK, D), wq, wk, wv, cq, ck, cv, gain.reshape(1, -1), cot.reshape(TOK, H * DV))
    att, gi, gq, gk, gv, tq, tk, tv, gg = pl.pallas_call(
        unpack,
        out_shape=[
            sd((TOK, H * DV), bf16), sd((TOK, D), bf16),
            sd((ROWS, H * F), f32), sd((ROWS, H * F), f32), sd((ROWS, H * DV), f32),
            sd((3, H * F), f32), sd((3, H * F), f32), sd((3, H * DV), f32), sd((1, H * DV), f32),
        ],
        in_specs=[vmem] * 3,
        out_specs=[vmem] * 9,
        scratch_shapes=[V((256, ROWS), f32)],
        name="unpack",
    )(att, gi, fg)
    return att[None], gi[None], gq, gk, gv, tq, tk, tv, gg.reshape(-1)


def solution(mesh):
    rows = P("fsdp", "seq", None)
    return jax.shard_map(
        on_device,
        mesh=mesh,
        in_specs=(rows, P("fsdp", None), P("fsdp", None), P("fsdp", None), P(), P(), P(), P(), rows),
        out_specs=(
            rows, rows, P("fsdp", None), P("fsdp", None), P("fsdp", None), P(), P(), P(), P(),
        ),
        check_vma=False,
    )
```

```python
import itertools

import jax
import jax.numpy as jnp
from jax import lax
from jax.experimental import pallas as pl
from jax.experimental.pallas import tpu as pltpu
from jax.sharding import PartitionSpec as P

MESH = pl.DeviceIdType.MESH
H, F, DV = 8, 16, 128
NX, NY, NZ, GROUP = 4, 4, 8, 8
TOK, D = 128, 2048
T = GROUP * TOK
ROWS = D // NX
CH = 2 * F + DV
BANDS = F // 2
PHI = F * (BANDS + 2)
SMALL = 16
PIECE = 80
FULL = NZ * PIECE + SMALL
BT = 256
HALF = TOK // 2
ORDER = (0, 1, 7, 2, 6, 3, 5, 4)
CHUNKS = ((0, 1), (1, 3), (3, 5), (5, 8))
FAR_FIRST = (4, 3, 5, 2, 6, 1, 7)
f32, bf16 = jnp.float32, jnp.bfloat16
MATES = [(0, 1), (1, 0), (3, 0), (1, 1), (3, 1), (2, 0), (2, 1)]


def piece_rows(lo, hi):
    return slice(SMALL + lo * PIECE if lo else 0, SMALL + hi * PIECE)


def nn(a, b):
    return lax.dot_general(a, b, (((1,), (0,)), ((), ())), preferred_element_type=f32)


def nt(a, b):
    return lax.dot_general(a, b, (((1,), (1,)), ((), ())), preferred_element_type=f32)


def pair_rows(u, weighted):
    scale = 1.0 / 32.0 if weighted else 1.0
    bands = [scale * u * u]
    for d in range(1, BANDS):
        bands.append((2.0 * scale if weighted else 1.0) * u * pltpu.roll(u, d, 0))
    bands.append((2.0 * scale if weighted else 1.0) * u[:BANDS] * u[BANDS:])
    one = lax.broadcasted_iota(jnp.int32, (F - BANDS, u.shape[1]), 0) == 0
    return jnp.concatenate(bands + [jnp.where(one, 1.0, 0.0), 0.25 * u if weighted else u], 0)


def pair_rows_back(u, grad, weighted):
    scale = 1.0 / 32.0 if weighted else 1.0
    total = grad[F * (BANDS + 1) :] * (0.25 if weighted else 1.0) + 2.0 * scale * grad[:F] * u
    twice = 2.0 * scale if weighted else 1.0
    for d in range(1, BANDS):
        e = twice * grad[F * d : F * (d + 1)]
        total += e * pltpu.roll(u, d, 0) + pltpu.roll(e * u, F - d, 0)
    e = twice * grad[F * BANDS : F * BANDS + BANDS]
    return total + jnp.concatenate([e * u[BANDS:], e * u[:BANDS]], 0)


def kernel(
    a_in, wq_in, wk_in, wv_in, cq_in, ck_in, cv_in, gain_in, cot_in,
    att_o, gi_o, fg_out_o,
    fg_o, cq, ck, cv, gain, cot, AS, HS, HF, HR, HA, WC, WV, COT, TPAD, TCOL, PT, XT, KPAD, QPAD, KN, VN, VB, QS, PHQ, PHK,
    SS, SR, SA, GS, GR, GA, WT, OT, COTT, DO, DQ, DK, DVT, ATN, CG, CHS, CHR, DPT, DPN, TDV, TDQK,
    TQK, GI, CM, SMF, SMB, SMR, XS, XR, XO, ZS, ZR, ZB, ss, rs, ls,
):
    s = lax.axis_index("seq")
    f = lax.axis_index("fsdp")
    z, j = lax.div(s, 8), lax.rem(s, 8)
    y, c = lax.div(j, 2), lax.rem(j, 2)
    ids = itertools.count()

    def at(dx=0, dy=0, dz=0, dc=0):
        zz, yy, cc = lax.rem(z + dz + NZ, NZ), lax.rem(y + dy, NY), lax.rem(c + dc, 2)
        return {"seq": (zz * NY + yy) * 2 + cc, "fsdp": lax.rem(f + dx, NX)}

    def mate(dy, dc):
        return lax.rem(y + dy, NY) * 2 + lax.rem(c + dc, 2)

    def rc(src, dst, to):
        i = next(ids)
        return pltpu.make_async_remote_copy(
            src_ref=src, dst_ref=dst, send_sem=ss.at[i], recv_sem=rs.at[i],
            device_id=to, device_id_type=MESH,
        )

    def blk(i, size):
        return pl.ds(pl.multiple_of(i * size, size), size)

    bar = pltpu.get_barrier_semaphore()
    peers = [at(dx=k) for k in range(1, NX)] + [at(dy=dy, dc=dc) for dy, dc in MATES]
    peers += [at(dz=k) for k in range(1, NZ)]
    for p in peers:
        pl.semaphore_signal(bar, inc=1, device_id=p, device_id_type=MESH)
    own_rows, own_w = blk(1 + j, TOK), blk(f, ROWS)
    fetch = [
        pltpu.make_async_copy(src, dst, ls.at[2 + i])
        for i, (src, dst) in enumerate((
            (a_in, AS.at[own_rows]),
            (wq_in, WC.at[own_w, 0:128]),
            (wk_in, WC.at[own_w, 128:256]),
            (wv_in.at[:, blk(j, DV)], WC.at[own_w, 256:384]),
            (wv_in, WV.at[own_w]),
            (cot_in, cot),
            (cq_in, cq), (ck_in, ck), (cv_in, cv), (gain_in, gain),
        ))
    ]
    for cp in fetch:
        cp.start()

    @pl.when(z == 0)
    def _():
        HR[...] = jnp.zeros_like(HR)

    TPAD[...] = jnp.zeros_like(TPAD)
    for cp in fetch:
        cp.wait()
    x = AS[own_rows, :][TOK - 16 :, :].astype(f32)
    for i in range(8):
        HF[2 * i : 2 * i + 2, :] = x[14:16, i * 256 : (i + 1) * 256]
    HS[...] = HF[...].astype(bf16)
    COT[blk(j, TOK)] = cot[:, blk(j, DV)]

    TPAD[0:3, 0:128] = cq[...]
    TPAD[0:3, 128:256] = ck[...]
    TPAD[0:3, 256:384] = cv[:, blk(j, DV)]
    TPAD[3:4, 256:384] = gain[:, blk(j, DV)]
    for i in range(3):
        TCOL[i * 128 : (i + 1) * 128, :] = TPAD[:, i * 128 : (i + 1) * 128].T

    pl.semaphore_wait(bar, len(peers))
    halo_z = rc(HS, HR, at(dz=1))
    halo_g = [rc(HR, HR, at(dy=dy, dc=dc)) for dy, dc in MATES]
    last = j == GROUP - 1

    @pl.when(jnp.logical_and(last, z < NZ - 1))
    def _():
        halo_z.start()

    def tok_rows(chip_y, part=None):
        base = (1 + lax.rem(chip_y + NY, NY) * 2 + c) * TOK
        if part is None:
            return pl.ds(pl.multiple_of(base, TOK), TOK)
        return pl.ds(pl.multiple_of(base + part * HALF, HALF), HALF)

    mine = tok_rows(y)
    a_sib = rc(AS.at[mine], AS.at[mine], at(dc=1))
    up, down = {}, {}
    for p_ in (0, 1):
        src = AS.at[tok_rows(y, p_)]
        up[p_] = rc(src, AS.at[tok_rows(y, p_)], at(dy=1))
        down[p_] = rc(src, AS.at[tok_rows(y, p_)], at(dy=3))
    relay_up = rc(AS.at[tok_rows(y - 1, 0)], AS.at[tok_rows(y - 1, 0)], at(dy=1))
    relay_down = rc(AS.at[tok_rows(y + 1, 1)], AS.at[tok_rows(y + 1, 1)], at(dy=3))
    across = {}
    for name, rows in (
        ("up", tok_rows(y - 1)), ("down", tok_rows(y + 1)),
        ("far0", tok_rows(y + 2, 0)), ("far1", tok_rows(y + 2, 1)),
    ):
        across[name] = rc(AS.at[rows], AS.at[rows], at(dc=1))
    up[0].start()
    down[1].start()
    up[1].start()
    down[0].start()
    a_sib.start()
    mine_half = blk(2 * f + c, ROWS // 2)
    wqk_out, wh_out, wv_out = {}, {}, {}
    for k in (1, 3, 2):
        wqk_out[k] = rc(WC.at[mine_half, 0:256], WC.at[mine_half, 0:256], at(dx=k))
        wh_out[k] = rc(WC.at[own_w, 256:384], WC.at[own_w, 256:384], at(dx=k))
        wv_out[k] = rc(WV.at[mine_half], WV.at[mine_half], at(dx=k))
    for k in (1, 3, 2):
        wqk_out[k].start()
    for k in (1, 3, 2):
        wh_out[k].start()
    cot_out = [
        rc(cot.at[:, blk(mate(dy, dc), DV)], COT.at[blk(j, TOK)], at(dy=dy, dc=dc))
        for dy, dc in MATES
    ]

    @pl.when(jnp.logical_and(last, z > 0))
    def _():
        halo_z.wait_recv()
        for cp in halo_g:
            cp.start()

    up[0].wait_recv()
    relay_up.start()
    down[1].wait_recv()
    relay_down.start()
    w_fwd, wv_fwd = [], {}
    for k in (1, 3, 2):
        from_x = lax.rem(f + NX - k, NX)
        rows = blk(2 * from_x + c, ROWS // 2)
        wqk_out[k].wait_recv()
        cp = rc(WC.at[rows, 0:256], WC.at[rows, 0:256], at(dc=1))
        cp.start()
        w_fwd.append(cp)
        wv_fwd[k] = rc(WV.at[rows], WV.at[rows], at(dc=1))
    up[1].wait_recv()
    across["up"].start()
    down[0].wait_recv()
    across["down"].start()
    for k in (1, 3, 2):
        wh_out[k].wait_recv()
    for k in (1, 3, 2):
        wv_out[k].start()
    a_sib.wait_recv()
    for cp in w_fwd:
        cp.wait_recv()

    def project(chip_y):
        chip = lax.rem(chip_y + NY, NY)
        p = nn(AS[pl.ds(pl.multiple_of(TOK + chip * 2 * TOK, TOK), 2 * TOK)], WC[...])
        cols = pl.ds(pl.multiple_of(TOK + chip * 2 * TOK, TOK), 2 * TOK)
        PT[:, cols] = p.astype(bf16).astype(f32).T

    project(y)
    across["up"].wait_recv()
    project(y - 1)
    across["down"].wait_recv()
    project(y + 1)
    relay_up.wait_recv()
    across["far0"].start()
    relay_down.wait_recv()
    across["far1"].start()
    for cp in cot_out:
        cp.start()

    @pl.when(jnp.logical_and(jnp.logical_not(last), z > 0))
    def _():
        for (dy, dc), cp in zip(MATES, halo_g):
            from_j = lax.rem(y + NY - dy, NY) * 2 + lax.rem(c + dc, 2)

            @pl.when(from_j == GROUP - 1)
            def _():
                cp.wait_recv()

    HF[...] = HR[...].astype(f32)
    HA[...] = jnp.zeros_like(HA)
    for i in range(8):
        HA[14:16, i * 256 : (i + 1) * 256] = HF[2 * i : 2 * i + 2, :]
    AS[0 : TOK - 16] = jnp.zeros((TOK - 16, D), bf16)
    AS[TOK - 16 : TOK] = HA[...].astype(bf16)
    ph = nn(AS[TOK - 16 : TOK], WC[...]).astype(bf16).astype(f32)
    PT[:, 0:TOK] = jnp.concatenate([jnp.zeros((TOK - 16, 384), f32), ph], 0).T
    across["far0"].wait_recv()
    across["far1"].wait_recv()
    project(y + 2)

    q_rows, k_rows = blk(j, F), pl.ds(pl.multiple_of(128 + j * F, F), F)
    parts = ((q_rows, 0, F), (k_rows, F, F), (pl.ds(256, DV), 2 * F, DV))
    for rows, to, size in parts:
        p, taps = PT[rows, :], TCOL[rows, :]
        XT[to : to + size, :] = (
            taps[:, 0:1] * p[:, TOK:]
            + taps[:, 1:2] * pltpu.roll(p, 1, 1)[:, TOK:]
            + taps[:, 2:3] * pltpu.roll(p, 2, 1)[:, TOK:]
        )
    q, k, v = XT[0:F, :], XT[F : 2 * F, :], XT[2 * F :, :]
    VB[...] = v.astype(bf16)
    PHK[...] = pair_rows(k, False).astype(bf16)
    SS[...] = nt(PHK[...], VB[...]).astype(bf16)
    s_out = {k: rc(SS, SR.at[k - 1], at(dz=k)) for k in FAR_FIRST}
    for k_, cp in s_out.items():
        pl.when(z + k_ < NZ)(cp.start)
    PHQ[...] = pair_rows(q, True).astype(bf16)
    KPAD[...] = jnp.zeros_like(KPAD)
    KPAD[0:F, :] = k
    KN[...] = KPAD[...].T.astype(bf16)
    QPAD[...] = jnp.zeros_like(QPAD)
    QPAD[0:F, :] = (0.25 * q).astype(bf16)
    QS[...] = k.astype(bf16)
    VN[...] = v.T.astype(bf16)
    COTT[...] = jnp.zeros_like(COTT)
    seen = lax.broadcasted_iota(jnp.int32, (BT, BT), 0) <= lax.broadcasted_iota(
        jnp.int32, (BT, BT), 1
    )

    def causal(block):
        n = block.shape[0]
        tail = jnp.where(seen, block[n - BT :], 0.0)
        return tail if n == BT else jnp.concatenate([block[: n - BT], tail], 0)

    for tb in range(T // BT):
        n, cols = (tb + 1) * BT, slice(tb * BT, (tb + 1) * BT)
        sc = nn(KN[:n, :], QPAD[:, cols])
        w = causal(1.0 + sc * (1.0 + 0.5 * sc)).astype(bf16)
        WT[:n, cols] = w
        OT[:, cols] = nn(VB[:, :n], w)
    for cp in cot_out:
        cp.wait_recv()
    COTT[...] = COT[...].astype(f32).T
    SA[...] = jnp.zeros_like(SA)
    for k_, cp in s_out.items():

        @pl.when(z >= k_)
        def _():
            cp.wait_recv()
            SA[...] += SR[k_ - 1].astype(f32)

    gcol = TCOL[256:384, 3:4]
    o = OT[...] + nn(SA[...].T.astype(bf16), PHQ[...])
    r = lax.rsqrt(jnp.mean(o * o, 0, keepdims=True) + 1e-06)
    hat = o * r
    ct = COTT[...]
    gain_grad = jnp.sum(ct * hat, 1, keepdims=True)
    gn = ct * gcol
    DO[...] = (r * (gn - hat * jnp.mean(gn * hat, 0, keepdims=True))).astype(bf16)
    GS[...] = nt(PHQ[...], DO[...]).astype(bf16)
    g_out = {k: rc(GS, GR.at[k - 1], at(dz=NZ - k)) for k in FAR_FIRST}
    for k_, cp in g_out.items():
        pl.when(z >= k_)(cp.start)
    ATN[...] = (hat * gcol).T.astype(bf16)
    att_out = [
        rc(ATN.at[blk(mate(dy, dc), TOK)], att_o.at[:, blk(j, DV)], at(dy=dy, dc=dc))
        for dy, dc in MATES
    ]
    for cp in att_out:
        cp.start()
    att_mine = pltpu.make_async_copy(ATN.at[blk(j, TOK)], att_o.at[:, blk(j, DV)], ls.at[0])
    att_mine.start()
    DQ[...] = pair_rows_back(q, nn(SA[...].astype(bf16), DO[...]), True)
    DK[...] = jnp.zeros_like(DK)
    DVT[...] = jnp.zeros_like(DVT)
    for tb in range(T // BT):
        n, cols = (tb + 1) * BT, slice(tb * BT, (tb + 1) * BT)
        sc = nn(KN[:n, :], QPAD[:, cols])
        ds = causal(nn(VN[:n, :], DO[:, cols]) * (1.0 + sc)).astype(bf16)
        DQ[:, cols] += 0.25 * nn(QS[:, :n], ds)
        DK[:, :n] += nt(QPAD[0:F, cols], ds)
        DVT[:, :n] += nt(DO[:, cols], WT[:n, cols])
    GA[...] = jnp.zeros_like(GA)
    for k_, cp in g_out.items():

        @pl.when(z + k_ < NZ)
        def _():
            cp.wait_recv()
            GA[...] += GR[k_ - 1].astype(f32)

    dk = DK[...] + pair_rows_back(k, nn(GA[...].astype(bf16), VB[...]), False)
    CG[0:F, TOK : TOK + T] = DQ[...]
    CG[F : 2 * F, TOK : TOK + T] = dk
    CG[2 * F :, TOK : TOK + T] = DVT[...] + nn(GA[...].T.astype(bf16), PHK[...])
    CHS[...] = CG[:, TOK : 2 * TOK].astype(bf16)
    ch_out = rc(CHS, CHR, at(dz=NZ - 1))
    pl.when(z > 0)(ch_out.start)
    CG[:, 0:TOK] = jnp.zeros((CH, TOK), f32)
    CG[:, TOK + T :] = jnp.zeros((CH, TOK), f32)

    def conv_back(rows, to, size, first, count):
        g, taps = CG[to : to + size, first : first + count + TOK], TCOL[rows, :]
        n = count + TOK
        return (
            taps[:, 0:1] * g[:, :count]
            + taps[:, 1:2] * pltpu.roll(g, n - 1, 1)[:, :count]
            + taps[:, 2:3] * pltpu.roll(g, n - 2, 1)[:, :count]
        )

    for rows, to, size in parts:
        DPT[to : to + size, :] = conv_back(rows, to, size, 0, T + TOK).astype(bf16)
    x_out = {k: rc(XS.at[k - 1], XR.at[k - 1], at(dx=k)) for k in (1, 3, 2)}

    sm_out = {k: rc(SMB, SMR.at[k - 1], at(dx=k)) for k in (1, 3, 2)}
    SMF[...] = jnp.zeros_like(SMF)

    def weight_part(to_x):
        return nn(DPT[...], AS[:, blk(to_x, ROWS)])

    for k_ in (2, 1, 3):
        part = weight_part(lax.rem(f + k_, NX)).astype(bf16)
        for b in range(4):
            XS[k_ - 1, b * CH : (b + 1) * CH, :] = part[:, b * 128 : (b + 1) * 128]
        x_out[k_].start()
    part = weight_part(f)
    for b in range(4):
        XO[b * CH : (b + 1) * CH, :] = part[:, b * 128 : (b + 1) * 128]
    lane = lax.broadcasted_iota(jnp.int32, (DV, 128), 1)
    CM[...] = jnp.zeros_like(CM)
    for rows, to, size in parts:
        p, g = PT[rows, :], CG[to : to + size, TOK : TOK + T]
        sums = [
            jnp.sum(g * (pltpu.roll(p, i, 1) if i else p)[:, TOK:], 1, keepdims=True)
            for i in range(3)
        ]
        if size == DV:
            sums.append(gain_grad)
        tile = jnp.zeros((size, 128), f32)
        for i, col in enumerate(sums):
            tile = jnp.where(lane[:size] == i, col, tile)
        CM[rows, :] = tile
    for i, (lo, n) in enumerate(((0, 3), (3, 3), (6, 4))):
        SMF[lo : lo + n, :] = CM[i * 128 : (i + 1) * 128, :].T[0:n, :]
    SMB[...] = SMF[...].astype(bf16)
    for cp in sm_out.values():
        cp.start()

    @pl.when(z < NZ - 1)
    def _():
        ch_out.wait_recv()
        CG[:, TOK + T :] = CHR[...].astype(f32)

    for rows, to, size in parts:
        DPT[to : to + size, T:] = conv_back(rows, to, size, T, TOK).astype(bf16)
    DPN[...] = DPT[2 * F :, TOK:].astype(f32).T.astype(bf16)
    dp_out = []
    for dy, dc in MATES:
        m = mate(dy, dc)
        dp_out.append(rc(DPN.at[blk(m, TOK)], TDV.at[:, blk(j, DV)], at(dy=dy, dc=dc)))
        dp_out.append(
            rc(DPT.at[0 : 2 * F, blk(1 + m, TOK)], TDQK.at[blk(j, 2 * F)], at(dy=dy, dc=dc))
        )
    for cp in dp_out:
        cp.start()
    TDV[:, blk(j, DV)] = DPN[blk(j, TOK)]
    TDQK[blk(j, 2 * F)] = DPT[0 : 2 * F, blk(1 + j, TOK)]
    for k_ in (1, 3, 2):
        wv_out[k_].wait_recv()
        wv_fwd[k_].start()
    for k_ in (1, 3, 2):
        x_out[k_].wait_recv()
        XO[...] += XR[k_ - 1].astype(f32)
        sm_out[k_].wait_recv()
        SMF[...] += SMR[k_ - 1].astype(f32)
    for b in range(4):
        nat = XO[b * CH + 2 * F : (b + 1) * CH, :].T
        for i in range(2):
            ZS[2 * b + i, 0:64, :] = nat[i * 64 : (i + 1) * 64].astype(bf16)
            ZS[2 * b + i, 64:PIECE, :] = XO[b * CH + F * i : b * CH + F * (i + 1), :].astype(bf16)
            ZS[2 * b + i, PIECE:, :] = SMF[...].astype(bf16)
    z_out = {
        k: rc(ZS.at[lax.rem(z + k, NZ)], ZR.at[k - 1], at(dz=k)) for k in FAR_FIRST
    }
    for cp in z_out.values():
        cp.start()
    red = ZS[z].astype(f32)
    for k_, cp in z_out.items():
        cp.wait_recv()
        red += ZR[k_ - 1].astype(f32)
    ZB[...] = red.astype(bf16)
    zg_out = {
        k: rc(ZB.at[0:PIECE], fg_o.at[j, piece_rows(ORDER.index(k), ORDER.index(k) + 1)], at(dz=k))
        for k in ORDER[1:]
    }
    for cp in zg_out.values():
        cp.start()
    fg_o[j, 0:SMALL, :] = ZB[PIECE:, :]
    fg_o[j, SMALL : SMALL + PIECE, :] = ZB[0:PIECE, :]
    fg_sib, fg_out, fg_fwd = [], {}, []

    def to_group(ci):
        rows = piece_rows(*CHUNKS[ci])
        for dy in (2, 1, 3):
            fg_out[ci, dy] = rc(fg_o.at[j, rows], fg_o.at[j, rows], at(dy=dy))
            fg_out[ci, dy].start()
        fg_sib.append(rc(fg_o.at[j, rows], fg_o.at[j, rows], at(dc=1)))
        fg_sib[-1].start()

    to_group(0)
    for k_ in (1, 3, 2):
        wv_fwd[k_].wait_recv()
    for cp in dp_out:
        cp.wait_recv()
    tq = jnp.concatenate([TDQK[2 * F * h : 2 * F * h + F, :] for h in range(H)], 0)
    tk = jnp.concatenate([TDQK[2 * F * h + F : 2 * F * h + 2 * F, :] for h in range(H)], 0)
    TQK[...] = jnp.concatenate([tq, tk], 0).astype(f32).T.astype(bf16)

    def input_grad(i, carry):
        rows = blk(i, 256)
        gi = nt(TDV[...], WV[rows]) + nt(TQK[...], WC[rows, 0:256])
        GI[:, rows] = gi.astype(bf16)
        return carry

    lax.fori_loop(0, D // 256, input_grad, 0)
    gi_copy = pltpu.make_async_copy(GI, gi_o, ls.at[1])
    gi_copy.start()
    for ci in range(1, len(CHUNKS)):
        for k_ in ORDER[slice(*CHUNKS[ci])]:
            zg_out[k_].wait_recv()
        to_group(ci)
    fg_leave = []

    def leave(ci):
        fg_sib[ci].wait_recv()
        for cp in fg_fwd[3 * ci : 3 * ci + 3]:
            cp.wait_recv()
        rows = piece_rows(*CHUNKS[ci])
        cp = pltpu.make_async_copy(fg_o.at[:, rows], fg_out_o.at[:, rows], ls.at[12 + ci])
        cp.start()
        fg_leave.append(cp)

    for ci, chunk in enumerate(CHUNKS):
        rows = piece_rows(*chunk)
        for dy in (1, 3, 2):
            fg_out[ci, dy].wait_recv()
            from_j = lax.rem(y + NY - dy, NY) * 2 + c
            cp = rc(fg_o.at[from_j, rows], fg_o.at[from_j, rows], at(dc=1))
            cp.start()
            fg_fwd.append(cp)
        if ci:
            leave(ci - 1)
    leave(len(CHUNKS) - 1)
    for cp in att_out:
        cp.wait_recv()
    att_mine.wait()
    for cp in fg_leave:
        cp.wait()
    gi_copy.wait()
    pl.when(jnp.logical_and(last, z < NZ - 1))(halo_z.wait_send)

    @pl.when(jnp.logical_and(last, z > 0))
    def _():
        for cp in halo_g:
            cp.wait_send()

    for k_, cp in s_out.items():
        pl.when(z + k_ < NZ)(cp.wait_send)
    for k_, cp in g_out.items():
        pl.when(z >= k_)(cp.wait_send)
    pl.when(z > 0)(ch_out.wait_send)
    done = [a_sib, relay_up, relay_down] + fg_sib + cot_out + w_fwd + att_out + dp_out + fg_fwd
    for group in (up, down, across, sm_out, wqk_out, wh_out, wv_out, wv_fwd, x_out, z_out, zg_out, fg_out):
        done += list(group.values())
    for cp in done:
        cp.wait_send()


def unpack(
    att, gi, fg, att_o, gi_o, gq_o, gk_o, gv_o, tq_o, tk_o, tv_o, gg_o,
    ATT, GI, FG, GV, QTF, GQ, GK, TQ, TK, TV, GG, ins, outs,
):
    z = lax.div(lax.axis_index("seq"), GROUP)
    heads = [pltpu.make_async_copy(fg.at[h], FG.at[h], ins.at[h]) for h in range(H)]
    passed = [
        pltpu.make_async_copy(att, ATT, ins.at[H]), pltpu.make_async_copy(gi, GI, ins.at[H + 1])
    ]
    for cp in heads + passed:
        cp.start()
    leaving = []

    def leave(src, dst):
        cp = pltpu.make_async_copy(src, dst, outs.at[len(leaving)])
        cp.start()
        leaving.append(cp)

    qk_sum = jnp.zeros((8, 128), f32)
    for h in range(H):
        heads[h].wait()
        lanes = slice(h * DV, (h + 1) * DV)
        for i, k in enumerate(ORDER):
            piece = lax.rem(z + NZ - k, NZ)
            band, kind = lax.div(piece, 2), lax.rem(piece, 2)
            rows = pl.ds(pl.multiple_of(piece * 64, 64), 64)
            cols = pl.ds(pl.multiple_of(band * 128, 128), 128)
            base = SMALL + i * PIECE
            GV[rows, lanes] = FG[h, base : base + 64, :].astype(f32)
            row = pl.ds(pl.multiple_of(kind * 128 + h * F, F), F)
            QTF[row, cols] = FG[h, base + 64 : base + PIECE, :].astype(f32)
        leave(GV.at[:, lanes], gv_o.at[:, lanes])
        sm = FG[h, 0:SMALL, :].astype(f32)
        qk_sum += sm[0:8]
        TV[:, lanes] = sm[6:9]
        GG[:, lanes] = sm[9:10]
    TQ[...] = qk_sum[0:3]
    TK[...] = qk_sum[3:6]
    GQ[...] = QTF[0:128, :].T
    GK[...] = QTF[128:256, :].T
    for src, dst in ((TQ, tq_o), (TK, tk_o), (TV, tv_o), (GG, gg_o), (GQ, gq_o), (GK, gk_o)):
        leave(src, dst)
    for cp, src, dst in zip(passed, (ATT, GI), (att_o, gi_o)):
        cp.wait()
        leave(src, dst)
    for cp in leaving:
        cp.wait()


N_SEMS = 136


def on_device(a, wq, wk, wv, cq, ck, cv, gain, cot):
    sd = jax.ShapeDtypeStruct
    V = pltpu.VMEM
    vmem, anywhere = pl.BlockSpec(memory_space=V), pl.BlockSpec(memory_space=pl.ANY)
    scratch = [
        V((H, FULL, 128), bf16),
        V((3, H * F), f32), V((3, H * F), f32), V((3, H * DV), f32), V((1, H * DV), f32),
        V((TOK, H * DV), bf16),
        V((T + TOK, D), bf16), V((16, 256), bf16), V((16, 256), f32), V((16, 256), bf16),
        V((16, D), f32),
        V((D, 384), bf16), V((D, H * DV), bf16), V((T, DV), bf16),
        V((128, 384), f32), V((384, 128), f32), V((384, T + TOK), f32),
        V((CH, T), f32), V((128, T), f32), V((128, T), bf16), V((T, 128), bf16), V((T, DV), bf16),
        V((DV, T), bf16), V((F, T), bf16), V((PHI, T), bf16), V((PHI, T), bf16),
        V((PHI, DV), bf16), V((NZ - 1, PHI, DV), bf16), V((PHI, DV), f32),
        V((PHI, DV), bf16), V((NZ - 1, PHI, DV), bf16), V((PHI, DV), f32),
        V((T, T), bf16), V((DV, T), f32), V((DV, T), f32), V((DV, T), bf16),
        V((F, T), f32), V((F, T), f32), V((DV, T), f32), V((T, DV), bf16),
        V((CH, T + 2 * TOK), f32), V((CH, TOK), bf16), V((CH, TOK), bf16),
        V((CH, T + TOK), bf16), V((T, DV), bf16), V((TOK, H * DV), bf16),
        V((H * 2 * F, TOK), bf16), V((TOK, H * 2 * F), bf16), V((TOK, D), bf16),
        V((384, 128), f32), V((SMALL, 128), f32), V((SMALL, 128), bf16),
        V((NX - 1, SMALL, 128), bf16),
        V((NX - 1, 4 * CH, 128), bf16), V((NX - 1, 4 * CH, 128), bf16),
        V((4 * CH, 128), f32),
        V((NZ, PIECE + SMALL, 128), bf16), V((NZ - 1, PIECE + SMALL, 128), bf16),
        V((PIECE + SMALL, 128), bf16),
        pltpu.SemaphoreType.DMA((N_SEMS,)), pltpu.SemaphoreType.DMA((N_SEMS,)),
        pltpu.SemaphoreType.DMA((16,)),
    ]
    att, gi, fg = pl.pallas_call(
        kernel,
        out_shape=[
            sd((TOK, H * DV), bf16), sd((TOK, D), bf16), sd((H, FULL, 128), bf16),
        ],
        in_specs=[anywhere] * 9,
        out_specs=[anywhere] * 3,
        scratch_shapes=scratch,
        compiler_params=pltpu.CompilerParams(
            collective_id=0, has_side_effects=True, vmem_limit_bytes=56 * 2**20
        ),
        name="based_layer",
    )(a.reshape(TOK, D), wq, wk, wv, cq, ck, cv, gain.reshape(1, -1), cot.reshape(TOK, H * DV))
    att, gi, gq, gk, gv, tq, tk, tv, gg = pl.pallas_call(
        unpack,
        out_shape=[
            sd((TOK, H * DV), bf16), sd((TOK, D), bf16),
            sd((ROWS, H * F), f32), sd((ROWS, H * F), f32), sd((ROWS, H * DV), f32),
            sd((3, H * F), f32), sd((3, H * F), f32), sd((3, H * DV), f32), sd((1, H * DV), f32),
        ],
        in_specs=[anywhere] * 3,
        out_specs=[anywhere] * 9,
        scratch_shapes=[
            V((TOK, H * DV), bf16), V((TOK, D), bf16), V((H, FULL, 128), bf16),
            V((ROWS, H * DV), f32), V((256, ROWS), f32), V((ROWS, H * F), f32),
            V((ROWS, H * F), f32), V((3, H * F), f32), V((3, H * F), f32), V((3, H * DV), f32),
            V((1, H * DV), f32),
            pltpu.SemaphoreType.DMA((H + 2,)), pltpu.SemaphoreType.DMA((H + 8,)),
        ],
        name="unpack",
    )(att, gi, fg)
    return att[None], gi[None], gq, gk, gv, tq, tk, tv, gg.reshape(-1)


def solution(mesh):
    rows = P("fsdp", "seq", None)
    return jax.shard_map(
        on_device,
        mesh=mesh,
        in_specs=(rows, P("fsdp", None), P("fsdp", None), P("fsdp", None), P(), P(), P(), P(), rows),
        out_specs=(
            rows, rows, P("fsdp", None), P("fsdp", None), P("fsdp", None), P(), P(), P(), P(),
        ),
        check_vma=False,
    )
```

```python
import itertools

import jax
import jax.numpy as jnp
from jax import lax
from jax.experimental import pallas as pl
from jax.experimental.pallas import tpu as pltpu
from jax.sharding import PartitionSpec as P

MESH = pl.DeviceIdType.MESH
H, F, DV = 8, 16, 128
NX, NY, NZ, GROUP = 4, 4, 8, 8
TOK, D = 128, 2048
T = GROUP * TOK
ROWS = D // NX
CH = 2 * F + DV
KV = F + DV
BANDS = F // 2
PHI = F * (BANDS + 2)
SMALL = 16
PIECE = 80
FULL = NZ * PIECE + SMALL
BT = 256
HALF = TOK // 2
ORDER = (0, 1, 7, 2, 6, 3, 5, 4)
CHUNKS = ((0, 1), (1, 3), (3, 5), (5, 8))
FAR_FIRST = (4, 3, 5, 2, 6, 1, 7)
f32, bf16 = jnp.float32, jnp.bfloat16
MATES = [(0, 1), (1, 0), (3, 0), (1, 1), (3, 1), (2, 0), (2, 1)]


def piece_rows(lo, hi):
    return slice(SMALL + lo * PIECE if lo else 0, SMALL + hi * PIECE)


def nn(a, b):
    return lax.dot_general(a, b, (((1,), (0,)), ((), ())), preferred_element_type=f32)


def nt(a, b):
    return lax.dot_general(a, b, (((1,), (1,)), ((), ())), preferred_element_type=f32)


def pair_rows(u, weighted):
    scale = 1.0 / 32.0 if weighted else 1.0
    bands = [scale * u * u]
    for d in range(1, BANDS):
        bands.append((2.0 * scale if weighted else 1.0) * u * pltpu.roll(u, d, 0))
    bands.append((2.0 * scale if weighted else 1.0) * u[:BANDS] * u[BANDS:])
    one = lax.broadcasted_iota(jnp.int32, (F - BANDS, u.shape[1]), 0) == 0
    return jnp.concatenate(bands + [jnp.where(one, 1.0, 0.0), 0.25 * u if weighted else u], 0)


def pair_rows_back(u, grad, weighted):
    scale = 1.0 / 32.0 if weighted else 1.0
    total = grad[F * (BANDS + 1) :] * (0.25 if weighted else 1.0) + 2.0 * scale * grad[:F] * u
    twice = 2.0 * scale if weighted else 1.0
    for d in range(1, BANDS):
        e = twice * grad[F * d : F * (d + 1)]
        total += e * pltpu.roll(u, d, 0) + pltpu.roll(e * u, F - d, 0)
    e = twice * grad[F * BANDS : F * BANDS + BANDS]
    return total + jnp.concatenate([e * u[BANDS:], e * u[:BANDS]], 0)


def kernel(
    a_in, wq_in, wk_in, wv_in, cq_in, ck_in, cv_in, gain_in, cot_in,
    att_o, gi_o, fg_out_o,
    fg_o, cq, ck, cv, gain, cot, AS, HS, HF, HR, HA, WC, WV, COT, TPAD, TCOL, PT, XT, KPAD, QPAD, KN, VN, VB, QS, PHQ, PHK,
    SS, SR, SA, GS, GR, GA, WT, OT, COTT, DO, DQ, DK, DVT, ATN, CG, CHS, CHR, DPT, DPN, TDV, TDQK,
    TQK, GI, CM, SMF, SMB, SMR, XQ, XQR, XS, XR, XO, ZS, ZR, ZB, ss, rs, ls,
):
    s = lax.axis_index("seq")
    f = lax.axis_index("fsdp")
    z, j = lax.div(s, 8), lax.rem(s, 8)
    y, c = lax.div(j, 2), lax.rem(j, 2)
    ids = itertools.count()

    def at(dx=0, dy=0, dz=0, dc=0):
        zz, yy, cc = lax.rem(z + dz + NZ, NZ), lax.rem(y + dy, NY), lax.rem(c + dc, 2)
        return {"seq": (zz * NY + yy) * 2 + cc, "fsdp": lax.rem(f + dx, NX)}

    def mate(dy, dc):
        return lax.rem(y + dy, NY) * 2 + lax.rem(c + dc, 2)

    def rc(src, dst, to):
        i = next(ids)
        return pltpu.make_async_remote_copy(
            src_ref=src, dst_ref=dst, send_sem=ss.at[i], recv_sem=rs.at[i],
            device_id=to, device_id_type=MESH,
        )

    def blk(i, size):
        return pl.ds(pl.multiple_of(i * size, size), size)

    bar = pltpu.get_barrier_semaphore()
    peers = [at(dx=k) for k in range(1, NX)] + [at(dy=dy, dc=dc) for dy, dc in MATES]
    peers += [at(dz=k) for k in range(1, NZ)]
    for p in peers:
        pl.semaphore_signal(bar, inc=1, device_id=p, device_id_type=MESH)
    own_rows, own_w = blk(1 + j, TOK), blk(f, ROWS)
    fetch = [
        pltpu.make_async_copy(src, dst, ls.at[2 + i])
        for i, (src, dst) in enumerate((
            (a_in, AS.at[own_rows]),
            (wq_in, WC.at[own_w, 0:128]),
            (wk_in, WC.at[own_w, 128:256]),
            (wv_in.at[:, blk(j, DV)], WC.at[own_w, 256:384]),
            (wv_in, WV.at[own_w]),
            (cot_in, cot),
            (cq_in, cq), (ck_in, ck), (cv_in, cv), (gain_in, gain),
        ))
    ]
    for cp in fetch:
        cp.start()

    @pl.when(z == 0)
    def _():
        HR[...] = jnp.zeros_like(HR)

    TPAD[...] = jnp.zeros_like(TPAD)
    for cp in fetch:
        cp.wait()
    x = AS[own_rows, :][TOK - 16 :, :].astype(f32)
    for i in range(8):
        HF[2 * i : 2 * i + 2, :] = x[14:16, i * 256 : (i + 1) * 256]
    HS[...] = HF[...].astype(bf16)
    COT[blk(j, TOK)] = cot[:, blk(j, DV)]

    TPAD[0:3, 0:128] = cq[...]
    TPAD[0:3, 128:256] = ck[...]
    TPAD[0:3, 256:384] = cv[:, blk(j, DV)]
    TPAD[3:4, 256:384] = gain[:, blk(j, DV)]
    for i in range(3):
        TCOL[i * 128 : (i + 1) * 128, :] = TPAD[:, i * 128 : (i + 1) * 128].T

    pl.semaphore_wait(bar, len(peers))
    halo_z = rc(HS, HR, at(dz=1))
    halo_g = [rc(HR, HR, at(dy=dy, dc=dc)) for dy, dc in MATES]
    last = j == GROUP - 1

    @pl.when(jnp.logical_and(last, z < NZ - 1))
    def _():
        halo_z.start()

    def tok_rows(chip_y, part=None):
        base = (1 + lax.rem(chip_y + NY, NY) * 2 + c) * TOK
        if part is None:
            return pl.ds(pl.multiple_of(base, TOK), TOK)
        return pl.ds(pl.multiple_of(base + part * HALF, HALF), HALF)

    mine = tok_rows(y)
    a_sib = rc(AS.at[mine], AS.at[mine], at(dc=1))
    up, down = {}, {}
    for p_ in (0, 1):
        src = AS.at[tok_rows(y, p_)]
        up[p_] = rc(src, AS.at[tok_rows(y, p_)], at(dy=1))
        down[p_] = rc(src, AS.at[tok_rows(y, p_)], at(dy=3))
    relay_up = rc(AS.at[tok_rows(y - 1, 0)], AS.at[tok_rows(y - 1, 0)], at(dy=1))
    relay_down = rc(AS.at[tok_rows(y + 1, 1)], AS.at[tok_rows(y + 1, 1)], at(dy=3))
    across = {}
    for name, rows in (
        ("up", tok_rows(y - 1)), ("down", tok_rows(y + 1)),
        ("far0", tok_rows(y + 2, 0)), ("far1", tok_rows(y + 2, 1)),
    ):
        across[name] = rc(AS.at[rows], AS.at[rows], at(dc=1))
    up[0].start()
    down[1].start()
    up[1].start()
    down[0].start()
    a_sib.start()
    mine_half = blk(2 * f + c, ROWS // 2)
    wqk_out, wh_out, wv_out = {}, {}, {}
    for k in (1, 3, 2):
        wqk_out[k] = rc(WC.at[mine_half, 0:256], WC.at[mine_half, 0:256], at(dx=k))
        wh_out[k] = rc(WC.at[own_w, 256:384], WC.at[own_w, 256:384], at(dx=k))
        wv_out[k] = rc(WV.at[mine_half], WV.at[mine_half], at(dx=k))
    for k in (1, 3, 2):
        wqk_out[k].start()
    for k in (1, 3, 2):
        wh_out[k].start()
    cot_out = [
        rc(cot.at[:, blk(mate(dy, dc), DV)], COT.at[blk(j, TOK)], at(dy=dy, dc=dc))
        for dy, dc in MATES
    ]

    @pl.when(jnp.logical_and(last, z > 0))
    def _():
        halo_z.wait_recv()
        for cp in halo_g:
            cp.start()

    up[0].wait_recv()
    relay_up.start()
    down[1].wait_recv()
    relay_down.start()
    w_fwd, wv_fwd = [], {}
    for k in (1, 3, 2):
        from_x = lax.rem(f + NX - k, NX)
        rows = blk(2 * from_x + c, ROWS // 2)
        wqk_out[k].wait_recv()
        cp = rc(WC.at[rows, 0:256], WC.at[rows, 0:256], at(dc=1))
        cp.start()
        w_fwd.append(cp)
        wv_fwd[k] = rc(WV.at[rows], WV.at[rows], at(dc=1))
    up[1].wait_recv()
    across["up"].start()
    down[0].wait_recv()
    across["down"].start()
    for k in (1, 3, 2):
        wh_out[k].wait_recv()
    for k in (1, 3, 2):
        wv_out[k].start()
    a_sib.wait_recv()
    for cp in w_fwd:
        cp.wait_recv()

    def project(chip_y):
        chip = lax.rem(chip_y + NY, NY)
        p = nn(AS[pl.ds(pl.multiple_of(TOK + chip * 2 * TOK, TOK), 2 * TOK)], WC[...])
        cols = pl.ds(pl.multiple_of(TOK + chip * 2 * TOK, TOK), 2 * TOK)
        PT[:, cols] = p.astype(bf16).astype(f32).T

    project(y)
    across["up"].wait_recv()
    project(y - 1)
    across["down"].wait_recv()
    project(y + 1)
    relay_up.wait_recv()
    across["far0"].start()
    relay_down.wait_recv()
    across["far1"].start()
    for cp in cot_out:
        cp.start()

    @pl.when(jnp.logical_and(jnp.logical_not(last), z > 0))
    def _():
        for (dy, dc), cp in zip(MATES, halo_g):
            from_j = lax.rem(y + NY - dy, NY) * 2 + lax.rem(c + dc, 2)

            @pl.when(from_j == GROUP - 1)
            def _():
                cp.wait_recv()

    HF[...] = HR[...].astype(f32)
    HA[...] = jnp.zeros_like(HA)
    for i in range(8):
        HA[14:16, i * 256 : (i + 1) * 256] = HF[2 * i : 2 * i + 2, :]
    AS[0 : TOK - 16] = jnp.zeros((TOK - 16, D), bf16)
    AS[TOK - 16 : TOK] = HA[...].astype(bf16)
    ph = nn(AS[TOK - 16 : TOK], WC[...]).astype(bf16).astype(f32)
    PT[:, 0:TOK] = jnp.concatenate([jnp.zeros((TOK - 16, 384), f32), ph], 0).T
    across["far0"].wait_recv()
    across["far1"].wait_recv()
    project(y + 2)

    q_rows, k_rows = blk(j, F), pl.ds(pl.multiple_of(128 + j * F, F), F)
    parts = ((q_rows, 0, F), (k_rows, F, F), (pl.ds(256, DV), 2 * F, DV))
    for rows, to, size in parts:
        p, taps = PT[rows, :], TCOL[rows, :]
        XT[to : to + size, :] = (
            taps[:, 0:1] * p[:, TOK:]
            + taps[:, 1:2] * pltpu.roll(p, 1, 1)[:, TOK:]
            + taps[:, 2:3] * pltpu.roll(p, 2, 1)[:, TOK:]
        )
    q, k, v = XT[0:F, :], XT[F : 2 * F, :], XT[2 * F :, :]
    VB[...] = v.astype(bf16)
    PHK[...] = pair_rows(k, False).astype(bf16)
    SS[...] = nt(PHK[...], VB[...]).astype(bf16)
    s_out = {k: rc(SS, SR.at[k - 1], at(dz=k)) for k in FAR_FIRST}
    for k_, cp in s_out.items():
        pl.when(z + k_ < NZ)(cp.start)
    PHQ[...] = pair_rows(q, True).astype(bf16)
    KPAD[...] = jnp.zeros_like(KPAD)
    KPAD[0:F, :] = k
    KN[...] = KPAD[...].T.astype(bf16)
    QPAD[...] = jnp.zeros_like(QPAD)
    QPAD[0:F, :] = (0.25 * q).astype(bf16)
    QS[...] = k.astype(bf16)
    VN[...] = v.T.astype(bf16)
    COTT[...] = jnp.zeros_like(COTT)
    seen = lax.broadcasted_iota(jnp.int32, (BT, BT), 0) <= lax.broadcasted_iota(
        jnp.int32, (BT, BT), 1
    )

    def causal(block):
        n = block.shape[0]
        tail = jnp.where(seen, block[n - BT :], 0.0)
        return tail if n == BT else jnp.concatenate([block[: n - BT], tail], 0)

    for tb in range(T // BT):
        n, cols = (tb + 1) * BT, slice(tb * BT, (tb + 1) * BT)
        sc = nn(KN[:n, :], QPAD[:, cols])
        w = causal(1.0 + sc * (1.0 + 0.5 * sc)).astype(bf16)
        WT[:n, cols] = w
        OT[:, cols] = nn(VB[:, :n], w)
    for cp in cot_out:
        cp.wait_recv()
    COTT[...] = COT[...].astype(f32).T
    SA[...] = jnp.zeros_like(SA)
    for k_, cp in s_out.items():

        @pl.when(z >= k_)
        def _():
            cp.wait_recv()
            SA[...] += SR[k_ - 1].astype(f32)

    gcol = TCOL[256:384, 3:4]
    o = OT[...] + nn(SA[...].T.astype(bf16), PHQ[...])
    r = lax.rsqrt(jnp.mean(o * o, 0, keepdims=True) + 1e-06)
    hat = o * r
    ct = COTT[...]
    gain_grad = jnp.sum(ct * hat, 1, keepdims=True)
    gn = ct * gcol
    DO[...] = (r * (gn - hat * jnp.mean(gn * hat, 0, keepdims=True))).astype(bf16)
    GS[...] = nt(PHQ[...], DO[...]).astype(bf16)
    g_out = {k: rc(GS, GR.at[k - 1], at(dz=NZ - k)) for k in FAR_FIRST}
    for k_, cp in g_out.items():
        pl.when(z >= k_)(cp.start)
    ATN[...] = (hat * gcol).T.astype(bf16)
    att_out = [
        rc(ATN.at[blk(mate(dy, dc), TOK)], att_o.at[:, blk(j, DV)], at(dy=dy, dc=dc))
        for dy, dc in MATES
    ]
    for cp in att_out:
        cp.start()
    att_mine = pltpu.make_async_copy(ATN.at[blk(j, TOK)], att_o.at[:, blk(j, DV)], ls.at[0])
    att_mine.start()
    DQ[...] = pair_rows_back(q, nn(SA[...].astype(bf16), DO[...]), True)
    DK[...] = jnp.zeros_like(DK)
    DVT[...] = jnp.zeros_like(DVT)
    for tb in range(T // BT):
        n, cols = (tb + 1) * BT, slice(tb * BT, (tb + 1) * BT)
        sc = nn(KN[:n, :], QPAD[:, cols])
        ds = causal(nn(VN[:n, :], DO[:, cols]) * (1.0 + sc)).astype(bf16)
        DQ[:, cols] += 0.25 * nn(QS[:, :n], ds)
        DK[:, :n] += nt(QPAD[0:F, cols], ds)
        DVT[:, :n] += nt(DO[:, cols], WT[:n, cols])
    CG[:, 0:TOK] = jnp.zeros((CH, TOK), f32)
    CG[:, TOK + T :] = jnp.zeros((CH, TOK), f32)

    def conv_back(rows, to, size, first, count):
        g, taps = CG[to : to + size, first : first + count + TOK], TCOL[rows, :]
        n = count + TOK
        return (
            taps[:, 0:1] * g[:, :count]
            + taps[:, 1:2] * pltpu.roll(g, n - 1, 1)[:, :count]
            + taps[:, 2:3] * pltpu.roll(g, n - 2, 1)[:, :count]
        )

    CG[0:F, TOK : TOK + T] = DQ[...]
    DPT[0:F, :] = conv_back(q_rows, 0, F, 0, T + TOK).astype(bf16)
    xq_out = {k: rc(XQ.at[k - 1], XQR.at[k - 1], at(dx=k)) for k in (1, 3, 2)}
    for k_ in (2, 1, 3, 0):
        part = nn(DPT[0:F, :], AS[:, blk(lax.rem(f + k_, NX), ROWS)])
        for b in range(4):
            if k_:
                XQ[k_ - 1, b * F : (b + 1) * F, :] = part[:, b * 128 : (b + 1) * 128].astype(bf16)
            else:
                XO[b * CH : b * CH + F, :] = part[:, b * 128 : (b + 1) * 128]
        if k_:
            xq_out[k_].start()
    GA[...] = jnp.zeros_like(GA)
    for k_, cp in g_out.items():

        @pl.when(z + k_ < NZ)
        def _():
            cp.wait_recv()
            GA[...] += GR[k_ - 1].astype(f32)

    dk = DK[...] + pair_rows_back(k, nn(GA[...].astype(bf16), VB[...]), False)
    CG[F : 2 * F, TOK : TOK + T] = dk
    CG[2 * F :, TOK : TOK + T] = DVT[...] + nn(GA[...].T.astype(bf16), PHK[...])
    CHS[...] = CG[:, TOK : 2 * TOK].astype(bf16)
    ch_out = rc(CHS, CHR, at(dz=NZ - 1))
    pl.when(z > 0)(ch_out.start)
    for rows, to, size in parts:
        if to:
            DPT[to : to + size, :] = conv_back(rows, to, size, 0, T + TOK).astype(bf16)
    x_out = {k: rc(XS.at[k - 1], XR.at[k - 1], at(dx=k)) for k in (1, 3, 2)}

    sm_out = {k: rc(SMB, SMR.at[k - 1], at(dx=k)) for k in (1, 3, 2)}
    SMF[...] = jnp.zeros_like(SMF)

    def weight_part(to_x):
        return nn(DPT[F:, :], AS[:, blk(to_x, ROWS)])

    for k_ in (2, 1, 3):
        part = weight_part(lax.rem(f + k_, NX)).astype(bf16)
        for b in range(4):
            XS[k_ - 1, b * KV : (b + 1) * KV, :] = part[:, b * 128 : (b + 1) * 128]
        x_out[k_].start()
    part = weight_part(f)
    for b in range(4):
        XO[b * CH + F : (b + 1) * CH, :] = part[:, b * 128 : (b + 1) * 128]
    lane = lax.broadcasted_iota(jnp.int32, (DV, 128), 1)
    CM[...] = jnp.zeros_like(CM)
    for rows, to, size in parts:
        p, g = PT[rows, :], CG[to : to + size, TOK : TOK + T]
        sums = [
            jnp.sum(g * (pltpu.roll(p, i, 1) if i else p)[:, TOK:], 1, keepdims=True)
            for i in range(3)
        ]
        if size == DV:
            sums.append(gain_grad)
        tile = jnp.zeros((size, 128), f32)
        for i, col in enumerate(sums):
            tile = jnp.where(lane[:size] == i, col, tile)
        CM[rows, :] = tile
    for i, (lo, n) in enumerate(((0, 3), (3, 3), (6, 4))):
        SMF[lo : lo + n, :] = CM[i * 128 : (i + 1) * 128, :].T[0:n, :]
    SMB[...] = SMF[...].astype(bf16)
    for cp in sm_out.values():
        cp.start()

    @pl.when(z < NZ - 1)
    def _():
        ch_out.wait_recv()
        CG[:, TOK + T :] = CHR[...].astype(f32)

    for rows, to, size in parts:
        DPT[to : to + size, T:] = conv_back(rows, to, size, T, TOK).astype(bf16)
    DPN[...] = DPT[2 * F :, TOK:].astype(f32).T.astype(bf16)
    dp_out = []
    for dy, dc in MATES:
        m = mate(dy, dc)
        dp_out.append(rc(DPN.at[blk(m, TOK)], TDV.at[:, blk(j, DV)], at(dy=dy, dc=dc)))
        dp_out.append(
            rc(DPT.at[0 : 2 * F, blk(1 + m, TOK)], TDQK.at[blk(j, 2 * F)], at(dy=dy, dc=dc))
        )
    for cp in dp_out:
        cp.start()
    TDV[:, blk(j, DV)] = DPN[blk(j, TOK)]
    TDQK[blk(j, 2 * F)] = DPT[0 : 2 * F, blk(1 + j, TOK)]
    for k_ in (1, 3, 2):
        wv_out[k_].wait_recv()
        wv_fwd[k_].start()
    for k_ in (1, 3, 2):
        x_out[k_].wait_recv()
        xq_out[k_].wait_recv()
        for b in range(4):
            XO[b * CH : b * CH + F, :] += XQR[k_ - 1, b * F : (b + 1) * F, :].astype(f32)
            XO[b * CH + F : (b + 1) * CH, :] += XR[k_ - 1, b * KV : (b + 1) * KV, :].astype(f32)
        sm_out[k_].wait_recv()
        SMF[...] += SMR[k_ - 1].astype(f32)
    for b in range(4):
        nat = XO[b * CH + 2 * F : (b + 1) * CH, :].T
        for i in range(2):
            ZS[2 * b + i, 0:64, :] = nat[i * 64 : (i + 1) * 64].astype(bf16)
            ZS[2 * b + i, 64:PIECE, :] = XO[b * CH + F * i : b * CH + F * (i + 1), :].astype(bf16)
            ZS[2 * b + i, PIECE:, :] = SMF[...].astype(bf16)
    z_out = {
        k: rc(ZS.at[lax.rem(z + k, NZ)], ZR.at[k - 1], at(dz=k)) for k in FAR_FIRST
    }
    for cp in z_out.values():
        cp.start()
    red = ZS[z].astype(f32)
    for k_, cp in z_out.items():
        cp.wait_recv()
        red += ZR[k_ - 1].astype(f32)
    ZB[...] = red.astype(bf16)
    zg_out = {
        k: rc(ZB.at[0:PIECE], fg_o.at[j, piece_rows(ORDER.index(k), ORDER.index(k) + 1)], at(dz=k))
        for k in ORDER[1:]
    }
    for cp in zg_out.values():
        cp.start()
    fg_o[j, 0:SMALL, :] = ZB[PIECE:, :]
    fg_o[j, SMALL : SMALL + PIECE, :] = ZB[0:PIECE, :]
    fg_sib, fg_out, fg_fwd = [], {}, []

    def to_group(ci):
        rows = piece_rows(*CHUNKS[ci])
        for dy in (2, 1, 3):
            fg_out[ci, dy] = rc(fg_o.at[j, rows], fg_o.at[j, rows], at(dy=dy))
            fg_out[ci, dy].start()
        fg_sib.append(rc(fg_o.at[j, rows], fg_o.at[j, rows], at(dc=1)))
        fg_sib[-1].start()

    to_group(0)
    for k_ in (1, 3, 2):
        wv_fwd[k_].wait_recv()
    for cp in dp_out:
        cp.wait_recv()
    tq = jnp.concatenate([TDQK[2 * F * h : 2 * F * h + F, :] for h in range(H)], 0)
    tk = jnp.concatenate([TDQK[2 * F * h + F : 2 * F * h + 2 * F, :] for h in range(H)], 0)
    TQK[...] = jnp.concatenate([tq, tk], 0).astype(f32).T.astype(bf16)

    def input_grad(i, carry):
        rows = blk(i, 256)
        gi = nt(TDV[...], WV[rows]) + nt(TQK[...], WC[rows, 0:256])
        GI[:, rows] = gi.astype(bf16)
        return carry

    lax.fori_loop(0, D // 256, input_grad, 0)
    gi_copy = pltpu.make_async_copy(GI, gi_o, ls.at[1])
    gi_copy.start()
    for ci in range(1, len(CHUNKS)):
        for k_ in ORDER[slice(*CHUNKS[ci])]:
            zg_out[k_].wait_recv()
        to_group(ci)
    fg_leave = []

    def leave(ci):
        fg_sib[ci].wait_recv()
        for cp in fg_fwd[3 * ci : 3 * ci + 3]:
            cp.wait_recv()
        rows = piece_rows(*CHUNKS[ci])
        cp = pltpu.make_async_copy(fg_o.at[:, rows], fg_out_o.at[:, rows], ls.at[12 + ci])
        cp.start()
        fg_leave.append(cp)

    for ci, chunk in enumerate(CHUNKS):
        rows = piece_rows(*chunk)
        for dy in (1, 3, 2):
            fg_out[ci, dy].wait_recv()
            from_j = lax.rem(y + NY - dy, NY) * 2 + c
            cp = rc(fg_o.at[from_j, rows], fg_o.at[from_j, rows], at(dc=1))
            cp.start()
            fg_fwd.append(cp)
        if ci:
            leave(ci - 1)
    leave(len(CHUNKS) - 1)
    for cp in att_out:
        cp.wait_recv()
    att_mine.wait()
    for cp in fg_leave:
        cp.wait()
    gi_copy.wait()
    pl.when(jnp.logical_and(last, z < NZ - 1))(halo_z.wait_send)

    @pl.when(jnp.logical_and(last, z > 0))
    def _():
        for cp in halo_g:
            cp.wait_send()

    for k_, cp in s_out.items():
        pl.when(z + k_ < NZ)(cp.wait_send)
    for k_, cp in g_out.items():
        pl.when(z >= k_)(cp.wait_send)
    pl.when(z > 0)(ch_out.wait_send)
    done = [a_sib, relay_up, relay_down] + fg_sib + cot_out + w_fwd + att_out + dp_out + fg_fwd
    for group in (up, down, across, sm_out, xq_out, wqk_out, wh_out, wv_out, wv_fwd, x_out, z_out, zg_out, fg_out):
        done += list(group.values())
    for cp in done:
        cp.wait_send()


def unpack(
    att, gi, fg, att_o, gi_o, gq_o, gk_o, gv_o, tq_o, tk_o, tv_o, gg_o,
    ATT, GI, FG, GV, QTF, GQ, GK, TQ, TK, TV, GG, ins, outs,
):
    z = lax.div(lax.axis_index("seq"), GROUP)
    heads = [pltpu.make_async_copy(fg.at[h], FG.at[h], ins.at[h]) for h in range(H)]
    passed = [
        pltpu.make_async_copy(att, ATT, ins.at[H]), pltpu.make_async_copy(gi, GI, ins.at[H + 1])
    ]
    for cp in heads + passed:
        cp.start()
    leaving = []

    def leave(src, dst):
        cp = pltpu.make_async_copy(src, dst, outs.at[len(leaving)])
        cp.start()
        leaving.append(cp)

    qk_sum = jnp.zeros((8, 128), f32)
    for h in range(H):
        heads[h].wait()
        lanes = slice(h * DV, (h + 1) * DV)
        for i, k in enumerate(ORDER):
            piece = lax.rem(z + NZ - k, NZ)
            band, kind = lax.div(piece, 2), lax.rem(piece, 2)
            rows = pl.ds(pl.multiple_of(piece * 64, 64), 64)
            cols = pl.ds(pl.multiple_of(band * 128, 128), 128)
            base = SMALL + i * PIECE
            GV[rows, lanes] = FG[h, base : base + 64, :].astype(f32)
            row = pl.ds(pl.multiple_of(kind * 128 + h * F, F), F)
            QTF[row, cols] = FG[h, base + 64 : base + PIECE, :].astype(f32)
        leave(GV.at[:, lanes], gv_o.at[:, lanes])
        sm = FG[h, 0:SMALL, :].astype(f32)
        qk_sum += sm[0:8]
        TV[:, lanes] = sm[6:9]
        GG[:, lanes] = sm[9:10]
    TQ[...] = qk_sum[0:3]
    TK[...] = qk_sum[3:6]
    GQ[...] = QTF[0:128, :].T
    GK[...] = QTF[128:256, :].T
    for src, dst in ((TQ, tq_o), (TK, tk_o), (TV, tv_o), (GG, gg_o), (GQ, gq_o), (GK, gk_o)):
        leave(src, dst)
    for cp, src, dst in zip(passed, (ATT, GI), (att_o, gi_o)):
        cp.wait()
        leave(src, dst)
    for cp in leaving:
        cp.wait()


N_SEMS = 140


def on_device(a, wq, wk, wv, cq, ck, cv, gain, cot):
    sd = jax.ShapeDtypeStruct
    V = pltpu.VMEM
    vmem, anywhere = pl.BlockSpec(memory_space=V), pl.BlockSpec(memory_space=pl.ANY)
    scratch = [
        V((H, FULL, 128), bf16),
        V((3, H * F), f32), V((3, H * F), f32), V((3, H * DV), f32), V((1, H * DV), f32),
        V((TOK, H * DV), bf16),
        V((T + TOK, D), bf16), V((16, 256), bf16), V((16, 256), f32), V((16, 256), bf16),
        V((16, D), f32),
        V((D, 384), bf16), V((D, H * DV), bf16), V((T, DV), bf16),
        V((128, 384), f32), V((384, 128), f32), V((384, T + TOK), f32),
        V((CH, T), f32), V((128, T), f32), V((128, T), bf16), V((T, 128), bf16), V((T, DV), bf16),
        V((DV, T), bf16), V((F, T), bf16), V((PHI, T), bf16), V((PHI, T), bf16),
        V((PHI, DV), bf16), V((NZ - 1, PHI, DV), bf16), V((PHI, DV), f32),
        V((PHI, DV), bf16), V((NZ - 1, PHI, DV), bf16), V((PHI, DV), f32),
        V((T, T), bf16), V((DV, T), f32), V((DV, T), f32), V((DV, T), bf16),
        V((F, T), f32), V((F, T), f32), V((DV, T), f32), V((T, DV), bf16),
        V((CH, T + 2 * TOK), f32), V((CH, TOK), bf16), V((CH, TOK), bf16),
        V((CH, T + TOK), bf16), V((T, DV), bf16), V((TOK, H * DV), bf16),
        V((H * 2 * F, TOK), bf16), V((TOK, H * 2 * F), bf16), V((TOK, D), bf16),
        V((384, 128), f32), V((SMALL, 128), f32), V((SMALL, 128), bf16),
        V((NX - 1, SMALL, 128), bf16),
        V((NX - 1, 4 * F, 128), bf16), V((NX - 1, 4 * F, 128), bf16),
        V((NX - 1, 4 * KV, 128), bf16), V((NX - 1, 4 * KV, 128), bf16),
        V((4 * CH, 128), f32),
        V((NZ, PIECE + SMALL, 128), bf16), V((NZ - 1, PIECE + SMALL, 128), bf16),
        V((PIECE + SMALL, 128), bf16),
        pltpu.SemaphoreType.DMA((N_SEMS,)), pltpu.SemaphoreType.DMA((N_SEMS,)),
        pltpu.SemaphoreType.DMA((16,)),
    ]
    att, gi, fg = pl.pallas_call(
        kernel,
        out_shape=[
            sd((TOK, H * DV), bf16), sd((TOK, D), bf16), sd((H, FULL, 128), bf16),
        ],
        in_specs=[anywhere] * 9,
        out_specs=[anywhere] * 3,
        scratch_shapes=scratch,
        compiler_params=pltpu.CompilerParams(
            collective_id=0, has_side_effects=True, vmem_limit_bytes=56 * 2**20
        ),
        name="based_layer",
    )(a.reshape(TOK, D), wq, wk, wv, cq, ck, cv, gain.reshape(1, -1), cot.reshape(TOK, H * DV))
    att, gi, gq, gk, gv, tq, tk, tv, gg = pl.pallas_call(
        unpack,
        out_shape=[
            sd((TOK, H * DV), bf16), sd((TOK, D), bf16),
            sd((ROWS, H * F), f32), sd((ROWS, H * F), f32), sd((ROWS, H * DV), f32),
            sd((3, H * F), f32), sd((3, H * F), f32), sd((3, H * DV), f32), sd((1, H * DV), f32),
        ],
        in_specs=[anywhere] * 3,
        out_specs=[anywhere] * 9,
        scratch_shapes=[
            V((TOK, H * DV), bf16), V((TOK, D), bf16), V((H, FULL, 128), bf16),
            V((ROWS, H * DV), f32), V((256, ROWS), f32), V((ROWS, H * F), f32),
            V((ROWS, H * F), f32), V((3, H * F), f32), V((3, H * F), f32), V((3, H * DV), f32),
            V((1, H * DV), f32),
            pltpu.SemaphoreType.DMA((H + 2,)), pltpu.SemaphoreType.DMA((H + 8,)),
        ],
        name="unpack",
    )(att, gi, fg)
    return att[None], gi[None], gq, gk, gv, tq, tk, tv, gg.reshape(-1)


def solution(mesh):
    rows = P("fsdp", "seq", None)
    return jax.shard_map(
        on_device,
        mesh=mesh,
        in_specs=(rows, P("fsdp", None), P("fsdp", None), P("fsdp", None), P(), P(), P(), P(), rows),
        out_specs=(
            rows, rows, P("fsdp", None), P("fsdp", None), P("fsdp", None), P(), P(), P(), P(),
        ),
        check_vma=False,
    )
```

```python
import itertools

import jax
import jax.numpy as jnp
from jax import lax
from jax.experimental import pallas as pl
from jax.experimental.pallas import tpu as pltpu
from jax.sharding import PartitionSpec as P

MESH = pl.DeviceIdType.MESH
H, F, DV = 8, 16, 128
NX, NY, NZ, GROUP = 4, 4, 8, 8
TOK, D = 128, 2048
T = GROUP * TOK
ROWS = D // NX
CH = 2 * F + DV
BANDS = F // 2
PHI = F * (BANDS + 2)
SMALL = 16
PIECE = 80
FULL = NZ * PIECE + SMALL
BT = 256
HALF = TOK // 2
ORDER = (0, 1, 7, 2, 6, 3, 5, 4)
CHUNKS = ((0, 1), (1, 3), (3, 7), (7, 8))
FAR_FIRST = (4, 3, 5, 2, 6, 1, 7)
f32, bf16 = jnp.float32, jnp.bfloat16
MATES = [(0, 1), (1, 0), (3, 0), (1, 1), (3, 1), (2, 0), (2, 1)]


def piece_rows(lo, hi):
    return slice(SMALL + lo * PIECE if lo else 0, SMALL + hi * PIECE)


def nn(a, b):
    return lax.dot_general(a, b, (((1,), (0,)), ((), ())), preferred_element_type=f32)


def nt(a, b):
    return lax.dot_general(a, b, (((1,), (1,)), ((), ())), preferred_element_type=f32)


def pair_rows(u, weighted):
    scale = 1.0 / 32.0 if weighted else 1.0
    bands = [scale * u * u]
    for d in range(1, BANDS):
        bands.append((2.0 * scale if weighted else 1.0) * u * pltpu.roll(u, d, 0))
    bands.append((2.0 * scale if weighted else 1.0) * u[:BANDS] * u[BANDS:])
    one = lax.broadcasted_iota(jnp.int32, (F - BANDS, u.shape[1]), 0) == 0
    return jnp.concatenate(bands + [jnp.where(one, 1.0, 0.0), 0.25 * u if weighted else u], 0)


def pair_rows_back(u, grad, weighted):
    scale = 1.0 / 32.0 if weighted else 1.0
    total = grad[F * (BANDS + 1) :] * (0.25 if weighted else 1.0) + 2.0 * scale * grad[:F] * u
    twice = 2.0 * scale if weighted else 1.0
    for d in range(1, BANDS):
        e = twice * grad[F * d : F * (d + 1)]
        total += e * pltpu.roll(u, d, 0) + pltpu.roll(e * u, F - d, 0)
    e = twice * grad[F * BANDS : F * BANDS + BANDS]
    return total + jnp.concatenate([e * u[BANDS:], e * u[:BANDS]], 0)


def kernel(
    a_in, wq_in, wk_in, wv_in, cq_in, ck_in, cv_in, gain_in, cot_in,
    att_o, gi_o, fg_out_o,
    fg_o, cq, ck, cv, gain, cot, AS, HS, HF, HR, HA, WC, WV, COT, TPAD, TCOL, PT, XT, KPAD, QPAD, KN, VN, VB, QS, PHQ, PHK,
    SS, SR, SA, GS, GR, GA, WT, OT, COTT, DO, DQ, DK, DVT, ATN, CG, CHS, CHR, DPT, DPN, TDV, TDQK,
    TQK, GI, CM, SMF, SMB, SMR, XS, XR, XO, ZS, ZR, ZB, ss, rs, ls,
):
    s = lax.axis_index("seq")
    f = lax.axis_index("fsdp")
    z, j = lax.div(s, 8), lax.rem(s, 8)
    y, c = lax.div(j, 2), lax.rem(j, 2)
    ids = itertools.count()

    def at(dx=0, dy=0, dz=0, dc=0):
        zz, yy, cc = lax.rem(z + dz + NZ, NZ), lax.rem(y + dy, NY), lax.rem(c + dc, 2)
        return {"seq": (zz * NY + yy) * 2 + cc, "fsdp": lax.rem(f + dx, NX)}

    def mate(dy, dc):
        return lax.rem(y + dy, NY) * 2 + lax.rem(c + dc, 2)

    def rc(src, dst, to):
        i = next(ids)
        return pltpu.make_async_remote_copy(
            src_ref=src, dst_ref=dst, send_sem=ss.at[i], recv_sem=rs.at[i],
            device_id=to, device_id_type=MESH,
        )

    def blk(i, size):
        return pl.ds(pl.multiple_of(i * size, size), size)

    bar = pltpu.get_barrier_semaphore()
    peers = [at(dx=k) for k in range(1, NX)] + [at(dy=dy, dc=dc) for dy, dc in MATES]
    peers += [at(dz=k) for k in range(1, NZ)]
    for p in peers:
        pl.semaphore_signal(bar, inc=1, device_id=p, device_id_type=MESH)
    own_rows, own_w = blk(1 + j, TOK), blk(f, ROWS)
    fetch = [
        pltpu.make_async_copy(src, dst, ls.at[2 + i])
        for i, (src, dst) in enumerate((
            (a_in, AS.at[own_rows]),
            (wq_in, WC.at[own_w, 0:128]),
            (wk_in, WC.at[own_w, 128:256]),
            (wv_in.at[:, blk(j, DV)], WC.at[own_w, 256:384]),
            (wv_in, WV.at[own_w]),
            (cot_in, cot),
            (cq_in, cq), (ck_in, ck), (cv_in, cv), (gain_in, gain),
        ))
    ]
    for cp in fetch:
        cp.start()

    @pl.when(z == 0)
    def _():
        HR[...] = jnp.zeros_like(HR)

    TPAD[...] = jnp.zeros_like(TPAD)
    for cp in fetch:
        cp.wait()
    x = AS[own_rows, :][TOK - 16 :, :].astype(f32)
    for i in range(8):
        HF[2 * i : 2 * i + 2, :] = x[14:16, i * 256 : (i + 1) * 256]
    HS[...] = HF[...].astype(bf16)
    COT[blk(j, TOK)] = cot[:, blk(j, DV)]

    TPAD[0:3, 0:128] = cq[...]
    TPAD[0:3, 128:256] = ck[...]
    TPAD[0:3, 256:384] = cv[:, blk(j, DV)]
    TPAD[3:4, 256:384] = gain[:, blk(j, DV)]
    for i in range(3):
        TCOL[i * 128 : (i + 1) * 128, :] = TPAD[:, i * 128 : (i + 1) * 128].T

    pl.semaphore_wait(bar, len(peers))
    halo_z = rc(HS, HR, at(dz=1))
    halo_g = [rc(HR, HR, at(dy=dy, dc=dc)) for dy, dc in MATES]
    last = j == GROUP - 1

    @pl.when(jnp.logical_and(last, z < NZ - 1))
    def _():
        halo_z.start()

    def tok_rows(chip_y, part=None):
        base = (1 + lax.rem(chip_y + NY, NY) * 2 + c) * TOK
        if part is None:
            return pl.ds(pl.multiple_of(base, TOK), TOK)
        return pl.ds(pl.multiple_of(base + part * HALF, HALF), HALF)

    mine = tok_rows(y)
    a_sib = rc(AS.at[mine], AS.at[mine], at(dc=1))
    up, down = {}, {}
    for p_ in (0, 1):
        src = AS.at[tok_rows(y, p_)]
        up[p_] = rc(src, AS.at[tok_rows(y, p_)], at(dy=1))
        down[p_] = rc(src, AS.at[tok_rows(y, p_)], at(dy=3))
    relay_up = rc(AS.at[tok_rows(y - 1, 0)], AS.at[tok_rows(y - 1, 0)], at(dy=1))
    relay_down = rc(AS.at[tok_rows(y + 1, 1)], AS.at[tok_rows(y + 1, 1)], at(dy=3))
    across = {}
    for name, rows in (
        ("up", tok_rows(y - 1)), ("down", tok_rows(y + 1)),
        ("far0", tok_rows(y + 2, 0)), ("far1", tok_rows(y + 2, 1)),
    ):
        across[name] = rc(AS.at[rows], AS.at[rows], at(dc=1))
    up[0].start()
    down[1].start()
    up[1].start()
    down[0].start()
    a_sib.start()
    mine_half = blk(2 * f + c, ROWS // 2)
    wqk_out, wh_out, wv_out = {}, {}, {}
    for k in (1, 3, 2):
        wqk_out[k] = rc(WC.at[mine_half, 0:256], WC.at[mine_half, 0:256], at(dx=k))
        wh_out[k] = rc(WC.at[own_w, 256:384], WC.at[own_w, 256:384], at(dx=k))
        wv_out[k] = rc(WV.at[mine_half], WV.at[mine_half], at(dx=k))
    for k in (1, 3, 2):
        wqk_out[k].start()
    for k in (1, 3, 2):
        wh_out[k].start()
    cot_out = [
        rc(cot.at[:, blk(mate(dy, dc), DV)], COT.at[blk(j, TOK)], at(dy=dy, dc=dc))
        for dy, dc in MATES
    ]

    @pl.when(jnp.logical_and(last, z > 0))
    def _():
        halo_z.wait_recv()
        for cp in halo_g:
            cp.start()

    up[0].wait_recv()
    relay_up.start()
    down[1].wait_recv()
    relay_down.start()
    w_fwd, wv_fwd = [], {}
    for k in (1, 3, 2):
        from_x = lax.rem(f + NX - k, NX)
        rows = blk(2 * from_x + c, ROWS // 2)
        wqk_out[k].wait_recv()
        cp = rc(WC.at[rows, 0:256], WC.at[rows, 0:256], at(dc=1))
        cp.start()
        w_fwd.append(cp)
        wv_fwd[k] = rc(WV.at[rows], WV.at[rows], at(dc=1))
    up[1].wait_recv()
    across["up"].start()
    down[0].wait_recv()
    across["down"].start()
    for k in (1, 3, 2):
        wh_out[k].wait_recv()
    for k in (1, 3, 2):
        wv_out[k].start()
    a_sib.wait_recv()
    for cp in w_fwd:
        cp.wait_recv()

    def project(chip_y):
        chip = lax.rem(chip_y + NY, NY)
        p = nn(AS[pl.ds(pl.multiple_of(TOK + chip * 2 * TOK, TOK), 2 * TOK)], WC[...])
        cols = pl.ds(pl.multiple_of(TOK + chip * 2 * TOK, TOK), 2 * TOK)
        PT[:, cols] = p.astype(bf16).astype(f32).T

    project(y)
    across["up"].wait_recv()
    project(y - 1)
    across["down"].wait_recv()
    project(y + 1)
    relay_up.wait_recv()
    across["far0"].start()
    relay_down.wait_recv()
    across["far1"].start()
    for cp in cot_out:
        cp.start()

    @pl.when(jnp.logical_and(jnp.logical_not(last), z > 0))
    def _():
        for (dy, dc), cp in zip(MATES, halo_g):
            from_j = lax.rem(y + NY - dy, NY) * 2 + lax.rem(c + dc, 2)

            @pl.when(from_j == GROUP - 1)
            def _():
                cp.wait_recv()

    HF[...] = HR[...].astype(f32)
    HA[...] = jnp.zeros_like(HA)
    for i in range(8):
        HA[14:16, i * 256 : (i + 1) * 256] = HF[2 * i : 2 * i + 2, :]
    AS[0 : TOK - 16] = jnp.zeros((TOK - 16, D), bf16)
    AS[TOK - 16 : TOK] = HA[...].astype(bf16)
    ph = nn(AS[TOK - 16 : TOK], WC[...]).astype(bf16).astype(f32)
    PT[:, 0:TOK] = jnp.concatenate([jnp.zeros((TOK - 16, 384), f32), ph], 0).T
    across["far0"].wait_recv()
    across["far1"].wait_recv()
    project(y + 2)

    q_rows, k_rows = blk(j, F), pl.ds(pl.multiple_of(128 + j * F, F), F)
    parts = ((q_rows, 0, F), (k_rows, F, F), (pl.ds(256, DV), 2 * F, DV))
    for rows, to, size in parts:
        p, taps = PT[rows, :], TCOL[rows, :]
        XT[to : to + size, :] = (
            taps[:, 0:1] * p[:, TOK:]
            + taps[:, 1:2] * pltpu.roll(p, 1, 1)[:, TOK:]
            + taps[:, 2:3] * pltpu.roll(p, 2, 1)[:, TOK:]
        )
    q, k, v = XT[0:F, :], XT[F : 2 * F, :], XT[2 * F :, :]
    VB[...] = v.astype(bf16)
    PHK[...] = pair_rows(k, False).astype(bf16)
    SS[...] = nt(PHK[...], VB[...]).astype(bf16)
    s_out = {k: rc(SS, SR.at[k - 1], at(dz=k)) for k in FAR_FIRST}
    for k_, cp in s_out.items():
        pl.when(z + k_ < NZ)(cp.start)
    PHQ[...] = pair_rows(q, True).astype(bf16)
    KPAD[...] = jnp.zeros_like(KPAD)
    KPAD[0:F, :] = k
    KN[...] = KPAD[...].T.astype(bf16)
    QPAD[...] = jnp.zeros_like(QPAD)
    QPAD[0:F, :] = (0.25 * q).astype(bf16)
    QS[...] = k.astype(bf16)
    VN[...] = v.T.astype(bf16)
    COTT[...] = jnp.zeros_like(COTT)
    seen = lax.broadcasted_iota(jnp.int32, (BT, BT), 0) <= lax.broadcasted_iota(
        jnp.int32, (BT, BT), 1
    )

    def causal(block):
        n = block.shape[0]
        tail = jnp.where(seen, block[n - BT :], 0.0)
        return tail if n == BT else jnp.concatenate([block[: n - BT], tail], 0)

    for tb in range(T // BT):
        n, cols = (tb + 1) * BT, slice(tb * BT, (tb + 1) * BT)
        sc = nn(KN[:n, :], QPAD[:, cols])
        w = causal(1.0 + sc * (1.0 + 0.5 * sc)).astype(bf16)
        WT[:n, cols] = w
        OT[:, cols] = nn(VB[:, :n], w)
    for cp in cot_out:
        cp.wait_recv()
    COTT[...] = COT[...].astype(f32).T
    SA[...] = jnp.zeros_like(SA)
    for k_, cp in s_out.items():

        @pl.when(z >= k_)
        def _():
            cp.wait_recv()
            SA[...] += SR[k_ - 1].astype(f32)

    gcol = TCOL[256:384, 3:4]
    o = OT[...] + nn(SA[...].T.astype(bf16), PHQ[...])
    r = lax.rsqrt(jnp.mean(o * o, 0, keepdims=True) + 1e-06)
    hat = o * r
    ct = COTT[...]
    gain_grad = jnp.sum(ct * hat, 1, keepdims=True)
    gn = ct * gcol
    DO[...] = (r * (gn - hat * jnp.mean(gn * hat, 0, keepdims=True))).astype(bf16)
    GS[...] = nt(PHQ[...], DO[...]).astype(bf16)
    g_out = {k: rc(GS, GR.at[k - 1], at(dz=NZ - k)) for k in FAR_FIRST}
    for k_, cp in g_out.items():
        pl.when(z >= k_)(cp.start)
    ATN[...] = (hat * gcol).T.astype(bf16)
    att_out = [
        rc(ATN.at[blk(mate(dy, dc), TOK)], att_o.at[:, blk(j, DV)], at(dy=dy, dc=dc))
        for dy, dc in MATES
    ]
    for cp in att_out:
        cp.start()
    att_mine = pltpu.make_async_copy(ATN.at[blk(j, TOK)], att_o.at[:, blk(j, DV)], ls.at[0])
    att_mine.start()
    DQ[...] = pair_rows_back(q, nn(SA[...].astype(bf16), DO[...]), True)
    DK[...] = jnp.zeros_like(DK)
    DVT[...] = jnp.zeros_like(DVT)
    for tb in range(T // BT):
        n, cols = (tb + 1) * BT, slice(tb * BT, (tb + 1) * BT)
        sc = nn(KN[:n, :], QPAD[:, cols])
        ds = causal(nn(VN[:n, :], DO[:, cols]) * (1.0 + sc)).astype(bf16)
        DQ[:, cols] += 0.25 * nn(QS[:, :n], ds)
        DK[:, :n] += nt(QPAD[0:F, cols], ds)
        DVT[:, :n] += nt(DO[:, cols], WT[:n, cols])
    GA[...] = jnp.zeros_like(GA)
    for k_, cp in g_out.items():

        @pl.when(z + k_ < NZ)
        def _():
            cp.wait_recv()
            GA[...] += GR[k_ - 1].astype(f32)

    dk = DK[...] + pair_rows_back(k, nn(GA[...].astype(bf16), VB[...]), False)
    CG[0:F, TOK : TOK + T] = DQ[...]
    CG[F : 2 * F, TOK : TOK + T] = dk
    CG[2 * F :, TOK : TOK + T] = DVT[...] + nn(GA[...].T.astype(bf16), PHK[...])
    CHS[...] = CG[:, TOK : 2 * TOK].astype(bf16)
    ch_out = rc(CHS, CHR, at(dz=NZ - 1))
    pl.when(z > 0)(ch_out.start)
    CG[:, 0:TOK] = jnp.zeros((CH, TOK), f32)
    CG[:, TOK + T :] = jnp.zeros((CH, TOK), f32)

    def conv_back(rows, to, size, first, count):
        g, taps = CG[to : to + size, first : first + count + TOK], TCOL[rows, :]
        n = count + TOK
        return (
            taps[:, 0:1] * g[:, :count]
            + taps[:, 1:2] * pltpu.roll(g, n - 1, 1)[:, :count]
            + taps[:, 2:3] * pltpu.roll(g, n - 2, 1)[:, :count]
        )

    for rows, to, size in parts:
        DPT[to : to + size, :] = conv_back(rows, to, size, 0, T + TOK).astype(bf16)
    x_out = {k: rc(XS.at[k - 1], XR.at[k - 1], at(dx=k)) for k in (1, 3, 2)}

    sm_out = {k: rc(SMB, SMR.at[k - 1], at(dx=k)) for k in (1, 3, 2)}
    SMF[...] = jnp.zeros_like(SMF)

    def weight_part(to_x):
        return nn(DPT[...], AS[:, blk(to_x, ROWS)])

    for k_ in (2, 1, 3):
        part = weight_part(lax.rem(f + k_, NX)).astype(bf16)
        for b in range(4):
            XS[k_ - 1, b * CH : (b + 1) * CH, :] = part[:, b * 128 : (b + 1) * 128]
        x_out[k_].start()
    part = weight_part(f)
    for b in range(4):
        XO[b * CH : (b + 1) * CH, :] = part[:, b * 128 : (b + 1) * 128]
    lane = lax.broadcasted_iota(jnp.int32, (DV, 128), 1)
    CM[...] = jnp.zeros_like(CM)
    for rows, to, size in parts:
        p, g = PT[rows, :], CG[to : to + size, TOK : TOK + T]
        sums = [
            jnp.sum(g * (pltpu.roll(p, i, 1) if i else p)[:, TOK:], 1, keepdims=True)
            for i in range(3)
        ]
        if size == DV:
            sums.append(gain_grad)
        tile = jnp.zeros((size, 128), f32)
        for i, col in enumerate(sums):
            tile = jnp.where(lane[:size] == i, col, tile)
        CM[rows, :] = tile
    for i, (lo, n) in enumerate(((0, 3), (3, 3), (6, 4))):
        SMF[lo : lo + n, :] = CM[i * 128 : (i + 1) * 128, :].T[0:n, :]
    SMB[...] = SMF[...].astype(bf16)
    for cp in sm_out.values():
        cp.start()

    @pl.when(z < NZ - 1)
    def _():
        ch_out.wait_recv()
        CG[:, TOK + T :] = CHR[...].astype(f32)

    for rows, to, size in parts:
        DPT[to : to + size, T:] = conv_back(rows, to, size, T, TOK).astype(bf16)
    DPN[...] = DPT[2 * F :, TOK:].astype(f32).T.astype(bf16)
    dp_out = []
    for dy, dc in MATES:
        m = mate(dy, dc)
        dp_out.append(rc(DPN.at[blk(m, TOK)], TDV.at[:, blk(j, DV)], at(dy=dy, dc=dc)))
        dp_out.append(
            rc(DPT.at[0 : 2 * F, blk(1 + m, TOK)], TDQK.at[blk(j, 2 * F)], at(dy=dy, dc=dc))
        )
    for cp in dp_out:
        cp.start()
    TDV[:, blk(j, DV)] = DPN[blk(j, TOK)]
    TDQK[blk(j, 2 * F)] = DPT[0 : 2 * F, blk(1 + j, TOK)]
    for k_ in (1, 3, 2):
        wv_out[k_].wait_recv()
        wv_fwd[k_].start()
    for k_ in (1, 3, 2):
        x_out[k_].wait_recv()
        XO[...] += XR[k_ - 1].astype(f32)
        sm_out[k_].wait_recv()
        SMF[...] += SMR[k_ - 1].astype(f32)
    for b in range(4):
        nat = XO[b * CH + 2 * F : (b + 1) * CH, :].T
        for i in range(2):
            ZS[2 * b + i, 0:64, :] = nat[i * 64 : (i + 1) * 64].astype(bf16)
            ZS[2 * b + i, 64:PIECE, :] = XO[b * CH + F * i : b * CH + F * (i + 1), :].astype(bf16)
            ZS[2 * b + i, PIECE:, :] = SMF[...].astype(bf16)
    z_out = {
        k: rc(ZS.at[lax.rem(z + k, NZ)], ZR.at[k - 1], at(dz=k)) for k in FAR_FIRST
    }
    for cp in z_out.values():
        cp.start()
    red = ZS[z].astype(f32)
    for k_, cp in z_out.items():
        cp.wait_recv()
        red += ZR[k_ - 1].astype(f32)
    ZB[...] = red.astype(bf16)
    zg_out = {
        k: rc(ZB.at[0:PIECE], fg_o.at[j, piece_rows(ORDER.index(k), ORDER.index(k) + 1)], at(dz=k))
        for k in ORDER[1:]
    }
    for cp in zg_out.values():
        cp.start()
    fg_o[j, 0:SMALL, :] = ZB[PIECE:, :]
    fg_o[j, SMALL : SMALL + PIECE, :] = ZB[0:PIECE, :]
    fg_sib, fg_out, fg_fwd = [], {}, []

    def to_group(ci):
        rows = piece_rows(*CHUNKS[ci])
        for dy in (2, 1, 3):
            fg_out[ci, dy] = rc(fg_o.at[j, rows], fg_o.at[j, rows], at(dy=dy))
            fg_out[ci, dy].start()
        fg_sib.append(rc(fg_o.at[j, rows], fg_o.at[j, rows], at(dc=1)))
        fg_sib[-1].start()

    to_group(0)
    for k_ in (1, 3, 2):
        wv_fwd[k_].wait_recv()
    for cp in dp_out:
        cp.wait_recv()
    tq = jnp.concatenate([TDQK[2 * F * h : 2 * F * h + F, :] for h in range(H)], 0)
    tk = jnp.concatenate([TDQK[2 * F * h + F : 2 * F * h + 2 * F, :] for h in range(H)], 0)
    TQK[...] = jnp.concatenate([tq, tk], 0).astype(f32).T.astype(bf16)

    def input_grad(i, carry):
        rows = blk(i, 256)
        gi = nt(TDV[...], WV[rows]) + nt(TQK[...], WC[rows, 0:256])
        GI[:, rows] = gi.astype(bf16)
        return carry

    lax.fori_loop(0, D // 256, input_grad, 0)
    gi_copy = pltpu.make_async_copy(GI, gi_o, ls.at[1])
    gi_copy.start()
    for ci in range(1, len(CHUNKS)):
        for k_ in ORDER[slice(*CHUNKS[ci])]:
            zg_out[k_].wait_recv()
        to_group(ci)
    fg_leave = []

    def leave(ci):
        fg_sib[ci].wait_recv()
        for cp in fg_fwd[3 * ci : 3 * ci + 3]:
            cp.wait_recv()
        rows = piece_rows(*CHUNKS[ci])
        cp = pltpu.make_async_copy(fg_o.at[:, rows], fg_out_o.at[:, rows], ls.at[12 + ci])
        cp.start()
        fg_leave.append(cp)

    for ci, chunk in enumerate(CHUNKS):
        rows = piece_rows(*chunk)
        for dy in (1, 3, 2):
            fg_out[ci, dy].wait_recv()
            from_j = lax.rem(y + NY - dy, NY) * 2 + c
            cp = rc(fg_o.at[from_j, rows], fg_o.at[from_j, rows], at(dc=1))
            cp.start()
            fg_fwd.append(cp)
        if ci:
            leave(ci - 1)
    leave(len(CHUNKS) - 1)
    for cp in att_out:
        cp.wait_recv()
    att_mine.wait()
    for cp in fg_leave:
        cp.wait()
    gi_copy.wait()
    pl.when(jnp.logical_and(last, z < NZ - 1))(halo_z.wait_send)

    @pl.when(jnp.logical_and(last, z > 0))
    def _():
        for cp in halo_g:
            cp.wait_send()

    for k_, cp in s_out.items():
        pl.when(z + k_ < NZ)(cp.wait_send)
    for k_, cp in g_out.items():
        pl.when(z >= k_)(cp.wait_send)
    pl.when(z > 0)(ch_out.wait_send)
    done = [a_sib, relay_up, relay_down] + fg_sib + cot_out + w_fwd + att_out + dp_out + fg_fwd
    for group in (up, down, across, sm_out, wqk_out, wh_out, wv_out, wv_fwd, x_out, z_out, zg_out, fg_out):
        done += list(group.values())
    for cp in done:
        cp.wait_send()


def unpack(
    att, gi, fg, att_o, gi_o, gq_o, gk_o, gv_o, tq_o, tk_o, tv_o, gg_o,
    ATT, GI, FG, GV, QTF, GQ, GK, TQ, TK, TV, GG, ins, outs,
):
    z = lax.div(lax.axis_index("seq"), GROUP)
    heads = [pltpu.make_async_copy(fg.at[h], FG.at[h], ins.at[h]) for h in range(H)]
    passed = [
        pltpu.make_async_copy(att, ATT, ins.at[H]), pltpu.make_async_copy(gi, GI, ins.at[H + 1])
    ]
    for cp in heads + passed:
        cp.start()
    leaving = []

    def leave(src, dst):
        cp = pltpu.make_async_copy(src, dst, outs.at[len(leaving)])
        cp.start()
        leaving.append(cp)

    qk_sum = jnp.zeros((8, 128), f32)
    for h in range(H):
        heads[h].wait()
        lanes = slice(h * DV, (h + 1) * DV)
        for i, k in enumerate(ORDER):
            piece = lax.rem(z + NZ - k, NZ)
            band, kind = lax.div(piece, 2), lax.rem(piece, 2)
            rows = pl.ds(pl.multiple_of(piece * 64, 64), 64)
            cols = pl.ds(pl.multiple_of(band * 128, 128), 128)
            base = SMALL + i * PIECE
            GV[rows, lanes] = FG[h, base : base + 64, :].astype(f32)
            row = pl.ds(pl.multiple_of(kind * 128 + h * F, F), F)
            QTF[row, cols] = FG[h, base + 64 : base + PIECE, :].astype(f32)
        leave(GV.at[:, lanes], gv_o.at[:, lanes])
        sm = FG[h, 0:SMALL, :].astype(f32)
        qk_sum += sm[0:8]
        TV[:, lanes] = sm[6:9]
        GG[:, lanes] = sm[9:10]
    TQ[...] = qk_sum[0:3]
    TK[...] = qk_sum[3:6]
    GQ[...] = QTF[0:128, :].T
    GK[...] = QTF[128:256, :].T
    for src, dst in ((TQ, tq_o), (TK, tk_o), (TV, tv_o), (GG, gg_o), (GQ, gq_o), (GK, gk_o)):
        leave(src, dst)
    for cp, src, dst in zip(passed, (ATT, GI), (att_o, gi_o)):
        cp.wait()
        leave(src, dst)
    for cp in leaving:
        cp.wait()


N_SEMS = 136


def on_device(a, wq, wk, wv, cq, ck, cv, gain, cot):
    sd = jax.ShapeDtypeStruct
    V = pltpu.VMEM
    vmem, anywhere = pl.BlockSpec(memory_space=V), pl.BlockSpec(memory_space=pl.ANY)
    scratch = [
        V((H, FULL, 128), bf16),
        V((3, H * F), f32), V((3, H * F), f32), V((3, H * DV), f32), V((1, H * DV), f32),
        V((TOK, H * DV), bf16),
        V((T + TOK, D), bf16), V((16, 256), bf16), V((16, 256), f32), V((16, 256), bf16),
        V((16, D), f32),
        V((D, 384), bf16), V((D, H * DV), bf16), V((T, DV), bf16),
        V((128, 384), f32), V((384, 128), f32), V((384, T + TOK), f32),
        V((CH, T), f32), V((128, T), f32), V((128, T), bf16), V((T, 128), bf16), V((T, DV), bf16),
        V((DV, T), bf16), V((F, T), bf16), V((PHI, T), bf16), V((PHI, T), bf16),
        V((PHI, DV), bf16), V((NZ - 1, PHI, DV), bf16), V((PHI, DV), f32),
        V((PHI, DV), bf16), V((NZ - 1, PHI, DV), bf16), V((PHI, DV), f32),
        V((T, T), bf16), V((DV, T), f32), V((DV, T), f32), V((DV, T), bf16),
        V((F, T), f32), V((F, T), f32), V((DV, T), f32), V((T, DV), bf16),
        V((CH, T + 2 * TOK), f32), V((CH, TOK), bf16), V((CH, TOK), bf16),
        V((CH, T + TOK), bf16), V((T, DV), bf16), V((TOK, H * DV), bf16),
        V((H * 2 * F, TOK), bf16), V((TOK, H * 2 * F), bf16), V((TOK, D), bf16),
        V((384, 128), f32), V((SMALL, 128), f32), V((SMALL, 128), bf16),
        V((NX - 1, SMALL, 128), bf16),
        V((NX - 1, 4 * CH, 128), bf16), V((NX - 1, 4 * CH, 128), bf16),
        V((4 * CH, 128), f32),
        V((NZ, PIECE + SMALL, 128), bf16), V((NZ - 1, PIECE + SMALL, 128), bf16),
        V((PIECE + SMALL, 128), bf16),
        pltpu.SemaphoreType.DMA((N_SEMS,)), pltpu.SemaphoreType.DMA((N_SEMS,)),
        pltpu.SemaphoreType.DMA((16,)),
    ]
    att, gi, fg = pl.pallas_call(
        kernel,
        out_shape=[
            sd((TOK, H * DV), bf16), sd((TOK, D), bf16), sd((H, FULL, 128), bf16),
        ],
        in_specs=[anywhere] * 9,
        out_specs=[anywhere] * 3,
        scratch_shapes=scratch,
        compiler_params=pltpu.CompilerParams(
            collective_id=0, has_side_effects=True, vmem_limit_bytes=56 * 2**20
        ),
        name="based_layer",
    )(a.reshape(TOK, D), wq, wk, wv, cq, ck, cv, gain.reshape(1, -1), cot.reshape(TOK, H * DV))
    att, gi, gq, gk, gv, tq, tk, tv, gg = pl.pallas_call(
        unpack,
        out_shape=[
            sd((TOK, H * DV), bf16), sd((TOK, D), bf16),
            sd((ROWS, H * F), f32), sd((ROWS, H * F), f32), sd((ROWS, H * DV), f32),
            sd((3, H * F), f32), sd((3, H * F), f32), sd((3, H * DV), f32), sd((1, H * DV), f32),
        ],
        in_specs=[anywhere] * 3,
        out_specs=[anywhere] * 9,
        scratch_shapes=[
            V((TOK, H * DV), bf16), V((TOK, D), bf16), V((H, FULL, 128), bf16),
            V((ROWS, H * DV), f32), V((256, ROWS), f32), V((ROWS, H * F), f32),
            V((ROWS, H * F), f32), V((3, H * F), f32), V((3, H * F), f32), V((3, H * DV), f32),
            V((1, H * DV), f32),
            pltpu.SemaphoreType.DMA((H + 2,)), pltpu.SemaphoreType.DMA((H + 8,)),
        ],
        name="unpack",
    )(att, gi, fg)
    return att[None], gi[None], gq, gk, gv, tq, tk, tv, gg.reshape(-1)


def solution(mesh):
    rows = P("fsdp", "seq", None)
    return jax.shard_map(
        on_device,
        mesh=mesh,
        in_specs=(rows, P("fsdp", None), P("fsdp", None), P("fsdp", None), P(), P(), P(), P(), rows),
        out_specs=(
            rows, rows, P("fsdp", None), P("fsdp", None), P("fsdp", None), P(), P(), P(), P(),
        ),
        check_vma=False,
    )
```
